32 devices in a mesh: ctx: 8 (over y, x, core), tp: 4 (over z).
Axes of the slice: x: 2, y: 2, z: 4, core: 2. Of those that a mesh axis runs over, the one named last changes fastest.
Arguments:
- hidden_in: bfloat16 [2, 4096, 2048], P(None, 'ctx'), may hold values from -6 to 6
- seq_lengths: int32 [2, 3], replicated, may hold values from 1 to 2048, 4096 in all within a row
- token_order: int32 [2, 4096], replicated, may hold values from 0 to 4095, each once within a row
- attn_gain: float32 [2048], replicated, may hold values from 0.5 to 1.5
- w_query: bfloat16 [2048, 2048], P('ctx', 'tp'), may hold values from -0.125 to 0.125
- w_key: bfloat16 [2048, 1024], P('ctx', 'tp'), may hold values from -0.125 to 0.125
- w_value: bfloat16 [2048, 1024], P('ctx', 'tp'), may hold values from -0.125 to 0.125
- query_gain: float32 [128], replicated, may hold values from 0.5 to 1.5
- key_gain: float32 [128], replicated, may hold values from 0.5 to 1.5
- w_out: bfloat16 [2048, 2048], P('tp', 'ctx'), may hold values from -1 to 1
- mlp_gain: float32 [2048], replicated, may hold values from 0.5 to 1.5
- w_gate: bfloat16 [2048, 6144], P('ctx', 'tp'), may hold values from -0.125 to 0.125
- w_up: bfloat16 [2048, 6144], P('ctx', 'tp'), may hold values from -0.125 to 0.125
- w_down: bfloat16 [6144, 2048], P('tp', 'ctx'), may hold values from -0.078125 to 0.078125
- cotangent: bfloat16 [2, 4096, 2048], P(None, 'ctx'), may hold values from -6 to 6
Outputs:
- layer_out: bfloat16 [2, 4096, 2048], P(None, 'ctx')
- grad_input: float32 [2, 4096, 2048], P(None, 'ctx')
- grad_attn_gain: float32 [2048], P('ctx')
- grad_query: float32 [2048, 2048], P('ctx', 'tp')
- grad_key: float32 [2048, 1024], P('ctx', 'tp')
- grad_value: float32 [2048, 1024], P('ctx', 'tp')
- grad_query_gain: float32 [128], replicated
- grad_key_gain: float32 [128], replicated
- grad_out: float32 [2048, 2048], P('tp', 'ctx')
- grad_mlp_gain: float32 [2048], P('ctx')
- grad_gate: float32 [2048, 6144], P('ctx', 'tp')
- grad_up: float32 [2048, 6144], P('ctx', 'tp')
- grad_down: float32 [6144, 2048], P('tp', 'ctx')
The draws below stay inside these ranges and needn't reach their ends.
Inputs may be any that keep to these rules, and one draw needn't show every extreme that they name: `seq_lengths`: the 3 lengths of a micro-batch, packed in this order, fill its 4096 positions; the longest is exactly 2048. `token_order`: each row is a permutation of the packed positions; slots are dealt to the indices of ctx in runs of 512.
All inputs are finite; a program needn't handle non-finite values.
Results may differ from the reference program's by a relative error of at most 0.024.
Values may be sent and summed in bfloat16 or wider, within the bound.
A program may use at most 128 MiB of HBM per device.

```python
import math
import jax
import jax.numpy as jnp
import numpy as np
from jax import lax

D = 2048
HEADS = 16
KV_HEADS = 8
HEAD = 128
FF = 6144
MB = 2
SEQS = 3
TOKENS = 4096


def block_scale(key, extent, cuts, smallest, largest):
    gain = 1.0
    for dim, shards_of in cuts:
        draws = jax.random.uniform(jax.random.fold_in(jax.random.fold_in(key, 6), dim), (shards_of,), jnp.float32, smallest / len(cuts), largest / len(cuts))
        gain = gain * jnp.repeat(jnp.exp(draws), extent[dim] // shards_of).reshape((-1,) + (1,) * (len(extent) - 1 - dim))
    return gain


def profile(number_of, total, bound, skew):
    loads = [(1 << 20) // math.isqrt(grade ** skew) + 1 for grade in range(2, number_of + 1)]
    surplus, given = total - bound - (number_of - 1), [1] * (number_of - 1)
    while surplus > 0:
        free = [i for i in range(number_of - 1) if given[i] < bound]
        mass, left = sum([loads[i] for i in free]), surplus
        for i in free:
            extra = min(bound - given[i], max(1, left * loads[i] // mass), surplus)
            given[i] = given[i] + extra
            surplus = surplus - extra
    return np.array([bound] + given)


def uneven_parts(key, count, total, bound, lean):
    if count == 2:
        one = jax.random.randint(key, (), max(1, total - bound), min(bound, total - 1) + 1)
        return jnp.stack([one, total - one])
    tallies = jnp.asarray(profile(count, total, bound, lean), jnp.int32)
    pairs = (count - 1) // 2
    donor, taker = tallies[1:1 + 2 * pairs:2], tallies[2:2 + 2 * pairs:2]
    margin = jnp.minimum(donor - 1, bound - taker)
    shifted = jax.random.randint(jax.random.fold_in(key, 1), (pairs,), 0, 1 << 20) % (margin + 1)
    tallies = tallies.at[1:1 + 2 * pairs:2].set(donor - shifted).at[2:2 + 2 * pairs:2].set(taker + shifted)
    return tallies[jax.random.permutation(jax.random.fold_in(key, 2), count)]


def noise(own_key, dims, deviation, most, cuts=(), held_as=jnp.bfloat16):
    level = block_scale(own_key, dims, cuts, -0.22, 0.18) if cuts else 1.0
    values = jax.random.normal(own_key, dims, jnp.float32) * deviation * level
    return jnp.minimum(jnp.maximum(values, -most), most).astype(held_as)


def setup_inputs(seed: int = 0) -> dict:
    streams_of = jax.random.split(jax.random.key(seed), 16)
    hidden_in = noise(streams_of[0], (MB, TOKENS, D), 1.0, 6.0, ((1, 8),))
    seq_lengths = jax.vmap(lambda own: uneven_parts(own, SEQS, TOKENS, TOKENS // 2, 1))(jax.random.split(streams_of[1], MB)).reshape((MB, SEQS)).astype(jnp.int32)
    token_order = jax.vmap(lambda own: jax.random.permutation(own, TOKENS))(jax.random.split(streams_of[2], MB)).reshape((MB, TOKENS)).astype(jnp.int32)
    attn_gain = jnp.clip(1.0 + 0.1 * jax.random.normal(streams_of[3], (D,), jnp.float32), 0.5, 1.5)
    w_query = noise(streams_of[4], (D, HEADS * HEAD), D ** -0.5, 0.125, ((0, 8), (1, 4)))
    w_key = noise(streams_of[5], (D, KV_HEADS * HEAD), D ** -0.5, 0.125, ((0, 8), (1, 4)))
    w_value = noise(streams_of[6], (D, KV_HEADS * HEAD), D ** -0.5, 0.125, ((0, 8), (1, 4)))
    query_gain = jnp.clip(1.0 + 0.1 * jax.random.normal(streams_of[7], (HEAD,), jnp.float32), 0.5, 1.5)
    key_gain = jnp.clip(1.0 + 0.1 * jax.random.normal(streams_of[8], (HEAD,), jnp.float32), 0.5, 1.5)
    w_out = noise(streams_of[9], (HEADS * HEAD, D), (HEADS * HEAD // 64) ** -0.5, 1.0, ((0, 4), (1, 8)))
    mlp_gain = jnp.clip(1.0 + 0.1 * jax.random.normal(streams_of[10], (D,), jnp.float32), 0.5, 1.5)
    w_gate = noise(streams_of[11], (D, FF), D ** -0.5, 0.125, ((0, 8), (1, 4)))
    w_up = noise(streams_of[12], (D, FF), D ** -0.5, 0.125, ((0, 8), (1, 4)))
    w_down = noise(streams_of[13], (FF, D), FF ** -0.5, 0.078125, ((0, 4), (1, 8)))
    cotangent = noise(streams_of[14], (MB, TOKENS, D), 1.0, 6.0, ((1, 8),))
    return {"hidden_in": hidden_in, "seq_lengths": seq_lengths, "token_order": token_order, "attn_gain": attn_gain, "w_query": w_query, "w_key": w_key, "w_value": w_value, "query_gain": query_gain, "key_gain": key_gain, "w_out": w_out, "mlp_gain": mlp_gain, "w_gate": w_gate, "w_up": w_up, "w_down": w_down, "cotangent": cotangent}


EPSILON = 1e-06
THETA = 1000000.0

@jax.custom_vjp
def low(v):
    return lax.optimization_barrier(v.astype(jnp.bfloat16)).astype(jnp.float32)

@jax.custom_vjp
def low_back(v):
    return v

def low_keep(v):
    return (low(v), None)

def low_pass(kept, grad):
    return (grad,)

def back_keep(v):
    return (v, None)

def back_low(kept, grad):
    return (low(grad),)
low.defvjp(low_keep, low_pass)
low_back.defvjp(back_keep, back_low)

def matmul(left_side, right_side):
    return jnp.dot(left_side, right_side, precision=lax.Precision.HIGHEST, preferred_element_type=jnp.float32)

def rms_norm(values, gain_vec):
    return values * lax.rsqrt(lax.optimization_barrier(jnp.mean(values * values, axis=-1, keepdims=True)) + EPSILON) * gain_vec

def rotate(values, angles):
    half_size = values.shape[-1] // 2
    cosine = jnp.cos(angles)[:, None, :]
    sine_part = jnp.sin(angles)[:, None, :]
    front_part = values[..., :half_size]
    back_part = values[..., half_size:]
    return jnp.concatenate([front_part * cosine - back_part * sine_part, back_part * cosine + front_part * sine_part], axis=-1)

def layout(lengths_row, order_row):
    seq_ends = jnp.cumsum(lengths_row).astype(jnp.int32)
    seq_starts = (seq_ends - lengths_row).astype(jnp.int32)
    segment = lax.optimization_barrier(jnp.sum((order_row[:, None] >= seq_ends[None, :]).astype(jnp.int32), axis=1)).astype(jnp.int32)
    matches = segment[:, None] == jnp.arange(lengths_row.shape[0], dtype=jnp.int32)[None, :]
    offset = lax.optimization_barrier(jnp.sum(jnp.where(matches, seq_starts[None, :], 0), axis=1)).astype(jnp.int32)
    return (segment, (order_row - offset).astype(jnp.int32))

def angles_of(position, head_size):
    inverse = jnp.exp(jnp.arange(head_size // 2, dtype=jnp.float32) * (-2.0 * math.log(THETA) / head_size))
    return position.astype(jnp.float32)[:, None] * inverse[None, :]

def attend(query_rows, key_rows, value_rows, segment, packed):
    tokens_all = query_rows.shape[0]
    group_size = query_rows.shape[1] // key_rows.shape[1]
    key_full = jnp.repeat(key_rows, group_size, axis=1)
    value_full = jnp.repeat(value_rows, group_size, axis=1)
    score_scale = query_rows.shape[-1] ** (-0.5)
    block_rows = min(512, tokens_all)
    block_count = tokens_all // block_rows

    def one_block(pieces):
        query_block, segment_block, packed_block = pieces
        scores = low_back(jnp.einsum('qhd,khd->hqk', query_block, key_full, precision=lax.Precision.HIGHEST) * score_scale)
        allowed = (segment_block[:, None] == segment[None, :]) & (packed[None, :] <= packed_block[:, None])
        scores = jnp.where(allowed[None], scores, -1e+30)
        weights = jnp.exp(scores - lax.optimization_barrier(jnp.max(scores, axis=-1, keepdims=True)))
        weights = low(weights / lax.optimization_barrier(jnp.sum(weights, axis=-1, keepdims=True)))
        return jnp.einsum('hqk,khd->qhd', weights, value_full, precision=lax.Precision.HIGHEST)
    pieces = (query_rows.reshape(block_count, block_rows, query_rows.shape[1], query_rows.shape[2]), segment.reshape(block_count, block_rows), packed.reshape(block_count, block_rows))
    return lax.map(jax.checkpoint(one_block), pieces).reshape(query_rows.shape)

def layer(inputs, attn_gain, w_query, w_key, w_value, query_gain, key_gain, w_out, mlp_gain, w_gate, w_up, w_down, segment, packed, angles):
    tokens_all = inputs.shape[0]
    head_size = query_gain.shape[0]
    normed = low(rms_norm(inputs, attn_gain))
    query_raw = low_back(matmul(normed, w_query)).reshape(tokens_all, -1, head_size)
    key_raw = low_back(matmul(normed, w_key)).reshape(tokens_all, -1, head_size)
    value_rows = low(low_back(matmul(normed, w_value))).reshape(tokens_all, -1, head_size)
    query_rows = low(rotate(rms_norm(query_raw, query_gain), angles))
    key_rows = low(rotate(rms_norm(key_raw, key_gain), angles))
    mixed = low(low_back(attend(query_rows, key_rows, value_rows, segment, packed))).reshape(tokens_all, -1)
    middle = inputs + low_back(matmul(mixed, w_out))
    normed_two = low(rms_norm(middle, mlp_gain))
    gate_raw = low_back(matmul(normed_two, w_gate))
    up_raw = low_back(matmul(normed_two, w_up))
    hidden = low(gate_raw * jax.nn.sigmoid(gate_raw) * up_raw)
    return middle + low_back(matmul(hidden, w_down))

def reference(hidden_in, seq_lengths, token_order, attn_gain, w_query, w_key, w_value, query_gain, key_gain, w_out, mlp_gain, w_gate, w_up, w_down, cotangent):
    weight_list = tuple((item.astype(jnp.float32) for item in (attn_gain, w_query, w_key, w_value, query_gain, key_gain, w_out, mlp_gain, w_gate, w_up, w_down)))
    totals = tuple((jnp.zeros(item.shape, jnp.float32) for item in weight_list))
    outputs = []
    input_grads = []
    for micro_batch in range(MB):
        packed = token_order[micro_batch].astype(jnp.int32)
        segment, position = layout(seq_lengths[micro_batch].astype(jnp.int32), packed)
        angles = angles_of(position, query_gain.shape[0])

        def forward(inputs, *weight_args):
            return layer(inputs, *weight_args, segment, packed, angles)
        result, pullback = jax.vjp(forward, hidden_in[micro_batch].astype(jnp.float32), *weight_list)
        grads = pullback(cotangent[micro_batch].astype(jnp.float32))
        outputs.append(result.astype(jnp.bfloat16))
        input_grads.append(grads[0])
        totals = tuple((running + fresh for running, fresh in zip(totals, grads[1:])))
    return (jnp.stack(outputs), jnp.stack(input_grads), totals[0], totals[1], totals[2], totals[3], totals[4], totals[5], totals[6], totals[7], totals[8], totals[9], totals[10])
```

```python
import functools
import math

import jax
import jax.numpy as jnp
from jax import lax
from jax.experimental import pallas as pl
from jax.experimental.pallas import tpu as pltpu
from jax.sharding import PartitionSpec as P

EPSILON = 1e-06
THETA = 1000000.0
F32 = jnp.float32
BF16 = jnp.bfloat16
MESH = pl.DeviceIdType.MESH
VMEM = pltpu.VMEM
ANY = pl.ANY
LOG2E = math.log2(math.e)
SUB = 64
QROWS = 128
CHUNKS = 16
LAG = 2


def params(megabytes, collective=None):
    if collective is None:
        return pltpu.CompilerParams(vmem_limit_bytes=megabytes << 20)
    return pltpu.CompilerParams(
        vmem_limit_bytes=megabytes << 20, collective_id=collective, has_side_effects=True
    )


def nt(left_side, right_side):
    return lax.dot_general(
        left_side, right_side, (((1,), (1,)), ((), ())), preferred_element_type=F32
    )


def tn(left_side, right_side):
    return lax.dot_general(
        left_side, right_side, (((0,), (0,)), ((), ())), preferred_element_type=F32
    )


def nn(left_side, right_side):
    return jnp.dot(left_side, right_side, preferred_element_type=F32)


def whole(shape):
    return pl.BlockSpec(shape, lambda *ids: (0,) * len(shape))


def gather_kernel(count, n_ctx, *refs):
    sources, results, sems = refs[:count], refs[count : 2 * count], refs[2 * count :]
    own_sem, send_sem, recv_sem, pass_sem, take_sem = sems
    me = lax.axis_index("ctx")
    column = lax.axis_index("tp")
    chip, core = me // 2, lax.rem(me, 2)
    chips = n_ctx // 2
    partner = chip * 2 + 1 - core

    def peer(d):
        return jnp.bitwise_xor(chip, d) * 2 + core

    barrier = pltpu.get_barrier_semaphore()
    pl.semaphore_signal(barrier, inc=1, device_id=(partner, column), device_id_type=MESH)
    for d in range(1, chips):
        pl.semaphore_signal(barrier, inc=1, device_id=(peer(d), column), device_id_type=MESH)
    pl.semaphore_wait(barrier, chips)

    def rows_of(array, owner):
        rows = sources[array].shape[0]
        return results[array].at[pl.ds(pl.multiple_of(owner * rows, rows), rows)]

    def across(array, d):
        return pltpu.make_async_remote_copy(
            src_ref=sources[array],
            dst_ref=rows_of(array, me),
            send_sem=send_sem.at[array, d],
            recv_sem=recv_sem.at[array, d],
            device_id=(peer(d), column),
            device_id_type=MESH,
        )

    def passed(array, d):
        owner = peer(d)
        return pltpu.make_async_remote_copy(
            src_ref=sources[array] if d == 0 else rows_of(array, owner),
            dst_ref=rows_of(array, owner),
            send_sem=pass_sem.at[array, d],
            recv_sem=take_sem.at[array, d],
            device_id=(partner, column),
            device_id_type=MESH,
        )

    def local(array):
        return pltpu.make_async_copy(sources[array], rows_of(array, me), own_sem.at[array])

    for array in range(count):
        for d in range(1, chips):
            across(array, d).start()
        passed(array, 0).start()
        local(array).start()
    for array in range(count):
        for d in range(1, chips):
            across(array, d).wait_recv()
            passed(array, d).start()
    for array in range(count):
        local(array).wait()
        for d in range(chips):
            if d > 0:
                across(array, d).wait_send()
            passed(array, d).wait_send()
            passed(array, d).wait_recv()


def gather_ctx(arrays, n_ctx, collective):
    count = len(arrays)
    chips = n_ctx // 2
    dma = pltpu.SemaphoreType.DMA
    return pl.pallas_call(
        functools.partial(gather_kernel, count, n_ctx),
        out_shape=[
            jax.ShapeDtypeStruct((n_ctx * a.shape[0], a.shape[1]), a.dtype) for a in arrays
        ],
        in_specs=[pl.BlockSpec(memory_space=ANY)] * count,
        out_specs=[pl.BlockSpec(memory_space=ANY)] * count,
        scratch_shapes=[dma((count,))] + [dma((count, chips))] * 4,
        compiler_params=params(16, collective),
        name="gather_ctx",
    )(*arrays)


def qkv_kernel(heads, kv_heads, x_ref, w_ref, cos_ref, sin_ref, qg_ref, kg_ref, q_ref, kv_ref, raw_ref):
    head = qg_ref.shape[1]
    rows = nn(x_ref[...], w_ref[...])
    cosine, sine = cos_ref[...], sin_ref[...]

    def turn(part, gain):
        unit = part * lax.rsqrt(jnp.mean(part * part, axis=-1, keepdims=True) + EPSILON)
        scaled = unit * gain
        return (scaled * cosine + pltpu.roll(scaled, head // 2, 1) * sine).astype(BF16)

    for h in range(heads):
        part = rows[:, h * head : (h + 1) * head]
        raw_ref[:, h * head : (h + 1) * head] = part
        q_ref[:, h * head : (h + 1) * head] = turn(part, qg_ref[...])
    for n in range(kv_heads):
        at = (heads + 2 * n) * head
        part = rows[:, at : at + head]
        raw_ref[:, (heads + n) * head : (heads + n + 1) * head] = part
        kv_ref[:, 2 * n * head : (2 * n + 1) * head] = turn(part, kg_ref[...])
        kv_ref[:, (2 * n + 1) * head : (2 * n + 2) * head] = rows[:, at + head : at + 2 * head].astype(BF16)


def project_qkv(normed, weight, cosine, sine, query_gain, key_gain, heads, kv_heads):
    total, width = normed.shape
    head = query_gain.shape[1]
    block = 256
    row = lambda cols: pl.BlockSpec((block, cols), lambda i: (i, 0))
    return pl.pallas_call(
        functools.partial(qkv_kernel, heads, kv_heads),
        grid=(total // block,),
        out_shape=[
            jax.ShapeDtypeStruct((total, heads * head), BF16),
            jax.ShapeDtypeStruct((total, 2 * kv_heads * head), BF16),
            jax.ShapeDtypeStruct((total, (heads + kv_heads) * head), F32),
        ],
        in_specs=[
            row(width),
            whole(weight.shape),
            row(head),
            row(head),
            whole((1, head)),
            whole((1, head)),
        ],
        out_specs=[row(heads * head), row(2 * kv_heads * head), row((heads + kv_heads) * head)],
        compiler_params=params(40),
        name="project_qkv",
    )(normed, weight, cosine, sine, query_gain, key_gain)


def heads_to_rows(block, head):
    return jnp.concatenate(
        [block[:, g * head : (g + 1) * head] for g in range(block.shape[1] // head)], axis=0
    )


def rows_to_heads(block, rows):
    return jnp.concatenate(
        [block[g * rows : (g + 1) * rows] for g in range(block.shape[0] // rows)], axis=1
    )


def forward_kernel(head, lo_ref, hi_ref, q_ref, kv_ref, pk_ref, pq_ref, sq_ref, out_ref, mass_ref):
    block = pl.program_id(1)
    runs = kv_ref.shape[0]
    rows = q_ref.shape[0]
    group = q_ref.shape[1] // head
    scale = head ** (-0.5) * LOG2E
    query = heads_to_rows(q_ref[...], head)
    newest = jnp.concatenate([pq_ref[...]] * group, axis=0)
    oldest = jnp.concatenate([sq_ref[...]] * group, axis=0)

    def step(j, carry):
        total, mass = carry
        at = pl.ds(pl.multiple_of(j * SUB, SUB), SUB)
        keys = kv_ref[:, at, :head].reshape(runs * SUB, head)
        values = kv_ref[:, at, head:].reshape(runs * SUB, head)
        packed = pk_ref[j]
        allowed = (packed <= newest) & (packed >= oldest)
        probs = jnp.where(allowed, jnp.exp2(nt(query, keys) * scale), 0.0)
        mass = mass + jnp.sum(probs, axis=1, keepdims=True)
        return total + nn(probs.astype(BF16), values), mass

    start = (jnp.zeros((group * rows, head), F32), jnp.zeros((group * rows, 1), F32))
    total, mass = lax.fori_loop(lo_ref[block], hi_ref[block], step, start)
    out_ref[...] = rows_to_heads(total / mass, rows)
    mass_ref[0] = jnp.broadcast_to(jnp.log2(mass), (group * rows, 128)).T[0:1]


def attend_forward(query, kv, marks, head, kv_heads):
    lo, hi, pk_row, pq_col, sq_col = marks[:5]
    rows, width = query.shape
    runs = kv.shape[0]
    group = width // (kv_heads * head)
    blocks = rows // QROWS
    return pl.pallas_call(
        functools.partial(forward_kernel, head),
        grid_spec=pltpu.PrefetchScalarGridSpec(
            num_scalar_prefetch=2,
            grid=(kv_heads, blocks),
            in_specs=[
                pl.BlockSpec((QROWS, group * head), lambda n, i, *s: (i, n)),
                pl.BlockSpec((runs, rows, 2 * head), lambda n, i, *s: (0, 0, n)),
                whole(pk_row.shape),
                pl.BlockSpec((QROWS, 1), lambda n, i, *s: (i, 0)),
                pl.BlockSpec((QROWS, 1), lambda n, i, *s: (i, 0)),
            ],
            out_specs=[
                pl.BlockSpec((QROWS, group * head), lambda n, i, *s: (i, n)),
                pl.BlockSpec((1, 1, group * QROWS), lambda n, i, *s: (n * blocks + i, 0, 0)),
            ],
        ),
        out_shape=[
            jax.ShapeDtypeStruct((rows, width), F32),
            jax.ShapeDtypeStruct((kv_heads * blocks, 1, group * QROWS), F32),
        ],
        compiler_params=params(40),
        name="attend_forward",
    )(lo, hi, query, kv, pk_row, pq_col, sq_col)


def back(grad, unit, inverse, gain):
    scaled = grad * gain
    return inverse * (scaled - unit * jnp.mean(scaled * unit, axis=-1, keepdims=True))


def unturn(grad, cosine, sine):
    return grad * cosine - pltpu.roll(grad, grad.shape[1] // 2, 1) * sine


def backward_kernel(
    head,
    lo_ref,
    hi_ref,
    q_ref,
    kv_ref,
    pk_ref,
    pq_ref,
    sq_ref,
    g_ref,
    out_ref,
    mass_ref,
    raw_ref,
    cos_ref,
    sin_ref,
    gain_ref,
    dq_ref,
    dkv_ref,
    dgain_ref,
    dk_acc,
    dv_acc,
):
    n, block = pl.program_id(0), pl.program_id(1)
    runs = kv_ref.shape[0]
    rows = q_ref.shape[0]
    group = q_ref.shape[1] // head
    scale = head ** (-0.5)
    query = heads_to_rows(q_ref[...], head)
    grad = heads_to_rows(g_ref[...], head)
    mixed = heads_to_rows(out_ref[...], head)
    row_dot = jnp.sum(grad.astype(F32) * mixed, axis=1, keepdims=True)
    row_dot = jnp.broadcast_to(row_dot, (group * rows, 128)).T[0:1]
    mass = mass_ref[0]
    newest = jnp.concatenate([pq_ref[...]] * group, axis=1)
    oldest = jnp.concatenate([sq_ref[...]] * group, axis=1)

    @pl.when(block == 0)
    def _():
        dk_acc[...] = jnp.zeros_like(dk_acc)
        dv_acc[...] = jnp.zeros_like(dv_acc)

    @pl.when((block == 0) & (n == 0))
    def _():
        dgain_ref[...] = jnp.zeros_like(dgain_ref)

    def step(j, dq):
        at = pl.ds(pl.multiple_of(j * SUB, SUB), SUB)
        keys = kv_ref[:, at, :head].reshape(runs * SUB, head)
        values = kv_ref[:, at, head:].reshape(runs * SUB, head)
        packed = pk_ref[j][:, :1]
        allowed = (packed <= newest) & (packed >= oldest)
        probs = jnp.where(allowed, jnp.exp2(nt(keys, query) * (scale * LOG2E) - mass), 0.0)
        dscores = (probs * (nt(values, grad) - row_dot)).astype(BF16)
        dk_acc[:, at, :] += nn(dscores, query).reshape(runs, SUB, head)
        dv_acc[:, at, :] += nn(probs.astype(BF16), grad).reshape(runs, SUB, head)
        return dq + tn(dscores, keys)

    dq = lax.fori_loop(
        lo_ref[block], hi_ref[block], step, jnp.zeros((group * rows, head), F32)
    )
    dq = dq * scale
    cosine, sine = cos_ref[...], sin_ref[...]
    for g in range(group):
        own = unturn(dq[g * rows : (g + 1) * rows], cosine, sine)
        raw = raw_ref[:, g * head : (g + 1) * head]
        inverse = lax.rsqrt(jnp.mean(raw * raw, axis=-1, keepdims=True) + EPSILON)
        unit = raw * inverse
        dgain_ref[...] += jnp.sum(own * unit, axis=0, keepdims=True)
        dq_ref[:, g * head : (g + 1) * head] = back(own, unit, inverse, gain_ref[...]).astype(BF16)

    @pl.when(block == pl.num_programs(1) - 1)
    def _():
        dkv_ref[:, :, :head] = (dk_acc[...] * scale).astype(BF16)
        dkv_ref[:, :, head:] = dv_acc[...].astype(BF16)


def attend_backward(query, kv, marks, grad, out, mass, raw, cosine, sine, gain, head, kv_heads):
    lo, hi, unused, unused_too, unused_three, pk_col, pq_row, sq_row = marks
    rows, width = query.shape
    runs = kv.shape[0]
    group = width // (kv_heads * head)
    blocks = rows // QROWS
    own = lambda n, i, *s: (i, n)
    return pl.pallas_call(
        functools.partial(backward_kernel, head),
        grid_spec=pltpu.PrefetchScalarGridSpec(
            num_scalar_prefetch=2,
            grid=(kv_heads, blocks),
            in_specs=[
                pl.BlockSpec((QROWS, group * head), own),
                pl.BlockSpec((runs, rows, 2 * head), lambda n, i, *s: (0, 0, n)),
                whole(pk_col.shape),
                pl.BlockSpec((1, QROWS), lambda n, i, *s: (0, i)),
                pl.BlockSpec((1, QROWS), lambda n, i, *s: (0, i)),
                pl.BlockSpec((QROWS, group * head), own),
                pl.BlockSpec((QROWS, group * head), own),
                pl.BlockSpec((1, 1, group * QROWS), lambda n, i, *s: (n * blocks + i, 0, 0)),
                pl.BlockSpec((QROWS, group * head), own),
                pl.BlockSpec((QROWS, head), lambda n, i, *s: (i, 0)),
                pl.BlockSpec((QROWS, head), lambda n, i, *s: (i, 0)),
                whole((1, head)),
            ],
            out_specs=[
                pl.BlockSpec((QROWS, group * head), own),
                pl.BlockSpec((runs, rows, 2 * head), lambda n, i, *s: (0, 0, n)),
                whole((1, head)),
            ],
            scratch_shapes=[VMEM((runs, rows, head), F32)] * 2,
        ),
        out_shape=[
            jax.ShapeDtypeStruct((rows, width), BF16),
            jax.ShapeDtypeStruct(kv.shape, BF16),
            jax.ShapeDtypeStruct((1, head), F32),
        ],
        compiler_params=params(56),
        name="attend_backward",
    )(lo, hi, query, kv, pk_col, pq_row, sq_row, grad, out, mass, raw, cosine, sine, gain)


def key_back_kernel(head, kv_heads, grad_ref, raw_ref, cos_ref, sin_ref, gain_ref, out_ref, dgain_ref):
    cosine, sine = cos_ref[...], sin_ref[...]
    total = jnp.zeros((1, head), F32)
    for n in range(kv_heads):
        at = 2 * n * head
        own = unturn(grad_ref[:, at : at + head].astype(F32), cosine, sine)
        raw = raw_ref[:, n * head : (n + 1) * head]
        inverse = lax.rsqrt(jnp.mean(raw * raw, axis=-1, keepdims=True) + EPSILON)
        unit = raw * inverse
        total = total + jnp.sum(own * unit, axis=0, keepdims=True)
        out_ref[:, at : at + head] = back(own, unit, inverse, gain_ref[...]).astype(BF16)
        out_ref[:, at + head : at + 2 * head] = grad_ref[:, at + head : at + 2 * head]
    dgain_ref[...] = total


def key_back(grad, raw, cosine, sine, gain, kv_heads):
    rows = grad.shape[0]
    head = gain.shape[1]
    keys = pl.BlockSpec((rows, kv_heads * head), lambda i: (0, raw.shape[1] // (kv_heads * head) - 1))
    return pl.pallas_call(
        functools.partial(key_back_kernel, head, kv_heads),
        grid=(1,),
        out_shape=[jax.ShapeDtypeStruct(grad.shape, BF16), jax.ShapeDtypeStruct((1, head), F32)],
        in_specs=[whole(grad.shape), keys, whole((rows, head)), whole((rows, head)), whole((1, head))],
        out_specs=[whole(grad.shape), whole((1, head))],
        compiler_params=params(32),
        name="key_back",
    )(grad, raw, cosine, sine, gain)


def line_scratch(chunks, rows, width):
    dma = pltpu.SemaphoreType.DMA
    buffer = VMEM((chunks, rows, width), BF16)
    return [buffer] * 5 + [dma((2, chunks)), dma((2, chunks))]


def line_sum(n_tp, scratch, produce, consume):
    part, from_left, from_right, to_right, to_left, send_sem, recv_sem = scratch
    chunks = part.shape[0]
    place = lax.axis_index("tp")
    line = lax.axis_index("ctx")
    has_left, has_right = place > 0, place < n_tp - 1
    barrier = pltpu.get_barrier_semaphore()

    @pl.when(has_left)
    def _():
        pl.semaphore_signal(barrier, inc=1, device_id=(line, place - 1), device_id_type=MESH)

    @pl.when(has_right)
    def _():
        pl.semaphore_signal(barrier, inc=1, device_id=(line, place + 1), device_id_type=MESH)

    pl.semaphore_wait(barrier, has_left.astype(jnp.int32) + has_right.astype(jnp.int32))

    def right(c):
        return pltpu.make_async_remote_copy(
            src_ref=to_right.at[c],
            dst_ref=from_left.at[c],
            send_sem=send_sem.at[0, c],
            recv_sem=recv_sem.at[0, c],
            device_id=(line, place + 1),
            device_id_type=MESH,
        )

    def left(c):
        return pltpu.make_async_remote_copy(
            src_ref=to_left.at[c],
            dst_ref=from_right.at[c],
            send_sem=send_sem.at[1, c],
            recv_sem=recv_sem.at[1, c],
            device_id=(line, place - 1),
            device_id_type=MESH,
        )

    def plus(a, b):
        return (a.astype(F32) + b.astype(F32)).astype(BF16)

    late = LAG * jnp.maximum(place, n_tp - 1 - place)

    def step(s, carry):
        c_right = s - LAG * place
        c_left = s - LAG * (n_tp - 1 - place)
        c_out = s - late

        @pl.when(s < chunks)
        def _():
            part[s] = produce(s).astype(BF16)

        @pl.when((c_right >= 0) & (c_right < chunks))
        def _():
            @pl.when(jnp.logical_not(has_left))
            def _():
                to_right[c_right] = part[c_right]

            @pl.when(has_left)
            def _():
                right(c_right).wait_recv()
                to_right[c_right] = plus(part[c_right], from_left[c_right])

            @pl.when(has_right)
            def _():
                right(c_right).start()

        @pl.when((c_left >= 0) & (c_left < chunks))
        def _():
            @pl.when(jnp.logical_not(has_right))
            def _():
                to_left[c_left] = part[c_left]

            @pl.when(has_right)
            def _():
                left(c_left).wait_recv()
                to_left[c_left] = plus(part[c_left], from_right[c_left])

            @pl.when(has_left)
            def _():
                left(c_left).start()

        @pl.when((c_out >= 0) & (c_out < chunks))
        def _():
            @pl.when(has_right)
            def _():
                consume(c_out, to_right[c_out].astype(F32) + from_right[c_out].astype(F32))

            @pl.when(jnp.logical_not(has_right))
            def _():
                consume(c_out, to_right[c_out].astype(F32))

        return carry

    lax.fori_loop(0, chunks + LAG * (n_tp - 1), step, 0)

    def finish(c, carry):
        @pl.when(has_right)
        def _():
            right(c).wait_send()

        @pl.when(has_left)
        def _():
            left(c).wait_send()

        return carry

    lax.fori_loop(0, chunks, finish, 0)


def piece(c, rows):
    return pl.ds(pl.multiple_of(c * rows, rows), rows)


def mean_square(values):
    return jnp.mean(values * values, axis=-1, keepdims=True)


def attn_out_kernel(n_tp, mixed_ref, place_ref, w_ref, x_ref, gain_ref, own_ref, middle_ref, normed_ref, *scratch):
    rows = scratch[0].shape[1]

    def produce(c):
        own = nn(place_ref[piece(c, rows), :], mixed_ref[...].astype(BF16)).astype(BF16)
        own_ref[piece(c, rows), :] = own
        return nt(own, w_ref[...])

    def consume(c, total):
        middle = x_ref[piece(c, rows), :].astype(F32) + total
        middle_ref[piece(c, rows), :] = middle.astype(BF16)
        unit = middle * lax.rsqrt(mean_square(middle) + EPSILON)
        normed_ref[piece(c, rows), :] = (unit * gain_ref[...]).astype(BF16)

    line_sum(n_tp, scratch, produce, consume)


def attn_out(mixed, place, weight, inputs, gain, n_tp, collective):
    rows, width = inputs.shape
    return pl.pallas_call(
        functools.partial(attn_out_kernel, n_tp),
        out_shape=[
            jax.ShapeDtypeStruct(mixed.shape, BF16),
            jax.ShapeDtypeStruct((rows, width), BF16),
            jax.ShapeDtypeStruct((rows, width), BF16),
        ],
        in_specs=[pl.BlockSpec(memory_space=VMEM)] * 5,
        out_specs=[pl.BlockSpec(memory_space=VMEM)] * 3,
        scratch_shapes=line_scratch(CHUNKS, rows // CHUNKS, width),
        compiler_params=params(56, collective),
        name="attn_out",
    )(mixed, place, weight, inputs, gain)


def middle_back_kernel(n_tp, part_ref, g_ref, middle_ref, gain_ref, w_ref, low_ref, mixed_ref, dgain_ref, *scratch):
    rows = scratch[0].shape[1]
    dgain_ref[...] = jnp.zeros_like(dgain_ref)

    def produce(c):
        return part_ref[piece(c, rows), :]

    def consume(c, total):
        middle = middle_ref[piece(c, rows), :].astype(F32)
        inverse = lax.rsqrt(mean_square(middle) + EPSILON)
        unit = middle * inverse
        dgain_ref[...] += jnp.sum(total * unit, axis=0, keepdims=True)
        grad = g_ref[piece(c, rows), :].astype(F32) + back(total, unit, inverse, gain_ref[...])
        low = grad.astype(BF16)
        low_ref[piece(c, rows), :] = low
        mixed_ref[piece(c, rows), :] = nn(low, w_ref[...]).astype(BF16)

    line_sum(n_tp, scratch, produce, consume)


def middle_back(part, grad, middle, gain, weight, n_tp, collective):
    rows, width = grad.shape
    return pl.pallas_call(
        functools.partial(middle_back_kernel, n_tp),
        out_shape=[
            jax.ShapeDtypeStruct((rows, width), BF16),
            jax.ShapeDtypeStruct((rows, weight.shape[1]), BF16),
            jax.ShapeDtypeStruct((1, width), F32),
        ],
        in_specs=[pl.BlockSpec(memory_space=VMEM)] * 5,
        out_specs=[pl.BlockSpec(memory_space=VMEM)] * 3,
        scratch_shapes=line_scratch(CHUNKS, rows // CHUNKS, width),
        compiler_params=params(56, collective),
        name="middle_back",
    )(part, grad, middle, gain, weight)


def input_back_kernel(n_tp, gq_ref, gkv_ref, place_ref, w_ref, x_ref, mid_ref, gain_ref, out_ref, dgain_ref, *scratch):
    rows = scratch[0].shape[1]
    queries = gq_ref.shape[1]
    dgain_ref[...] = jnp.zeros_like(dgain_ref)

    def produce(c):
        place = place_ref[piece(c, rows), :]
        own_q = nn(place, gq_ref[...]).astype(BF16)
        own_kv = nn(place, gkv_ref[...]).astype(BF16)
        return nt(own_q, w_ref[:, :queries]) + nt(own_kv, w_ref[:, queries:])

    def consume(c, total):
        x = x_ref[piece(c, rows), :].astype(F32)
        inverse = lax.rsqrt(mean_square(x) + EPSILON)
        unit = x * inverse
        dgain_ref[...] += jnp.sum(total * unit, axis=0, keepdims=True)
        grad = mid_ref[piece(c, rows), :].astype(F32) + back(total, unit, inverse, gain_ref[...])
        out_ref[piece(c, rows), :] = grad.astype(BF16)

    line_sum(n_tp, scratch, produce, consume)


def input_back(gq, gkv, place, weight, inputs, mid, gain, n_tp, collective):
    rows, width = inputs.shape
    return pl.pallas_call(
        functools.partial(input_back_kernel, n_tp),
        out_shape=[
            jax.ShapeDtypeStruct((rows, width), BF16),
            jax.ShapeDtypeStruct((1, width), F32),
        ],
        in_specs=[pl.BlockSpec(memory_space=VMEM)] * 7,
        out_specs=[pl.BlockSpec(memory_space=VMEM)] * 2,
        scratch_shapes=line_scratch(CHUNKS, rows // CHUNKS, width),
        compiler_params=params(56, collective),
        name="input_back",
    )(gq, gkv, place, weight, inputs, mid, gain)


def mlp_kernel(share, middle_ref, x_ref, g_ref, wg_ref, wu_ref, wd_ref, hid_ref, gg_ref, gu_ref, down_ref, gn_ref, down_acc, gn_acc):
    step = pl.program_id(0)
    gate = nn(x_ref[...], wg_ref[...])
    up = nn(x_ref[...], wu_ref[...])
    grad = nn(g_ref[...], wd_ref[...])
    sigmoid = jax.nn.sigmoid(gate)
    silu = gate * sigmoid
    hidden = (silu * up).astype(BF16)
    g_up = (grad * silu).astype(BF16)
    g_gate = (grad * up * sigmoid * (1.0 + gate * (1.0 - sigmoid))).astype(BF16)
    hid_ref[...] = hidden
    gu_ref[...] = g_up
    gg_ref[...] = g_gate
    down = nt(hidden, wd_ref[...])
    gn = nt(g_gate, wg_ref[...]) + nt(g_up, wu_ref[...])

    @pl.when(step == 0)
    def _():
        down_acc[...] = down + middle_ref[...].astype(F32) * share
        gn_acc[...] = gn

    @pl.when(step > 0)
    def _():
        down_acc[...] += down
        gn_acc[...] += gn

    @pl.when(step == pl.num_programs(0) - 1)
    def _():
        down_ref[...] = down_acc[...].astype(BF16)
        gn_ref[...] = gn_acc[...].astype(BF16)


def mlp(middle, normed, grad, weight, n_tp):
    rows, width = normed.shape
    units = weight.shape[1] // 3
    tile = 256
    tiles = units // tile
    column = lambda at: pl.BlockSpec((width, tile), lambda j: (0, at * tiles + j))
    out = pl.BlockSpec((rows, tile), lambda j: (0, j))
    return pl.pallas_call(
        functools.partial(mlp_kernel, 1.0 / n_tp),
        grid=(tiles,),
        out_shape=[jax.ShapeDtypeStruct((rows, units), BF16)] * 3
        + [jax.ShapeDtypeStruct((rows, width), BF16)] * 2,
        in_specs=[whole((rows, width))] * 3 + [column(0), column(1), column(2)],
        out_specs=[out, out, out, whole((rows, width)), whole((rows, width))],
        scratch_shapes=[VMEM((rows, width), F32)] * 2,
        compiler_params=params(60),
        name="mlp",
    )(middle, normed, grad, weight, weight, weight)


def weight_kernel(starts, parts, *refs):
    out_ref = refs[-1]
    step = pl.program_id(0)
    at = 0
    for index, (lefts, first, last) in enumerate(starts):
        left_refs = [refs[i] for i in lefts]
        right_refs = refs[parts + at : parts + at + len(lefts)]
        at += len(lefts)

        @pl.when((step >= first) & (step < last))
        def _(left_refs=left_refs, right_refs=right_refs):
            total = tn(left_refs[0][...], right_refs[0][...])
            for left_ref, right_ref in zip(left_refs[1:], right_refs[1:]):
                total = total + tn(left_ref[...], right_ref[...])
            out_ref[...] = total.astype(BF16)


def weight_grads(lefts, groups, tile):
    rows, width = lefts[0].shape
    starts, specs, rights, at = [], [], [], 0
    for indices, sides in groups:
        tiles = sides[0].shape[1] // tile
        starts.append((indices, at, at + tiles))
        for side in sides:
            rights.append(side)
            specs.append(
                pl.BlockSpec(
                    (rows, tile), lambda j, at=at, tiles=tiles: (0, jnp.clip(j - at, 0, tiles - 1))
                )
            )
        at += tiles
    return pl.pallas_call(
        functools.partial(weight_kernel, starts, len(lefts)),
        grid=(at,),
        out_shape=jax.ShapeDtypeStruct((width, at * tile), BF16),
        in_specs=[whole((rows, width))] * len(lefts) + specs,
        out_specs=pl.BlockSpec((width, tile), lambda j: (0, j)),
        compiler_params=params(60),
        name="weight_grads",
    )(*lefts, *rights)


def gains_kernel(n_ctx, n_tp, x_ref, out_ref, got, send_sem, recv_sem, line_got, line_send, line_recv):
    me, place = lax.axis_index("ctx"), lax.axis_index("tp")
    barrier = pltpu.get_barrier_semaphore()
    others = [lax.rem(me + d, n_ctx) for d in range(1, n_ctx)]
    members = [lax.rem(place + d, n_tp) for d in range(1, n_tp)]
    for other in others:
        pl.semaphore_signal(barrier, inc=1, device_id=(other, place), device_id_type=MESH)
    for member in members:
        pl.semaphore_signal(barrier, inc=1, device_id=(me, member), device_id_type=MESH)
    pl.semaphore_wait(barrier, n_ctx + n_tp - 2)
    copies = [
        pltpu.make_async_remote_copy(
            src_ref=x_ref.at[other],
            dst_ref=got.at[d],
            send_sem=send_sem.at[d],
            recv_sem=recv_sem.at[d],
            device_id=(other, place),
            device_id_type=MESH,
        )
        for d, other in enumerate(others)
    ]
    for copy in copies:
        copy.start()
    total = x_ref[me]
    for d, copy in enumerate(copies):
        copy.wait()
        total = total + got[d]
    out_ref[...] = total
    copies = [
        pltpu.make_async_remote_copy(
            src_ref=out_ref,
            dst_ref=line_got.at[d],
            send_sem=line_send.at[d],
            recv_sem=line_recv.at[d],
            device_id=(me, member),
            device_id_type=MESH,
        )
        for d, member in enumerate(members)
    ]
    for copy in copies:
        copy.start()
    low = total[4:]
    for d, copy in enumerate(copies):
        copy.wait()
        low = low + line_got[d, 4:, :]
    out_ref[4:, :] = low


def sum_gains(blocks, n_ctx, n_tp, collective):
    dma = pltpu.SemaphoreType.DMA
    return pl.pallas_call(
        functools.partial(gains_kernel, n_ctx, n_tp),
        out_shape=jax.ShapeDtypeStruct((8, 128), F32),
        in_specs=[pl.BlockSpec(memory_space=VMEM)],
        out_specs=pl.BlockSpec(memory_space=VMEM),
        scratch_shapes=[
            VMEM((n_ctx - 1, 8, 128), F32),
            dma((n_ctx - 1,)),
            dma((n_ctx - 1,)),
            VMEM((n_tp - 1, 8, 128), F32),
            dma((n_tp - 1,)),
            dma((n_tp - 1,)),
        ],
        compiler_params=params(16, collective),
        name="sum_gains",
    )(blocks)


def sort_runs(packed_runs):
    place = jnp.sum((packed_runs[:, None, :] < packed_runs[:, :, None]).astype(jnp.int32), axis=2)
    slots = jnp.arange(packed_runs.shape[1], dtype=jnp.int32)
    in_order = jnp.sum(
        jnp.where(place[:, :, None] == slots[None, None, :], packed_runs[:, :, None], 0), axis=1
    )
    return place, in_order


def layout(lengths_row, order_row, rank, n_ctx, head):
    runs = order_row.reshape(n_ctx, -1)
    rows = runs.shape[1]
    place, in_order = sort_runs(runs)
    own_place = lax.dynamic_index_in_dim(place, rank, 0, keepdims=False)
    packed = lax.dynamic_index_in_dim(in_order, rank, 0, keepdims=False)
    starts = jnp.cumsum(lengths_row) - lengths_row
    first = jnp.max(jnp.where(starts[None, :] <= packed[:, None], starts[None, :], 0), axis=1)
    position = packed - first
    inverse = jnp.exp(jnp.arange(head // 2, dtype=F32) * (-2.0 * math.log(THETA) / head))
    angles = position.astype(F32)[:, None] * inverse[None, :]
    cosine, sine = jnp.cos(angles), jnp.sin(angles)
    cosine = jnp.concatenate([cosine, cosine], axis=1)
    sine = jnp.concatenate([-sine, sine], axis=1)
    slots = jnp.arange(rows, dtype=jnp.int32)
    to_slot = (own_place[:, None] == slots[None, :]).astype(BF16)
    to_sorted = (own_place[None, :] == slots[:, None]).astype(BF16)
    blocks = rows // SUB
    grouped = in_order.reshape(n_ctx, blocks, SUB)
    smallest = jnp.min(grouped[:, :, 0], axis=0)
    largest = jnp.max(grouped[:, :, SUB - 1], axis=0)
    oldest = first.reshape(-1, QROWS)[:, 0]
    newest = packed.reshape(-1, QROWS)[:, QROWS - 1]
    lo = jnp.sum((largest[None, :] < oldest[:, None]).astype(jnp.int32), axis=1)
    hi = jnp.sum((smallest[None, :] <= newest[:, None]).astype(jnp.int32), axis=1)
    keys = grouped.transpose(1, 0, 2).reshape(blocks, n_ctx * SUB)
    pk_col = jnp.broadcast_to(keys[:, :, None], (blocks, n_ctx * SUB, 8))
    marks = (
        lo,
        hi,
        keys[:, None, :],
        packed[:, None],
        first[:, None],
        pk_col,
        packed[None, :],
        first[None, :],
    )
    return to_slot, to_sorted, cosine, sine, marks


def on_device(
    n_ctx,
    n_tp,
    hidden_in,
    seq_lengths,
    token_order,
    attn_gain,
    w_query,
    w_key,
    w_value,
    query_gain,
    key_gain,
    w_out,
    mlp_gain,
    w_gate,
    w_up,
    w_down,
    cotangent,
):
    micro_count, rows, width = hidden_in.shape
    head = query_gain.shape[0]
    heads, kv_heads = w_query.shape[1] // head, w_key.shape[1] // head
    rank = lax.axis_index("ctx")
    queries = heads * head
    units = w_gate.shape[1]
    q_gain, k_gain = query_gain[None, :], key_gain[None, :]
    a_gain, m_gain = attn_gain[None, :], mlp_gain[None, :]

    pieces = [w_query]
    for n in range(kv_heads):
        at = slice(n * head, (n + 1) * head)
        pieces += [w_key[:, at], w_value[:, at]]
    qkv_w, out_w = gather_ctx([jnp.concatenate(pieces, axis=1), w_out.T], n_ctx, 0)
    mlp_own = jnp.concatenate([w_gate, w_up, w_down.T], axis=1)
    mlp_own, qkv_w = lax.optimization_barrier((mlp_own, qkv_w))
    mlp_w = lax.all_gather(mlp_own, "ctx", axis=0, tiled=True)

    orders = [layout(seq_lengths[b], token_order[b], rank, n_ctx, head) for b in range(micro_count)]
    inputs = hidden_in.astype(F32)
    inverse = lax.rsqrt(jnp.mean(inputs * inputs, axis=-1, keepdims=True) + EPSILON)
    normed = (inputs * inverse * attn_gain).astype(BF16)
    sorted_normed = [nn(orders[b][1], normed[b]).astype(BF16) for b in range(micro_count)]

    projected = []
    for b in range(micro_count):
        q, kv, raw = project_qkv(
            sorted_normed[b], qkv_w, orders[b][2], orders[b][3], q_gain, k_gain, heads, kv_heads
        )
        (kv_all,) = gather_ctx([kv], n_ctx, 1)
        projected.append((q, kv_all.reshape(n_ctx, rows, -1), raw))

    state = []
    for b in range(micro_count):
        q, kv_all, raw = projected[b]
        mixed_full, mass = attend_forward(q, kv_all, orders[b][4], head, kv_heads)
        mixed, middle, normed_two = attn_out(
            mixed_full, orders[b][0], out_w, hidden_in[b], m_gain, n_tp, 2
        )
        state.append((mixed_full, mass, mixed, middle, normed_two))

    fed = []
    for b in range(micro_count):
        mixed_full, mass, mixed, middle, normed_two = state[b]
        hidden, g_gate, g_up, down, g_n2 = mlp(middle, normed_two, cotangent[b], mlp_w, n_tp)
        g_mid, g_mixed, d_mlp_gain = middle_back(
            g_n2, cotangent[b], middle, m_gain, out_w, n_tp, 3
        )
        fed.append((hidden, g_gate, g_up, down, g_mid, g_mixed, d_mlp_gain))

    both = range(micro_count)
    tile = 512 if units % 512 == 0 else 256
    mlp_grads = weight_grads(
        [state[b][4] for b in both] + [cotangent[b] for b in both],
        [
            (tuple(both), [fed[b][1] for b in both]),
            (tuple(both), [fed[b][2] for b in both]),
            (tuple(micro_count + b for b in both), [fed[b][0] for b in both]),
        ],
        tile,
    )
    mlp_grads = lax.psum_scatter(mlp_grads, "ctx", scatter_dimension=0, tiled=True)

    downs = jnp.stack([fed[b][3] for b in both])
    downs, last = lax.optimization_barrier((downs, fed[-1][5]))
    fed[-1] = fed[-1][:5] + (last,) + fed[-1][6:]
    layer_out = lax.psum(downs, "tp")

    attended = []
    for b in both:
        q, kv_all, raw = projected[b]
        to_slot, to_sorted, cosine, sine, marks = orders[b]
        g_mixed = nn(to_sorted, fed[b][5]).astype(BF16)
        dq, dkv, d_query_gain = attend_backward(
            q, kv_all, marks, g_mixed, state[b][0], state[b][1], raw, cosine, sine, q_gain, head, kv_heads
        )
        dkv = lax.psum_scatter(
            dkv.reshape(n_ctx * rows, -1), "ctx", scatter_dimension=0, tiled=True
        )
        attended.append((dq, dkv, d_query_gain))

    grads_in, d_attn_gain, kv_low, d_key_gain = [], [], [], []
    for b in both:
        to_slot, to_sorted, cosine, sine, marks = orders[b]
        gkv, dk_gain = key_back(attended[b][1], projected[b][2], cosine, sine, k_gain, kv_heads)
        kv_low.append(gkv)
        d_key_gain.append(dk_gain)
        grad_in, da_gain = input_back(
            attended[b][0], gkv, to_slot, qkv_w, hidden_in[b], fed[b][4], a_gain, n_tp, 4
        )
        grads_in.append(grad_in)
        d_attn_gain.append(da_gain)

    tile = min(512, 2 * kv_heads * head, queries)
    attn_grads = weight_grads(
        [sorted_normed[b] for b in both] + [fed[b][4] for b in both],
        [
            (tuple(both), [attended[b][0] for b in both]),
            (tuple(both), [kv_low[b] for b in both]),
            (tuple(micro_count + b for b in both), [state[b][2] for b in both]),
        ],
        tile,
    )
    attn_grads = lax.psum_scatter(attn_grads, "ctx", scatter_dimension=0, tiled=True).astype(F32)

    share = width // n_ctx // 128
    own = lambda gain: sum(gain).reshape(n_ctx, share, 128)
    spread = lambda gain: jnp.broadcast_to(sum(gain)[None], (n_ctx, 1, 128))
    blank = jnp.zeros((n_ctx, 4 - 2 * share, 128), F32)
    low_blank = jnp.zeros((n_ctx, 2, 128), F32)
    gains = sum_gains(
        jnp.concatenate(
            [
                own(d_attn_gain),
                own([fed[b][6] for b in both]),
                blank,
                spread([attended[b][2] for b in both]),
                spread(d_key_gain),
                low_blank,
            ],
            axis=1,
        ),
        n_ctx,
        n_tp,
        5,
    )

    mlp_grads = mlp_grads.astype(F32)
    at = queries
    keys, values = [], []
    for n in range(kv_heads):
        keys.append(attn_grads[:, at : at + head])
        values.append(attn_grads[:, at + head : at + 2 * head])
        at += 2 * head
    return (
        layer_out,
        jnp.stack(grads_in).astype(F32),
        gains[:share].reshape(-1),
        attn_grads[:, :queries],
        jnp.concatenate(keys, axis=1),
        jnp.concatenate(values, axis=1),
        gains[4],
        gains[5],
        attn_grads[:, at:].T,
        gains[share : 2 * share].reshape(-1),
        mlp_grads[:, :units],
        mlp_grads[:, units : 2 * units],
        mlp_grads[:, 2 * units :].T,
    )


def solution(mesh):
    rows = P("ctx", "tp")
    columns = P("tp", "ctx")
    tokens = P(None, "ctx", None)
    in_specs = (
        tokens,
        P(),
        P(),
        P(),
        rows,
        rows,
        rows,
        P(),
        P(),
        columns,
        P(),
        rows,
        rows,
        columns,
        tokens,
    )
    out_specs = (
        tokens,
        tokens,
        P("ctx"),
        rows,
        rows,
        rows,
        P(),
        P(),
        columns,
        P("ctx"),
        rows,
        rows,
        columns,
    )
    return jax.shard_map(
        functools.partial(on_device, mesh.shape["ctx"], mesh.shape["tp"]),
        mesh=mesh,
        in_specs=in_specs,
        out_specs=out_specs,
        check_vma=False,
    )
```

```python
import functools
import math

import jax
import jax.numpy as jnp
from jax import lax
from jax.experimental import pallas as pl
from jax.experimental.pallas import tpu as pltpu
from jax.sharding import PartitionSpec as P

EPSILON = 1e-06
THETA = 1000000.0
F32 = jnp.float32
BF16 = jnp.bfloat16
MESH = pl.DeviceIdType.MESH
VMEM = pltpu.VMEM
ANY = pl.ANY
LOG2E = math.log2(math.e)
SUB = 64
QROWS = 128
CHUNKS = 16
LAG = 2


def params(megabytes, collective=None):
    if collective is None:
        return pltpu.CompilerParams(vmem_limit_bytes=megabytes << 20)
    return pltpu.CompilerParams(
        vmem_limit_bytes=megabytes << 20, collective_id=collective, has_side_effects=True
    )


def nt(left_side, right_side):
    return lax.dot_general(
        left_side, right_side, (((1,), (1,)), ((), ())), preferred_element_type=F32
    )


def tn(left_side, right_side):
    return lax.dot_general(
        left_side, right_side, (((0,), (0,)), ((), ())), preferred_element_type=F32
    )


def nn(left_side, right_side):
    return jnp.dot(left_side, right_side, preferred_element_type=F32)


def whole(shape):
    return pl.BlockSpec(shape, lambda *ids: (0,) * len(shape))


def after(value, *others):
    return lax.optimization_barrier((value, others))[0]


def gather_parts(sources, results, sems, n_ctx):
    own_sem, send_sem, recv_sem, pass_sem, take_sem = sems
    count = len(sources)
    me = lax.axis_index("ctx")
    column = lax.axis_index("tp")
    chip, core = me // 2, lax.rem(me, 2)
    chips = n_ctx // 2
    partner = chip * 2 + 1 - core

    def peer(d):
        return jnp.bitwise_xor(chip, d) * 2 + core

    def rows_of(array, owner):
        rows = sources[array].shape[0]
        return results[array].at[pl.ds(pl.multiple_of(owner * rows, rows), rows)]

    def across(array, d):
        return pltpu.make_async_remote_copy(
            src_ref=sources[array],
            dst_ref=rows_of(array, me),
            send_sem=send_sem.at[array, d],
            recv_sem=recv_sem.at[array, d],
            device_id=(peer(d), column),
            device_id_type=MESH,
        )

    def passed(array, d):
        owner = peer(d)
        return pltpu.make_async_remote_copy(
            src_ref=sources[array] if d == 0 else rows_of(array, owner),
            dst_ref=rows_of(array, owner),
            send_sem=pass_sem.at[array, d],
            recv_sem=take_sem.at[array, d],
            device_id=(partner, column),
            device_id_type=MESH,
        )

    def local(array):
        return pltpu.make_async_copy(sources[array], rows_of(array, me), own_sem.at[array])

    def onward(array, d):
        rows = sources[array].shape[0]
        half = rows // 2
        slot = 3 if d == 1 else 0

        def of(owner):
            at = pl.multiple_of(owner * rows + (0 if d == 1 else half), half)
            return results[array].at[pl.ds(at, half)]

        return pltpu.make_async_remote_copy(
            src_ref=of(peer(d)),
            dst_ref=of(peer(d)),
            send_sem=send_sem.at[array, slot],
            recv_sem=recv_sem.at[array, slot],
            device_id=(peer(3 - d), column),
            device_id_type=MESH,
        )

    direct = range(1, chips) if chips != 4 else (1, 2)

    def start():
        for d in direct:
            for array in range(count):
                across(array, d).start()
        for array in range(count):
            passed(array, 0).start()
            local(array).start()

    def relay(array, d):
        if d in direct:
            across(array, d).wait_recv()
            if chips == 4:
                onward(array, d).start()
        else:
            onward(array, 1).wait_recv()
            onward(array, 2).wait_recv()
        passed(array, d).start()

    def finish():
        for array in range(count):
            local(array).wait()
            for d in range(chips):
                if d in direct:
                    across(array, d).wait_send()
                elif d > 0:
                    onward(array, 1).wait_send()
                    onward(array, 2).wait_send()
                passed(array, d).wait_send()
                passed(array, d).wait_recv()

    peers = [(partner, column)] + [(peer(d), column) for d in direct]
    return peers, start, relay, finish


def gather_kernel(count, n_ctx, *refs):
    peers, start, relay, finish = gather_parts(
        refs[:count], refs[count : 2 * count], refs[2 * count :], n_ctx
    )
    barrier = pltpu.get_barrier_semaphore()
    for peer in peers:
        pl.semaphore_signal(barrier, inc=1, device_id=peer, device_id_type=MESH)
    pl.semaphore_wait(barrier, len(peers))
    start()
    for array in range(count):
        for d in range(1, n_ctx // 2):
            relay(array, d)
    finish()


def gather_ctx(arrays, n_ctx, collective):
    count = len(arrays)
    chips = n_ctx // 2
    dma = pltpu.SemaphoreType.DMA
    return pl.pallas_call(
        functools.partial(gather_kernel, count, n_ctx),
        out_shape=[
            jax.ShapeDtypeStruct((n_ctx * a.shape[0], a.shape[1]), a.dtype) for a in arrays
        ],
        in_specs=[pl.BlockSpec(memory_space=ANY)] * count,
        out_specs=[pl.BlockSpec(memory_space=ANY)] * count,
        scratch_shapes=[dma((count,))] + [dma((count, chips))] * 4,
        compiler_params=params(16, collective),
        name="gather_ctx",
    )(*arrays)


def qkv_kernel(heads, kv_heads, x_ref, w_ref, cos_ref, sin_ref, qg_ref, kg_ref, q_ref, kv_ref, raw_ref):
    head = qg_ref.shape[1]
    rows = nn(x_ref[...], w_ref[...])
    cosine, sine = cos_ref[...], sin_ref[...]

    def turn(part, gain):
        unit = part * lax.rsqrt(jnp.mean(part * part, axis=-1, keepdims=True) + EPSILON)
        scaled = unit * gain
        return (scaled * cosine + pltpu.roll(scaled, head // 2, 1) * sine).astype(BF16)

    for h in range(heads):
        part = rows[:, h * head : (h + 1) * head]
        raw_ref[:, h * head : (h + 1) * head] = part
        q_ref[:, h * head : (h + 1) * head] = turn(part, qg_ref[...])
    for n in range(kv_heads):
        at = (heads + 2 * n) * head
        part = rows[:, at : at + head]
        raw_ref[:, (heads + n) * head : (heads + n + 1) * head] = part
        kv_ref[:, 2 * n * head : (2 * n + 1) * head] = turn(part, kg_ref[...])
        kv_ref[:, (2 * n + 1) * head : (2 * n + 2) * head] = rows[:, at + head : at + 2 * head].astype(BF16)


def project_qkv(normed, weight, cosine, sine, query_gain, key_gain, heads, kv_heads):
    total, width = normed.shape
    head = query_gain.shape[1]
    block = 256
    row = lambda cols: pl.BlockSpec((block, cols), lambda i: (i, 0))
    return pl.pallas_call(
        functools.partial(qkv_kernel, heads, kv_heads),
        grid=(total // block,),
        out_shape=[
            jax.ShapeDtypeStruct((total, heads * head), BF16),
            jax.ShapeDtypeStruct((total, 2 * kv_heads * head), BF16),
            jax.ShapeDtypeStruct((total, (heads + kv_heads) * head), F32),
        ],
        in_specs=[
            row(width),
            whole(weight.shape),
            row(head),
            row(head),
            whole((1, head)),
            whole((1, head)),
        ],
        out_specs=[row(heads * head), row(2 * kv_heads * head), row((heads + kv_heads) * head)],
        compiler_params=params(40),
        name="project_qkv",
    )(normed, weight, cosine, sine, query_gain, key_gain)


def heads_to_rows(block, head):
    return jnp.concatenate(
        [block[:, g * head : (g + 1) * head] for g in range(block.shape[1] // head)], axis=0
    )


def rows_to_heads(block, rows):
    return jnp.concatenate(
        [block[g * rows : (g + 1) * rows] for g in range(block.shape[0] // rows)], axis=1
    )


def forward_kernel(head, lo_ref, hi_ref, q_ref, kv_ref, pk_ref, pq_ref, sq_ref, out_ref, mass_ref):
    block = pl.program_id(1)
    runs = kv_ref.shape[0]
    rows = q_ref.shape[0]
    group = q_ref.shape[1] // head
    scale = head ** (-0.5) * LOG2E
    query = heads_to_rows(q_ref[...], head)
    newest = jnp.concatenate([pq_ref[...]] * group, axis=0)
    oldest = jnp.concatenate([sq_ref[...]] * group, axis=0)

    def step(j, carry):
        total, mass = carry
        at = pl.ds(pl.multiple_of(j * SUB, SUB), SUB)
        keys = kv_ref[:, at, :head].reshape(runs * SUB, head)
        values = kv_ref[:, at, head:].reshape(runs * SUB, head)
        packed = pk_ref[j]
        allowed = (packed <= newest) & (packed >= oldest)
        probs = jnp.where(allowed, jnp.exp2(nt(query, keys) * scale), 0.0)
        mass = mass + jnp.sum(probs, axis=1, keepdims=True)
        return total + nn(probs.astype(BF16), values), mass

    start = (jnp.zeros((group * rows, head), F32), jnp.zeros((group * rows, 1), F32))
    total, mass = lax.fori_loop(lo_ref[block], hi_ref[block], step, start)
    out_ref[...] = rows_to_heads(total / mass, rows)
    mass_ref[0] = jnp.broadcast_to(jnp.log2(mass), (group * rows, 128)).T[0:1]


def attend_forward(query, kv, marks, head, kv_heads):
    lo, hi, pk_row, pq_col, sq_col = marks[:5]
    rows, width = query.shape
    runs = kv.shape[0]
    group = width // (kv_heads * head)
    blocks = rows // QROWS
    return pl.pallas_call(
        functools.partial(forward_kernel, head),
        grid_spec=pltpu.PrefetchScalarGridSpec(
            num_scalar_prefetch=2,
            grid=(kv_heads, blocks),
            in_specs=[
                pl.BlockSpec((QROWS, group * head), lambda n, i, *s: (i, n)),
                pl.BlockSpec((runs, rows, 2 * head), lambda n, i, *s: (0, 0, n)),
                whole(pk_row.shape),
                pl.BlockSpec((QROWS, 1), lambda n, i, *s: (i, 0)),
                pl.BlockSpec((QROWS, 1), lambda n, i, *s: (i, 0)),
            ],
            out_specs=[
                pl.BlockSpec((QROWS, group * head), lambda n, i, *s: (i, n)),
                pl.BlockSpec((1, 1, group * QROWS), lambda n, i, *s: (n * blocks + i, 0, 0)),
            ],
        ),
        out_shape=[
            jax.ShapeDtypeStruct((rows, width), F32),
            jax.ShapeDtypeStruct((kv_heads * blocks, 1, group * QROWS), F32),
        ],
        compiler_params=params(40),
        name="attend_forward",
    )(lo, hi, query, kv, pk_row, pq_col, sq_col)


def back(grad, unit, inverse, gain):
    scaled = grad * gain
    return inverse * (scaled - unit * jnp.mean(scaled * unit, axis=-1, keepdims=True))


def unturn(grad, cosine, sine):
    return grad * cosine - pltpu.roll(grad, grad.shape[1] // 2, 1) * sine


def backward_kernel(
    head,
    lo_ref,
    hi_ref,
    q_ref,
    kv_ref,
    pk_ref,
    pq_ref,
    sq_ref,
    g_ref,
    out_ref,
    mass_ref,
    raw_ref,
    cos_ref,
    sin_ref,
    gain_ref,
    dq_ref,
    dkv_ref,
    dgain_ref,
    dk_acc,
    dv_acc,
):
    n, block = pl.program_id(0), pl.program_id(1)
    runs = kv_ref.shape[0]
    rows = q_ref.shape[0]
    group = q_ref.shape[1] // head
    scale = head ** (-0.5)
    query = heads_to_rows(q_ref[...], head)
    grad = heads_to_rows(g_ref[...], head)
    mixed = heads_to_rows(out_ref[...], head)
    row_dot = jnp.sum(grad.astype(F32) * mixed, axis=1, keepdims=True)
    row_dot = jnp.broadcast_to(row_dot, (group * rows, 128)).T[0:1]
    mass = mass_ref[0]
    newest = jnp.concatenate([pq_ref[...]] * group, axis=1)
    oldest = jnp.concatenate([sq_ref[...]] * group, axis=1)

    @pl.when(block == 0)
    def _():
        dk_acc[...] = jnp.zeros_like(dk_acc)
        dv_acc[...] = jnp.zeros_like(dv_acc)

    @pl.when((block == 0) & (n == 0))
    def _():
        dgain_ref[...] = jnp.zeros_like(dgain_ref)

    def step(j, dq):
        at = pl.ds(pl.multiple_of(j * SUB, SUB), SUB)
        keys = kv_ref[:, at, :head].reshape(runs * SUB, head)
        values = kv_ref[:, at, head:].reshape(runs * SUB, head)
        packed = jnp.broadcast_to(pk_ref[j], (8, pk_ref.shape[2])).T[:, :1]
        allowed = (packed <= newest) & (packed >= oldest)
        probs = jnp.where(allowed, jnp.exp2(nt(keys, query) * (scale * LOG2E) - mass), 0.0)
        dscores = (probs * (nt(values, grad) - row_dot)).astype(BF16)
        dk_acc[:, at, :] += nn(dscores, query).reshape(runs, SUB, head)
        dv_acc[:, at, :] += nn(probs.astype(BF16), grad).reshape(runs, SUB, head)
        return dq + tn(dscores, keys)

    dq = lax.fori_loop(
        lo_ref[block], hi_ref[block], step, jnp.zeros((group * rows, head), F32)
    )
    dq = dq * scale
    cosine, sine = cos_ref[...], sin_ref[...]
    for g in range(group):
        own = unturn(dq[g * rows : (g + 1) * rows], cosine, sine)
        raw = raw_ref[:, g * head : (g + 1) * head]
        inverse = lax.rsqrt(jnp.mean(raw * raw, axis=-1, keepdims=True) + EPSILON)
        unit = raw * inverse
        dgain_ref[...] += jnp.sum(own * unit, axis=0, keepdims=True)
        dq_ref[:, g * head : (g + 1) * head] = back(own, unit, inverse, gain_ref[...]).astype(BF16)

    @pl.when(block == pl.num_programs(1) - 1)
    def _():
        dkv_ref[:, :, :head] = (dk_acc[...] * scale).astype(BF16)
        dkv_ref[:, :, head:] = dv_acc[...].astype(BF16)


def attend_backward(query, kv, marks, grad, out, mass, raw, cosine, sine, gain, head, kv_heads):
    lo, hi, pk_row, unused, unused_too, pq_row, sq_row = marks
    rows, width = query.shape
    runs = kv.shape[0]
    group = width // (kv_heads * head)
    blocks = rows // QROWS
    own = lambda n, i, *s: (i, n)
    return pl.pallas_call(
        functools.partial(backward_kernel, head),
        grid_spec=pltpu.PrefetchScalarGridSpec(
            num_scalar_prefetch=2,
            grid=(kv_heads, blocks),
            in_specs=[
                pl.BlockSpec((QROWS, group * head), own),
                pl.BlockSpec((runs, rows, 2 * head), lambda n, i, *s: (0, 0, n)),
                whole(pk_row.shape),
                pl.BlockSpec((1, QROWS), lambda n, i, *s: (0, i)),
                pl.BlockSpec((1, QROWS), lambda n, i, *s: (0, i)),
                pl.BlockSpec((QROWS, group * head), own),
                pl.BlockSpec((QROWS, group * head), own),
                pl.BlockSpec((1, 1, group * QROWS), lambda n, i, *s: (n * blocks + i, 0, 0)),
                pl.BlockSpec((QROWS, group * head), own),
                pl.BlockSpec((QROWS, head), lambda n, i, *s: (i, 0)),
                pl.BlockSpec((QROWS, head), lambda n, i, *s: (i, 0)),
                whole((1, head)),
            ],
            out_specs=[
                pl.BlockSpec((QROWS, group * head), own),
                pl.BlockSpec((runs, rows, 2 * head), lambda n, i, *s: (0, 0, n)),
                whole((1, head)),
            ],
            scratch_shapes=[VMEM((runs, rows, head), F32)] * 2,
        ),
        out_shape=[
            jax.ShapeDtypeStruct((rows, width), BF16),
            jax.ShapeDtypeStruct(kv.shape, BF16),
            jax.ShapeDtypeStruct((1, head), F32),
        ],
        compiler_params=params(56),
        name="attend_backward",
    )(lo, hi, query, kv, pk_row, pq_row, sq_row, grad, out, mass, raw, cosine, sine, gain)


def key_back_kernel(head, kv_heads, grad_ref, raw_ref, cos_ref, sin_ref, gain_ref, out_ref, dgain_ref):
    cosine, sine = cos_ref[...], sin_ref[...]
    total = jnp.zeros((1, head), F32)
    for n in range(kv_heads):
        at = 2 * n * head
        own = unturn(grad_ref[:, at : at + head].astype(F32), cosine, sine)
        raw = raw_ref[:, n * head : (n + 1) * head]
        inverse = lax.rsqrt(jnp.mean(raw * raw, axis=-1, keepdims=True) + EPSILON)
        unit = raw * inverse
        total = total + jnp.sum(own * unit, axis=0, keepdims=True)
        out_ref[:, at : at + head] = back(own, unit, inverse, gain_ref[...]).astype(BF16)
        out_ref[:, at + head : at + 2 * head] = grad_ref[:, at + head : at + 2 * head]
    dgain_ref[...] = total


def key_back(grad, raw, cosine, sine, gain, kv_heads):
    rows = grad.shape[0]
    head = gain.shape[1]
    keys = pl.BlockSpec((rows, kv_heads * head), lambda i: (0, raw.shape[1] // (kv_heads * head) - 1))
    return pl.pallas_call(
        functools.partial(key_back_kernel, head, kv_heads),
        grid=(1,),
        out_shape=[jax.ShapeDtypeStruct(grad.shape, BF16), jax.ShapeDtypeStruct((1, head), F32)],
        in_specs=[whole(grad.shape), keys, whole((rows, head)), whole((rows, head)), whole((1, head))],
        out_specs=[whole(grad.shape), whole((1, head))],
        compiler_params=params(32),
        name="key_back",
    )(grad, raw, cosine, sine, gain)


def run_jobs(n_tp, line, jobs, collective, megabytes, name, alias=None):
    rows, width = line[2], line[3]
    chunks = CHUNKS
    dma = pltpu.SemaphoreType.DMA
    buffer = VMEM((chunks, rows // chunks, width), BF16)
    line_scratch = [buffer] * 5 + [dma((2, chunks)), dma((2, chunks))]
    parts = [(line[0], line[1], line_scratch)] + [job[:3] for job in jobs]
    space = lambda inside: pl.BlockSpec(memory_space=VMEM if inside else ANY)
    n_ins = [len(part[0]) for part in parts]
    n_outs = [len(part[1]) for part in parts]
    n_scratch = [len(part[2]) for part in parts]

    def kernel(*refs):
        def split(at, counts):
            groups = []
            for count in counts:
                groups.append(refs[at : at + count])
                at += count
            return groups

        ins = split(0, n_ins)
        outs = split(sum(n_ins), n_outs)
        scratch = split(sum(n_ins) + sum(n_outs), n_scratch)
        bound = [job[3](ins[i + 1], outs[i + 1], scratch[i + 1]) for i, job in enumerate(jobs)]
        produce, consume = line[4](ins[0], outs[0])
        line_sum(n_tp, scratch[0], produce, consume, bound)

    return pl.pallas_call(
        kernel,
        out_shape=[out[0] for part in parts for out in part[1]],
        in_specs=[space(inside) for part in parts for unused, inside in part[0]],
        out_specs=[space(inside) for part in parts for unused, inside in part[1]],
        scratch_shapes=[item for part in parts for item in part[2]],
        input_output_aliases=alias or {},
        compiler_params=params(megabytes, collective),
        name=name,
    )(*[array for part in parts for array, unused in part[0]])


def line_sum(n_tp, scratch, produce, consume, jobs):
    part, from_left, from_right, to_right, to_left, send_sem, recv_sem = scratch
    chunks = part.shape[0]
    place = lax.axis_index("tp")
    line = lax.axis_index("ctx")
    has_left, has_right = place > 0, place < n_tp - 1
    barrier = pltpu.get_barrier_semaphore()
    peers = [peer for job in jobs for peer in job[0]]
    for peer in peers:
        pl.semaphore_signal(barrier, inc=1, device_id=peer, device_id_type=MESH)

    @pl.when(has_left)
    def _():
        pl.semaphore_signal(barrier, inc=1, device_id=(line, place - 1), device_id_type=MESH)

    @pl.when(has_right)
    def _():
        pl.semaphore_signal(barrier, inc=1, device_id=(line, place + 1), device_id_type=MESH)

    pl.semaphore_wait(
        barrier, has_left.astype(jnp.int32) + has_right.astype(jnp.int32) + len(peers)
    )
    for job in jobs:
        job[1]()

    def right(c):
        return pltpu.make_async_remote_copy(
            src_ref=to_right.at[c],
            dst_ref=from_left.at[c],
            send_sem=send_sem.at[0, c],
            recv_sem=recv_sem.at[0, c],
            device_id=(line, place + 1),
            device_id_type=MESH,
        )

    def left(c):
        return pltpu.make_async_remote_copy(
            src_ref=to_left.at[c],
            dst_ref=from_right.at[c],
            send_sem=send_sem.at[1, c],
            recv_sem=recv_sem.at[1, c],
            device_id=(line, place - 1),
            device_id_type=MESH,
        )

    def plus(a, b):
        return (a.astype(F32) + b.astype(F32)).astype(BF16)

    late = LAG * jnp.maximum(place, n_tp - 1 - place)

    def step(s, carry):
        c_right = s - LAG * place
        c_left = s - LAG * (n_tp - 1 - place)
        c_out = s - late

        @pl.when(s < chunks)
        def _():
            part[s] = produce(s).astype(BF16)

        @pl.when((c_right >= 0) & (c_right < chunks))
        def _():
            @pl.when(jnp.logical_not(has_left))
            def _():
                to_right[c_right] = part[c_right]

            @pl.when(has_left)
            def _():
                right(c_right).wait_recv()
                to_right[c_right] = plus(part[c_right], from_left[c_right])

            @pl.when(has_right)
            def _():
                right(c_right).start()

        @pl.when((c_left >= 0) & (c_left < chunks))
        def _():
            @pl.when(jnp.logical_not(has_right))
            def _():
                to_left[c_left] = part[c_left]

            @pl.when(has_right)
            def _():
                left(c_left).wait_recv()
                to_left[c_left] = plus(part[c_left], from_right[c_left])

            @pl.when(has_left)
            def _():
                left(c_left).start()

        @pl.when((c_out >= 0) & (c_out < chunks))
        def _():
            @pl.when(has_right)
            def _():
                consume(c_out, to_right[c_out].astype(F32) + from_right[c_out].astype(F32))

            @pl.when(jnp.logical_not(has_right))
            def _():
                consume(c_out, to_right[c_out].astype(F32))

        for job in jobs:
            job[2](s)
        return carry

    lax.fori_loop(0, chunks + LAG * (n_tp - 1), step, 0)

    for job in jobs:
        job[3]()

    def finish(c, carry):
        @pl.when(has_right)
        def _():
            right(c).wait_send()

        @pl.when(has_left)
        def _():
            left(c).wait_send()

        return carry

    lax.fori_loop(0, chunks, finish, 0)


def piece(c, rows):
    return pl.ds(pl.multiple_of(c * rows, rows), rows)


def mean_square(values):
    return jnp.mean(values * values, axis=-1, keepdims=True)


def shape(rows, width, dtype=BF16):
    return jax.ShapeDtypeStruct((rows, width), dtype)


def attn_out_line(mixed, place, weight, inputs, gain):
    rows, width = inputs.shape
    size = rows // CHUNKS

    def bind(ins, outs):
        mixed_ref, place_ref, w_ref, x_ref, gain_ref = ins
        own_ref, middle_ref, normed_ref = outs

        def produce(c):
            own = nn(place_ref[piece(c, size), :], mixed_ref[...].astype(BF16)).astype(BF16)
            own_ref[piece(c, size), :] = own
            return nt(own, w_ref[...])

        def consume(c, total):
            middle = x_ref[piece(c, size), :].astype(F32) + total
            middle_ref[piece(c, size), :] = middle.astype(BF16)
            unit = middle * lax.rsqrt(mean_square(middle) + EPSILON)
            normed_ref[piece(c, size), :] = (unit * gain_ref[...]).astype(BF16)

        return produce, consume

    return (
        [(item, True) for item in (mixed, place, weight, inputs, gain)],
        [(shape(*mixed.shape), True), (shape(rows, width), True), (shape(rows, width), True)],
        rows,
        width,
        bind,
    )


def middle_back_line(part, grad, middle, gain, weight):
    rows, width = grad.shape
    size = rows // CHUNKS

    def bind(ins, outs):
        part_ref, g_ref, middle_ref, gain_ref, w_ref = ins
        low_ref, mixed_ref, dgain_ref = outs
        dgain_ref[...] = jnp.zeros_like(dgain_ref)

        def produce(c):
            return part_ref[piece(c, size), :]

        def consume(c, total):
            middle = middle_ref[piece(c, size), :].astype(F32)
            inverse = lax.rsqrt(mean_square(middle) + EPSILON)
            unit = middle * inverse
            dgain_ref[...] += jnp.sum(total * unit, axis=0, keepdims=True)
            grad = g_ref[piece(c, size), :].astype(F32) + back(total, unit, inverse, gain_ref[...])
            low = grad.astype(BF16)
            low_ref[piece(c, size), :] = low
            mixed_ref[piece(c, size), :] = nn(low, w_ref[...]).astype(BF16)

        return produce, consume

    return (
        [(item, True) for item in (part, grad, middle, gain, weight)],
        [(shape(rows, width), True), (shape(rows, weight.shape[1]), True), (shape(1, width, F32), True)],
        rows,
        width,
        bind,
    )


def input_back_line(gq, gkv, place, weight, inputs, mid, gain):
    rows, width = inputs.shape
    size = rows // CHUNKS

    def bind(ins, outs):
        gq_ref, gkv_ref, place_ref, w_ref, x_ref, mid_ref, gain_ref = ins
        out_ref, dgain_ref = outs
        queries = gq_ref.shape[1]
        dgain_ref[...] = jnp.zeros_like(dgain_ref)

        def produce(c):
            slots = place_ref[piece(c, size), :]
            own_q = nn(slots, gq_ref[...]).astype(BF16)
            own_kv = nn(slots, gkv_ref[...]).astype(BF16)
            return nt(own_q, w_ref[:, :queries]) + nt(own_kv, w_ref[:, queries:])

        def consume(c, total):
            x = x_ref[piece(c, size), :].astype(F32)
            inverse = lax.rsqrt(mean_square(x) + EPSILON)
            unit = x * inverse
            dgain_ref[...] += jnp.sum(total * unit, axis=0, keepdims=True)
            grad = mid_ref[piece(c, size), :].astype(F32) + back(total, unit, inverse, gain_ref[...])
            out_ref[piece(c, size), :] = grad.astype(BF16)

        return produce, consume

    return (
        [(item, True) for item in (gq, gkv, place, weight, inputs, mid, gain)],
        [(shape(rows, width), True), (shape(1, width, F32), True)],
        rows,
        width,
        bind,
    )


def gather_job(own, n_ctx):
    chips = n_ctx // 2
    dma = pltpu.SemaphoreType.DMA

    def bind(ins, outs, scratch):
        peers, start, relay, finish = gather_parts(ins, outs, scratch, n_ctx)

        def hook(s):
            for d in range(1, chips):

                @pl.when(s == CHUNKS - 2 * chips + 2 * d)
                def _(d=d):
                    relay(0, d)

        return peers, start, hook, finish

    return (
        [(own, False)],
        [(shape(n_ctx * own.shape[0], own.shape[1]), False)],
        [dma((1,))] + [dma((1, chips))] * 4,
        bind,
    )


def mlp_job(middle, normed, grad, weight, n_tp):
    rows, width = normed.shape
    units = weight.shape[1] // 3
    tile = 256
    tiles, down_tiles = units // tile, width // tile
    share = 1.0 / n_tp
    dma = pltpu.SemaphoreType.DMA

    def bind(ins, outs, scratch):
        middle_ref, x_ref, g_ref, w_hbm = ins
        hid_ref, gg_ref, gu_ref, down_ref, gn_ref = outs
        w_ref, sem = scratch

        def load(t, part):
            at = pl.ds(pl.multiple_of(part * units + t * tile, tile), tile)
            return pltpu.make_async_copy(w_hbm.at[:, at], w_ref.at[:, at], sem.at[part, t])

        def start():
            for t in range(tiles):
                for part in range(3):
                    load(t, part).start()

        def first(t):
            for part in range(3):
                load(t, part).wait()
            cols = [
                pl.ds(pl.multiple_of(part * units + t * tile, tile), tile) for part in range(3)
            ]
            gate = nn(x_ref[...], w_ref[:, cols[0]])
            up = nn(x_ref[...], w_ref[:, cols[1]])
            grad = nn(g_ref[...], w_ref[:, cols[2]])
            sigmoid = jax.nn.sigmoid(gate)
            silu = gate * sigmoid
            hid_ref[:, cols[0]] = (silu * up).astype(BF16)
            gu_ref[:, cols[0]] = (grad * silu).astype(BF16)
            gg_ref[:, cols[0]] = (grad * up * sigmoid * (1.0 + gate * (1.0 - sigmoid))).astype(BF16)

        def second(t):
            at = pl.ds(pl.multiple_of(t * tile, tile), tile)
            down = nt(hid_ref[...], w_ref[at, 2 * units :])
            down_ref[:, at] = (down + middle_ref[:, at].astype(F32) * share).astype(BF16)
            gn_ref[:, at] = (
                nt(gg_ref[...], w_ref[at, :units]) + nt(gu_ref[...], w_ref[at, units : 2 * units])
            ).astype(BF16)

        def hook(s):
            h = s - 1

            @pl.when((h >= 0) & (h < tiles))
            def _():
                first(h)

            @pl.when((h >= tiles) & (h < tiles + down_tiles))
            def _():
                second(h - tiles)

        return [], start, hook, lambda: None

    return (
        [(middle, True), (normed, True), (grad, True), (weight, False)],
        [(shape(rows, units), True)] * 3 + [(shape(rows, width), True)] * 2,
        [VMEM(weight.shape, BF16), dma((3, tiles))],
        bind,
    )


def weight_job(lefts, groups, tile, every, room):
    rows, width = lefts[0].shape
    rights = [side for unused, sides in groups for side in sides]
    counts = [sides[0].shape[1] // tile for unused, sides in groups]
    total = sum(counts)
    dma = pltpu.SemaphoreType.DMA
    sources = list(lefts) + rights

    def bind(ins, outs, scratch):
        (out_hbm,) = outs
        held, sems, out_buf, out_sem = scratch[: len(sources)], scratch[-3], scratch[-2], scratch[-1]

        def load(i):
            return pltpu.make_async_copy(ins[i], held[i], sems.at[i])

        def save(h):
            slot = lax.rem(h, 2)
            return pltpu.make_async_copy(
                out_buf.at[slot],
                out_hbm.at[:, pl.ds(pl.multiple_of(h * tile, tile), tile)],
                out_sem.at[slot],
            )

        def start():
            for i in range(len(sources)):
                load(i).start()

        def hook(s):
            @pl.when(s == 1)
            def _():
                for i in range(len(sources)):
                    load(i).wait()

            h = (s - 1) // every
            now = (s >= 1) & (lax.rem(s - 1, every) == 0) & (h < total)

            @pl.when(now & (h >= 2))
            def _():
                save(h - 2).wait()

            first, at = 0, len(lefts)
            for (indices, sides), count in zip(groups, counts):
                left_refs = [held[i] for i in indices]
                right_refs = held[at : at + len(sides)]
                at += len(sides)

                @pl.when(now & (h >= first) & (h < first + count))
                def _(left_refs=left_refs, right_refs=right_refs, first=first):
                    cols = pl.ds(pl.multiple_of((h - first) * tile, tile), tile)
                    grads = tn(left_refs[0][...], right_refs[0][:, cols])
                    for left_ref, right_ref in zip(left_refs[1:], right_refs[1:]):
                        grads = grads + tn(left_ref[...], right_ref[:, cols])
                    out_buf[lax.rem(h, 2)] = grads.astype(BF16)

                first += count

            @pl.when(now)
            def _():
                save(h).start()

        def finish():
            save(total - 2).wait()
            save(total - 1).wait()

        return [], start, hook, finish

    return (
        [(item, False) for item in sources] + [(room, False)],
        [(shape(width, total * tile), False)],
        [VMEM(item.shape, BF16) for item in sources]
        + [dma((len(sources),)), VMEM((2, width, tile), BF16), dma((2,))],
        bind,
    )


def scatter_job(whole_rows, n_ctx, dtype, first, second):
    total, width = whole_rows.shape
    rows = total // n_ctx
    chips = n_ctx // 2
    dma = pltpu.SemaphoreType.DMA

    def bind(ins, outs, scratch):
        (source,), (out_ref,) = ins, outs
        mine, near, far, load_sem, near_send, near_recv, far_send, far_recv = scratch
        me, column = lax.axis_index("ctx"), lax.axis_index("tp")
        chip, core = me // 2, lax.rem(me, 2)

        def block(d, which):
            at = (jnp.bitwise_xor(chip, d) * 2 + which) * rows
            return source.at[pl.ds(pl.multiple_of(at, rows), rows)]

        def load(d):
            return pltpu.make_async_copy(block(d, core), mine.at[d], load_sem.at[d])

        def beside(d):
            return pltpu.make_async_remote_copy(
                src_ref=block(d, 1 - core),
                dst_ref=near.at[d],
                send_sem=near_send.at[d],
                recv_sem=near_recv.at[d],
                device_id=(chip * 2 + 1 - core, column),
                device_id_type=MESH,
            )

        def across(d):
            return pltpu.make_async_remote_copy(
                src_ref=mine.at[d],
                dst_ref=far.at[d - 1],
                send_sem=far_send.at[d],
                recv_sem=far_recv.at[d],
                device_id=(jnp.bitwise_xor(chip, d) * 2 + core, column),
                device_id_type=MESH,
            )

        peers = [(chip * 2 + 1 - core, column)] + [
            (jnp.bitwise_xor(chip, d) * 2 + core, column) for d in range(1, chips)
        ]
        order = list(range(chips - 1, -1, -1))

        def start():
            for d in order:
                load(d).start()
                beside(d).start()

        def near_sum():
            for d in order:
                load(d).wait()
                beside(d).wait_recv()
                mine[d] = (mine[d].astype(F32) + near[d].astype(F32)).astype(BF16)
                if d > 0:
                    across(d).start()

        def far_sum():
            for d in range(1, chips):
                across(d).wait_recv()
            result = mine[0].astype(F32)
            for d in range(1, chips):
                result = result + far[d - 1].astype(F32)
            out_ref[...] = result.astype(dtype)

        def hook(s):
            @pl.when(s == first)
            def _():
                near_sum()

            @pl.when(s == second)
            def _():
                far_sum()

        def finish():
            for d in range(chips):
                beside(d).wait_send()
                if d > 0:
                    across(d).wait_send()

        return peers, start, hook, finish

    return (
        [(whole_rows, False)],
        [(shape(rows, width, dtype), True)],
        [
            VMEM((chips, rows, width), BF16),
            VMEM((chips, rows, width), BF16),
            VMEM((chips - 1, rows, width), BF16),
        ]
        + [dma((chips,))] * 5,
        bind,
    )


def weight_kernel(starts, parts, *refs):
    out_ref = refs[-1]
    step = pl.program_id(0)
    at = 0
    for index, (lefts, first, last) in enumerate(starts):
        left_refs = [refs[i] for i in lefts]
        right_refs = refs[parts + at : parts + at + len(lefts)]
        at += len(lefts)

        @pl.when((step >= first) & (step < last))
        def _(left_refs=left_refs, right_refs=right_refs):
            total = tn(left_refs[0][...], right_refs[0][...])
            for left_ref, right_ref in zip(left_refs[1:], right_refs[1:]):
                total = total + tn(left_ref[...], right_ref[...])
            out_ref[...] = total.astype(BF16)


def weight_grads(lefts, groups, tile):
    rows, width = lefts[0].shape
    starts, specs, rights, at = [], [], [], 0
    for indices, sides in groups:
        tiles = sides[0].shape[1] // tile
        starts.append((indices, at, at + tiles))
        for side in sides:
            rights.append(side)
            specs.append(
                pl.BlockSpec(
                    (rows, tile), lambda j, at=at, tiles=tiles: (0, jnp.clip(j - at, 0, tiles - 1))
                )
            )
        at += tiles
    return pl.pallas_call(
        functools.partial(weight_kernel, starts, len(lefts)),
        grid=(at,),
        out_shape=jax.ShapeDtypeStruct((width, at * tile), BF16),
        in_specs=[whole((rows, width))] * len(lefts) + specs,
        out_specs=pl.BlockSpec((width, tile), lambda j: (0, j)),
        compiler_params=params(60),
        name="weight_grads",
    )(*lefts, *rights)


def gains_kernel(n_ctx, n_tp, x_ref, out_ref, got, send_sem, recv_sem, line_got, line_send, line_recv):
    me, place = lax.axis_index("ctx"), lax.axis_index("tp")
    barrier = pltpu.get_barrier_semaphore()
    others = [lax.rem(me + d, n_ctx) for d in range(1, n_ctx)]
    members = [lax.rem(place + d, n_tp) for d in range(1, n_tp)]
    for other in others:
        pl.semaphore_signal(barrier, inc=1, device_id=(other, place), device_id_type=MESH)
    for member in members:
        pl.semaphore_signal(barrier, inc=1, device_id=(me, member), device_id_type=MESH)
    pl.semaphore_wait(barrier, n_ctx + n_tp - 2)
    copies = [
        pltpu.make_async_remote_copy(
            src_ref=x_ref.at[other],
            dst_ref=got.at[d],
            send_sem=send_sem.at[d],
            recv_sem=recv_sem.at[d],
            device_id=(other, place),
            device_id_type=MESH,
        )
        for d, other in enumerate(others)
    ]
    for copy in copies:
        copy.start()
    total = x_ref[me]
    for d, copy in enumerate(copies):
        copy.wait()
        total = total + got[d]
    out_ref[...] = total
    copies = [
        pltpu.make_async_remote_copy(
            src_ref=out_ref,
            dst_ref=line_got.at[d],
            send_sem=line_send.at[d],
            recv_sem=line_recv.at[d],
            device_id=(me, member),
            device_id_type=MESH,
        )
        for d, member in enumerate(members)
    ]
    for copy in copies:
        copy.start()
    low = total[4:]
    for d, copy in enumerate(copies):
        copy.wait()
        low = low + line_got[d, 4:, :]
    out_ref[4:, :] = low


def sum_gains(blocks, n_ctx, n_tp, collective):
    dma = pltpu.SemaphoreType.DMA
    return pl.pallas_call(
        functools.partial(gains_kernel, n_ctx, n_tp),
        out_shape=jax.ShapeDtypeStruct((8, 128), F32),
        in_specs=[pl.BlockSpec(memory_space=VMEM)],
        out_specs=pl.BlockSpec(memory_space=VMEM),
        scratch_shapes=[
            VMEM((n_ctx - 1, 8, 128), F32),
            dma((n_ctx - 1,)),
            dma((n_ctx - 1,)),
            VMEM((n_tp - 1, 8, 128), F32),
            dma((n_tp - 1,)),
            dma((n_tp - 1,)),
        ],
        compiler_params=params(16, collective),
        name="sum_gains",
    )(blocks)


def sort_runs(packed_runs):
    place = jnp.sum((packed_runs[:, None, :] < packed_runs[:, :, None]).astype(jnp.int32), axis=2)
    slots = jnp.arange(packed_runs.shape[1], dtype=jnp.int32)
    in_order = jnp.sum(
        jnp.where(place[:, :, None] == slots[None, None, :], packed_runs[:, :, None], 0), axis=1
    )
    return place, in_order


def layout(lengths_row, order_row, rank, n_ctx, head):
    runs = order_row.reshape(n_ctx, -1)
    rows = runs.shape[1]
    place, in_order = sort_runs(runs)
    own_place = lax.dynamic_index_in_dim(place, rank, 0, keepdims=False)
    packed = lax.dynamic_index_in_dim(in_order, rank, 0, keepdims=False)
    starts = jnp.cumsum(lengths_row) - lengths_row
    first = jnp.max(jnp.where(starts[None, :] <= packed[:, None], starts[None, :], 0), axis=1)
    position = packed - first
    inverse = jnp.exp(jnp.arange(head // 2, dtype=F32) * (-2.0 * math.log(THETA) / head))
    angles = position.astype(F32)[:, None] * inverse[None, :]
    cosine, sine = jnp.cos(angles), jnp.sin(angles)
    cosine = jnp.concatenate([cosine, cosine], axis=1)
    sine = jnp.concatenate([-sine, sine], axis=1)
    slots = jnp.arange(rows, dtype=jnp.int32)
    to_slot = (own_place[:, None] == slots[None, :]).astype(BF16)
    to_sorted = (own_place[None, :] == slots[:, None]).astype(BF16)
    blocks = rows // SUB
    grouped = in_order.reshape(n_ctx, blocks, SUB)
    smallest = jnp.min(grouped[:, :, 0], axis=0)
    largest = jnp.max(grouped[:, :, SUB - 1], axis=0)
    oldest = first.reshape(-1, QROWS)[:, 0]
    newest = packed.reshape(-1, QROWS)[:, QROWS - 1]
    lo = jnp.sum((largest[None, :] < oldest[:, None]).astype(jnp.int32), axis=1)
    hi = jnp.sum((smallest[None, :] <= newest[:, None]).astype(jnp.int32), axis=1)
    keys = grouped.transpose(1, 0, 2).reshape(blocks, n_ctx * SUB)
    marks = (
        lo,
        hi,
        keys[:, None, :],
        packed[:, None],
        first[:, None],
        packed[None, :],
        first[None, :],
    )
    return to_slot, to_sorted, cosine, sine, marks


def on_device(
    n_ctx,
    n_tp,
    hidden_in,
    seq_lengths,
    token_order,
    attn_gain,
    w_query,
    w_key,
    w_value,
    query_gain,
    key_gain,
    w_out,
    mlp_gain,
    w_gate,
    w_up,
    w_down,
    cotangent,
):
    micro_count, rows, width = hidden_in.shape
    head = query_gain.shape[0]
    heads, kv_heads = w_query.shape[1] // head, w_key.shape[1] // head
    rank = lax.axis_index("ctx")
    queries = heads * head
    units = w_gate.shape[1]
    q_gain, k_gain = query_gain[None, :], key_gain[None, :]
    a_gain, m_gain = attn_gain[None, :], mlp_gain[None, :]

    pieces = [w_query]
    for n in range(kv_heads):
        at = slice(n * head, (n + 1) * head)
        pieces += [w_key[:, at], w_value[:, at]]
    qkv_w, out_w = gather_ctx([jnp.concatenate(pieces, axis=1), w_out.T], n_ctx, 0)
    mlp_own = jnp.concatenate([w_gate, w_up, w_down.T], axis=1)
    orders = [layout(seq_lengths[b], token_order[b], rank, n_ctx, head) for b in range(micro_count)]
    inputs = hidden_in.astype(F32)
    inverse = lax.rsqrt(jnp.mean(inputs * inputs, axis=-1, keepdims=True) + EPSILON)
    normed = (inputs * inverse * attn_gain).astype(BF16)
    both = range(micro_count)
    last = micro_count - 1
    sorted_normed = [nn(orders[b][1], normed[b]).astype(BF16) for b in both]
    projected = [
        project_qkv(
            sorted_normed[b], qkv_w, orders[b][2], orders[b][3], q_gain, k_gain, heads, kv_heads
        )
        for b in both
    ]
    kv_own = after([p[1] for p in projected], projected[last][0])
    (kv_first,) = gather_ctx([kv_own[0]], n_ctx, 1)
    kv_all = [kv_first.reshape(n_ctx, rows, -1)]
    mlp_w = lax.all_gather(after(mlp_own, kv_first), "ctx", axis=0, tiled=True)

    def forward(b):
        return attend_forward(projected[b][0], kv_all[b], orders[b][4], head, kv_heads)

    def out_line(b):
        return attn_out_line(attended[b][0], orders[b][0], out_w, hidden_in[b], m_gain)

    def middle_line(b):
        return middle_back_line(fed[b][4], cotangent[b], middles[b][1], m_gain, out_w)

    def feed(b):
        return mlp_job(middles[b][1], middles[b][2], cotangent[b], mlp_w, n_tp)

    attended, middles, fed, mids, backs = [], [], [], [], []
    attended.append(forward(0))
    results = run_jobs(n_tp, out_line(0), [gather_job(kv_own[1], n_ctx)], 2, 40, "attn_out_gather")
    middles.append(results[:3])
    kv_all.append(results[3].reshape(n_ctx, rows, -1))
    attended.append(forward(1))
    results = run_jobs(n_tp, out_line(1), [feed(0)], 3, 60, "attn_out_mlp")
    middles.append(results[:3])
    fed.append(results[3:])
    results = run_jobs(n_tp, middle_line(0), [feed(1)], 4, 60, "middle_back_mlp")
    mids.append(results[:3])
    fed.append(results[3:])

    layer_out = jnp.stack(lax.psum([fed[b][3] for b in both], "tp"))

    def backward(b, grad):
        q, unused, raw = projected[b]
        to_slot, to_sorted, cosine, sine, marks = orders[b]
        g_mixed = nn(to_sorted, grad).astype(BF16)
        mixed_full, mass = attended[b]
        return attend_backward(
            q, kv_all[b], marks, g_mixed, mixed_full, mass, raw, cosine, sine, q_gain, head, kv_heads
        )

    backs.append(backward(0, mids[0][1]))
    tile = 512 if units % 512 == 0 else 256
    line = middle_line(1)
    line[0][0] = (after(line[0][0][0], backs[0][0]), True)
    results = run_jobs(
        n_tp,
        line,
        [
            weight_job(
                [middles[b][2] for b in both] + [cotangent[b] for b in both],
                [
                    (tuple(both), [fed[b][1] for b in both]),
                    (tuple(both), [fed[b][2] for b in both]),
                    (tuple(micro_count + b for b in both), [fed[b][0] for b in both]),
                ],
                tile,
                2,
                mlp_w,
            ),
            scatter_job(backs[0][1].reshape(n_ctx * rows, -1), n_ctx, BF16, 4, 16),
        ],
        5,
        60,
        "middle_back_weights",
        {5 + 5 * micro_count: 3},
    )
    mids.append(results[:3])
    mlp_grads = lax.psum_scatter(results[3], "ctx", scatter_dimension=0, tiled=True)
    dkv_first = results[4]
    backs.append(backward(1, mids[1][1]))

    def key_part(b, dkv):
        return key_back(dkv, projected[b][2], orders[b][2], orders[b][3], k_gain, kv_heads)

    def in_line(b, gkv):
        return input_back_line(
            backs[b][0], gkv, orders[b][0], qkv_w, hidden_in[b], mids[b][0], a_gain
        )

    gkv_first, dk_gain_first = key_part(0, after(dkv_first, backs[1][0]))
    results = run_jobs(
        n_tp,
        in_line(0, gkv_first),
        [scatter_job(backs[1][1].reshape(n_ctx * rows, -1), n_ctx, BF16, 4, 16)],
        6,
        60,
        "input_back_keys",
    )
    grad_in_first, da_gain_first, dkv_last = results
    gkv_last, dk_gain_last = key_part(1, dkv_last)
    tile = min(512, 2 * kv_heads * head, queries)
    gkvs = [gkv_first, gkv_last]
    attn_grads = weight_grads(
        [sorted_normed[b] for b in both] + [mids[b][0] for b in both],
        [
            (tuple(both), [backs[b][0] for b in both]),
            (tuple(both), [gkvs[b] for b in both]),
            (tuple(micro_count + b for b in both), [middles[b][0] for b in both]),
        ],
        tile,
    )
    results = run_jobs(
        n_tp,
        in_line(1, gkv_last),
        [scatter_job(attn_grads, n_ctx, F32, 5, 20)],
        7,
        60,
        "input_back_weights",
    )
    grad_in_last, da_gain_last, attn_grads = results
    grads_in = [grad_in_first, grad_in_last]
    d_attn_gain = [da_gain_first, da_gain_last]
    d_key_gain = [dk_gain_first, dk_gain_last]

    share = width // n_ctx // 128
    own = lambda gain: sum(gain).reshape(n_ctx, share, 128)
    spread = lambda gain: jnp.broadcast_to(sum(gain)[None], (n_ctx, 1, 128))
    blank = jnp.zeros((n_ctx, 4 - 2 * share, 128), F32)
    low_blank = jnp.zeros((n_ctx, 2, 128), F32)
    gains = sum_gains(
        jnp.concatenate(
            [
                own(d_attn_gain),
                own([mids[b][2] for b in both]),
                blank,
                spread([backs[b][2] for b in both]),
                spread(d_key_gain),
                low_blank,
            ],
            axis=1,
        ),
        n_ctx,
        n_tp,
        8,
    )

    mlp_grads = mlp_grads.astype(F32)
    at = queries
    keys, values = [], []
    for n in range(kv_heads):
        keys.append(attn_grads[:, at : at + head])
        values.append(attn_grads[:, at + head : at + 2 * head])
        at += 2 * head
    return (
        layer_out,
        jnp.stack(grads_in).astype(F32),
        gains[:share].reshape(-1),
        attn_grads[:, :queries],
        jnp.concatenate(keys, axis=1),
        jnp.concatenate(values, axis=1),
        gains[4],
        gains[5],
        attn_grads[:, at:].T,
        gains[share : 2 * share].reshape(-1),
        mlp_grads[:, :units],
        mlp_grads[:, units : 2 * units],
        mlp_grads[:, 2 * units :].T,
    )


def solution(mesh):
    rows = P("ctx", "tp")
    columns = P("tp", "ctx")
    tokens = P(None, "ctx", None)
    in_specs = (
        tokens,
        P(),
        P(),
        P(),
        rows,
        rows,
        rows,
        P(),
        P(),
        columns,
        P(),
        rows,
        rows,
        columns,
        tokens,
    )
    out_specs = (
        tokens,
        tokens,
        P("ctx"),
        rows,
        rows,
        rows,
        P(),
        P(),
        columns,
        P("ctx"),
        rows,
        rows,
        columns,
    )
    return jax.shard_map(
        functools.partial(on_device, mesh.shape["ctx"], mesh.shape["tp"]),
        mesh=mesh,
        in_specs=in_specs,
        out_specs=out_specs,
        check_vma=False,
    )
```

```python
import functools
import math

import jax
import jax.numpy as jnp
from jax import lax
from jax.experimental import pallas as pl
from jax.experimental.pallas import tpu as pltpu
from jax.sharding import PartitionSpec as P

EPSILON = 1e-06
THETA = 1000000.0
F32 = jnp.float32
BF16 = jnp.bfloat16
MESH = pl.DeviceIdType.MESH
VMEM = pltpu.VMEM
ANY = pl.ANY
LOG2E = math.log2(math.e)
SUB = 64
QROWS = 256
CHUNKS = 16
LAG = 2
GROUP = 128


def params(megabytes, collective=None):
    if collective is None:
        return pltpu.CompilerParams(vmem_limit_bytes=megabytes << 20)
    return pltpu.CompilerParams(
        vmem_limit_bytes=megabytes << 20, collective_id=collective, has_side_effects=True
    )


def nt(left_side, right_side):
    return lax.dot_general(
        left_side, right_side, (((1,), (1,)), ((), ())), preferred_element_type=F32
    )


def tn(left_side, right_side):
    return lax.dot_general(
        left_side, right_side, (((0,), (0,)), ((), ())), preferred_element_type=F32
    )


def nn(left_side, right_side):
    return jnp.dot(left_side, right_side, preferred_element_type=F32)


def whole(shape):
    return pl.BlockSpec(shape, lambda *ids: (0,) * len(shape))


def after(value, *others):
    return lax.optimization_barrier((value, others))[0]


def gather_parts(sources, results, sems, n_ctx):
    own_sem, send_sem, recv_sem, pass_sem, take_sem = sems
    count = len(sources)
    me = lax.axis_index("ctx")
    column = lax.axis_index("tp")
    chip, core = me // 2, lax.rem(me, 2)
    chips = n_ctx // 2
    partner = chip * 2 + 1 - core

    def peer(d):
        return jnp.bitwise_xor(chip, d) * 2 + core

    def rows_of(array, owner):
        rows = sources[array].shape[0]
        return results[array].at[pl.ds(pl.multiple_of(owner * rows, rows), rows)]

    def across(array, d):
        return pltpu.make_async_remote_copy(
            src_ref=sources[array],
            dst_ref=rows_of(array, me),
            send_sem=send_sem.at[array, d],
            recv_sem=recv_sem.at[array, d],
            device_id=(peer(d), column),
            device_id_type=MESH,
        )

    def passed(array, d):
        owner = peer(d)
        return pltpu.make_async_remote_copy(
            src_ref=sources[array] if d == 0 else rows_of(array, owner),
            dst_ref=rows_of(array, owner),
            send_sem=pass_sem.at[array, d],
            recv_sem=take_sem.at[array, d],
            device_id=(partner, column),
            device_id_type=MESH,
        )

    def local(array):
        return pltpu.make_async_copy(sources[array], rows_of(array, me), own_sem.at[array])

    def onward(array, d):
        rows = sources[array].shape[0]
        half = rows // 2
        slot = 3 if d == 1 else 0

        def of(owner):
            at = pl.multiple_of(owner * rows + (0 if d == 1 else half), half)
            return results[array].at[pl.ds(at, half)]

        return pltpu.make_async_remote_copy(
            src_ref=of(peer(d)),
            dst_ref=of(peer(d)),
            send_sem=send_sem.at[array, slot],
            recv_sem=recv_sem.at[array, slot],
            device_id=(peer(3 - d), column),
            device_id_type=MESH,
        )

    direct = range(1, chips) if chips != 4 else (1, 2)

    def start():
        for d in direct:
            for array in range(count):
                across(array, d).start()
        for array in range(count):
            passed(array, 0).start()
            local(array).start()

    def relay(array, d):
        if d in direct:
            across(array, d).wait_recv()
            if chips == 4:
                onward(array, d).start()
        else:
            onward(array, 1).wait_recv()
            onward(array, 2).wait_recv()
        passed(array, d).start()

    def finish():
        for array in range(count):
            local(array).wait()
            for d in range(chips):
                if d in direct:
                    across(array, d).wait_send()
                elif d > 0:
                    onward(array, 1).wait_send()
                    onward(array, 2).wait_send()
                passed(array, d).wait_send()
                passed(array, d).wait_recv()

    peers = [(partner, column)] + [(peer(d), column) for d in direct]
    return peers, start, relay, finish


def gather_kernel(count, n_ctx, *refs):
    peers, start, relay, finish = gather_parts(
        refs[:count], refs[count : 2 * count], refs[2 * count :], n_ctx
    )
    barrier = pltpu.get_barrier_semaphore()
    for peer in peers:
        pl.semaphore_signal(barrier, inc=1, device_id=peer, device_id_type=MESH)
    pl.semaphore_wait(barrier, len(peers))
    start()
    for array in range(count):
        for d in range(1, n_ctx // 2):
            relay(array, d)
    finish()


def gather_ctx(arrays, n_ctx, collective):
    count = len(arrays)
    chips = n_ctx // 2
    dma = pltpu.SemaphoreType.DMA
    return pl.pallas_call(
        functools.partial(gather_kernel, count, n_ctx),
        out_shape=[
            jax.ShapeDtypeStruct((n_ctx * a.shape[0], a.shape[1]), a.dtype) for a in arrays
        ],
        in_specs=[pl.BlockSpec(memory_space=ANY)] * count,
        out_specs=[pl.BlockSpec(memory_space=ANY)] * count,
        scratch_shapes=[dma((count,))] + [dma((count, chips))] * 4,
        compiler_params=params(16, collective),
        name="gather_ctx",
    )(*arrays)


def qkv_kernel(heads, kv_heads, x_ref, w_ref, cos_ref, sin_ref, qg_ref, kg_ref, q_ref, kv_ref, raw_ref):
    head = qg_ref.shape[1]
    rows = nn(x_ref[...], w_ref[...])
    cosine, sine = cos_ref[...], sin_ref[...]

    def turn(part, gain):
        unit = part * lax.rsqrt(jnp.mean(part * part, axis=-1, keepdims=True) + EPSILON)
        scaled = unit * gain
        return (scaled * cosine + pltpu.roll(scaled, head // 2, 1) * sine).astype(BF16)

    for h in range(heads):
        part = rows[:, h * head : (h + 1) * head]
        raw_ref[:, h * head : (h + 1) * head] = part
        q_ref[:, h * head : (h + 1) * head] = turn(part, qg_ref[...])
    for n in range(kv_heads):
        at = (heads + 2 * n) * head
        part = rows[:, at : at + head]
        raw_ref[:, (heads + n) * head : (heads + n + 1) * head] = part
        kv_ref[:, 2 * n * head : (2 * n + 1) * head] = turn(part, kg_ref[...])
        kv_ref[:, (2 * n + 1) * head : (2 * n + 2) * head] = rows[:, at + head : at + 2 * head].astype(BF16)


def project_qkv(normed, weight, cosine, sine, query_gain, key_gain, heads, kv_heads):
    total, width = normed.shape
    head = query_gain.shape[1]
    block = 256
    row = lambda cols: pl.BlockSpec((block, cols), lambda i: (i, 0))
    return pl.pallas_call(
        functools.partial(qkv_kernel, heads, kv_heads),
        grid=(total // block,),
        out_shape=[
            jax.ShapeDtypeStruct((total, heads * head), BF16),
            jax.ShapeDtypeStruct((total, 2 * kv_heads * head), BF16),
            jax.ShapeDtypeStruct((total, (heads + kv_heads) * head), F32),
        ],
        in_specs=[
            row(width),
            whole(weight.shape),
            row(head),
            row(head),
            whole((1, head)),
            whole((1, head)),
        ],
        out_specs=[row(heads * head), row(2 * kv_heads * head), row((heads + kv_heads) * head)],
        compiler_params=params(40),
        name="project_qkv",
    )(normed, weight, cosine, sine, query_gain, key_gain)


def heads_to_rows(block, head):
    return jnp.concatenate(
        [block[:, g * head : (g + 1) * head] for g in range(block.shape[1] // head)], axis=0
    )


def rows_to_heads(block, rows):
    return jnp.concatenate(
        [block[g * rows : (g + 1) * rows] for g in range(block.shape[0] // rows)], axis=1
    )


def head_parts(block, head, kv_heads):
    wide = block.shape[1] // kv_heads
    return [heads_to_rows(block[:, n * wide : (n + 1) * wide], head) for n in range(kv_heads)]


def keys_and_values(kv_ref, at, n, head):
    runs = kv_ref.shape[0]
    take = lambda i: kv_ref[:, at, i * head : (i + 1) * head].reshape(runs * SUB, head)
    return take(2 * n), take(2 * n + 1)


def forward_kernel(head, kv_heads, lo_ref, hi_ref, q_ref, kv_ref, pk_ref, pq_ref, sq_ref, out_ref, mass_ref):
    block = pl.program_id(0)
    rows = q_ref.shape[0]
    wide = q_ref.shape[1] // kv_heads
    group = wide // head
    scale = head ** (-0.5) * LOG2E
    queries = head_parts(q_ref[...], head, kv_heads)
    newest, oldest = pq_ref[...], sq_ref[...]

    def step(j, carry):
        at = pl.ds(pl.multiple_of(j * SUB, SUB), SUB)
        packed = pk_ref[j]
        allowed = (packed <= newest) & (packed >= oldest)
        allowed = jnp.concatenate([allowed] * group, axis=0)
        result = []
        for n, (total, mass) in enumerate(carry):
            keys, values = keys_and_values(kv_ref, at, n, head)
            probs = jnp.where(allowed, jnp.exp2(nt(queries[n], keys) * scale), 0.0)
            for i in range(probs.shape[1] // 128):
                mass = mass + probs[:, i * 128 : (i + 1) * 128]
            result.append((total + nn(probs.astype(BF16), values), mass))
        return tuple(result)

    zero = (jnp.zeros((group * rows, head), F32), jnp.zeros((group * rows, 128), F32))
    results = lax.fori_loop(lo_ref[block], hi_ref[block], step, (zero,) * kv_heads)
    for n, (total, mass) in enumerate(results):
        mass = jnp.sum(mass, axis=1, keepdims=True)
        out_ref[:, n * wide : (n + 1) * wide] = rows_to_heads(total / mass, rows)
        mass_ref[0, n : n + 1] = jnp.broadcast_to(jnp.log2(mass), (group * rows, 128)).T[0:1]


def attend_forward(query, kv, marks, head, kv_heads):
    lo, hi, pk_row, pq_col, sq_col = marks[:5]
    rows, width = query.shape
    group = width // (kv_heads * head)
    blocks = rows // QROWS
    own = lambda i, *s: (i, 0)
    return pl.pallas_call(
        functools.partial(forward_kernel, head, kv_heads),
        grid_spec=pltpu.PrefetchScalarGridSpec(
            num_scalar_prefetch=2,
            grid=(blocks,),
            in_specs=[
                pl.BlockSpec((QROWS, width), own),
                whole(kv.shape),
                whole(pk_row.shape),
                pl.BlockSpec((QROWS, 1), own),
                pl.BlockSpec((QROWS, 1), own),
            ],
            out_specs=[
                pl.BlockSpec((QROWS, width), own),
                pl.BlockSpec((1, kv_heads, group * QROWS), lambda i, *s: (i, 0, 0)),
            ],
        ),
        out_shape=[
            jax.ShapeDtypeStruct((rows, width), F32),
            jax.ShapeDtypeStruct((blocks, kv_heads, group * QROWS), F32),
        ],
        compiler_params=params(40),
        name="attend_forward",
    )(lo, hi, query, kv, pk_row, pq_col, sq_col)


def back(grad, unit, inverse, gain):
    scaled = grad * gain
    return inverse * (scaled - unit * jnp.mean(scaled * unit, axis=-1, keepdims=True))


def unturn(grad, cosine, sine):
    return grad * cosine - pltpu.roll(grad, grad.shape[1] // 2, 1) * sine


def backward_kernel(
    head,
    kv_heads,
    lo_ref,
    hi_ref,
    q_ref,
    kv_ref,
    pk_ref,
    pq_ref,
    sq_ref,
    g_ref,
    out_ref,
    mass_ref,
    raw_ref,
    cos_ref,
    sin_ref,
    gain_ref,
    dq_ref,
    dkv_ref,
    dgain_ref,
    acc,
):
    block = pl.program_id(0)
    runs = kv_ref.shape[0]
    rows = q_ref.shape[0]
    group = q_ref.shape[1] // (kv_heads * head)
    scale = head ** (-0.5)
    queries = head_parts(q_ref[...], head, kv_heads)
    grads = head_parts(g_ref[...], head, kv_heads)
    mixed = head_parts(out_ref[...], head, kv_heads)
    dots = []
    for grad, own in zip(grads, mixed):
        dot = jnp.sum(grad.astype(F32) * own, axis=1, keepdims=True)
        dots.append(jnp.broadcast_to(dot, (group * rows, 128)).T[0:1])
    newest, oldest = pq_ref[0], sq_ref[0]

    @pl.when(block == 0)
    def _():
        acc[...] = jnp.zeros_like(acc)
        dgain_ref[...] = jnp.zeros_like(dgain_ref)

    def step(j, dqs):
        at = pl.ds(pl.multiple_of(j * SUB, SUB), SUB)
        packed = jnp.broadcast_to(pk_ref[j], (8, pk_ref.shape[2])).T[:, :1]
        allowed = (packed <= newest) & (packed >= oldest)
        result = []
        for n, dq in enumerate(dqs):
            keys, values = keys_and_values(kv_ref, at, n, head)
            scores = nt(keys, queries[n]) * (scale * LOG2E) - mass_ref[0, n : n + 1]
            probs = jnp.where(allowed, jnp.exp2(scores), 0.0)
            dscores = (probs * (nt(values, grads[n]) - dots[n])).astype(BF16)
            key_cols = slice(2 * n * head, (2 * n + 1) * head)
            value_cols = slice((2 * n + 1) * head, (2 * n + 2) * head)
            acc[:, at, key_cols] += nn(dscores, queries[n]).reshape(runs, SUB, head)
            acc[:, at, value_cols] += nn(probs.astype(BF16), grads[n]).reshape(runs, SUB, head)
            result.append(dq + tn(dscores, keys))
        return tuple(result)

    zero = jnp.zeros((group * rows, head), F32)
    dqs = lax.fori_loop(lo_ref[block], hi_ref[block], step, (zero,) * kv_heads)
    cosine, sine = cos_ref[...], sin_ref[...]
    for n in range(kv_heads):
        for g in range(group):
            own = unturn(dqs[n][g * rows : (g + 1) * rows] * scale, cosine, sine)
            cols = slice((n * group + g) * head, (n * group + g + 1) * head)
            raw = raw_ref[:, cols]
            inverse = lax.rsqrt(jnp.mean(raw * raw, axis=-1, keepdims=True) + EPSILON)
            unit = raw * inverse
            dgain_ref[...] += jnp.sum(own * unit, axis=0, keepdims=True)
            dq_ref[:, cols] = back(own, unit, inverse, gain_ref[...]).astype(BF16)

    @pl.when(block == pl.num_programs(0) - 1)
    def _():
        for n in range(kv_heads):
            key_cols = slice(2 * n * head, (2 * n + 1) * head)
            value_cols = slice((2 * n + 1) * head, (2 * n + 2) * head)
            dkv_ref[:, :, key_cols] = (acc[:, :, key_cols] * scale).astype(BF16)
            dkv_ref[:, :, value_cols] = acc[:, :, value_cols].astype(BF16)


def attend_backward(query, kv, marks, grad, out, mass, raw, cosine, sine, gain, head, kv_heads):
    lo, hi, pk_row, unused, unused_too, pq_row, sq_row = marks
    rows, width = query.shape
    group = width // (kv_heads * head)
    blocks = rows // QROWS
    own = lambda i, *s: (i, 0)
    line = lambda i, *s: (i, 0, 0)
    return pl.pallas_call(
        functools.partial(backward_kernel, head, kv_heads),
        grid_spec=pltpu.PrefetchScalarGridSpec(
            num_scalar_prefetch=2,
            grid=(blocks,),
            in_specs=[
                pl.BlockSpec((QROWS, width), own),
                whole(kv.shape),
                whole(pk_row.shape),
                pl.BlockSpec((1, 1, group * QROWS), line),
                pl.BlockSpec((1, 1, group * QROWS), line),
                pl.BlockSpec((QROWS, width), own),
                pl.BlockSpec((QROWS, width), own),
                pl.BlockSpec((1, kv_heads, group * QROWS), line),
                pl.BlockSpec((QROWS, width), own),
                pl.BlockSpec((QROWS, head), own),
                pl.BlockSpec((QROWS, head), own),
                whole((1, head)),
            ],
            out_specs=[pl.BlockSpec((QROWS, width), own), whole(kv.shape), whole((1, head))],
            scratch_shapes=[VMEM(kv.shape, F32)],
        ),
        out_shape=[
            jax.ShapeDtypeStruct((rows, width), BF16),
            jax.ShapeDtypeStruct(kv.shape, BF16),
            jax.ShapeDtypeStruct((1, head), F32),
        ],
        compiler_params=params(56),
        name="attend_backward",
    )(lo, hi, query, kv, pk_row, pq_row, sq_row, grad, out, mass, raw, cosine, sine, gain)


def key_back_kernel(head, kv_heads, grad_ref, raw_ref, cos_ref, sin_ref, gain_ref, out_ref, dgain_ref):
    cosine, sine = cos_ref[...], sin_ref[...]
    total = jnp.zeros((1, head), F32)
    for n in range(kv_heads):
        at = 2 * n * head
        own = unturn(grad_ref[:, at : at + head].astype(F32), cosine, sine)
        raw = raw_ref[:, n * head : (n + 1) * head]
        inverse = lax.rsqrt(jnp.mean(raw * raw, axis=-1, keepdims=True) + EPSILON)
        unit = raw * inverse
        total = total + jnp.sum(own * unit, axis=0, keepdims=True)
        out_ref[:, at : at + head] = back(own, unit, inverse, gain_ref[...]).astype(BF16)
        out_ref[:, at + head : at + 2 * head] = grad_ref[:, at + head : at + 2 * head]
    dgain_ref[...] = total


def key_back(grad, raw, cosine, sine, gain, kv_heads):
    rows = grad.shape[0]
    head = gain.shape[1]
    keys = pl.BlockSpec((rows, kv_heads * head), lambda i: (0, raw.shape[1] // (kv_heads * head) - 1))
    return pl.pallas_call(
        functools.partial(key_back_kernel, head, kv_heads),
        grid=(1,),
        out_shape=[jax.ShapeDtypeStruct(grad.shape, BF16), jax.ShapeDtypeStruct((1, head), F32)],
        in_specs=[whole(grad.shape), keys, whole((rows, head)), whole((rows, head)), whole((1, head))],
        out_specs=[whole(grad.shape), whole((1, head))],
        compiler_params=params(32),
        name="key_back",
    )(grad, raw, cosine, sine, gain)


LOAD, SAVE = "load", "save"


class One:
    def __init__(self, array, index):
        self.array, self.index = array, index
        self.shape, self.dtype = array.shape[1:], array.dtype


def source(item):
    return item.array if isinstance(item, One) else item


class Loaded:
    def __init__(self, source, held, sem):
        self.ref = held
        self.copy = lambda: pltpu.make_async_copy(source, held, sem)

    def start(self):
        self.copy().start()

    def wait(self):
        self.copy().wait()


class Saved:
    def __init__(self, held, result, sems, axis):
        self.ref, self.result, self.sems, self.axis = held, result, sems, axis
        self.count = sems.shape[0]

    def part(self, i):
        size = self.ref.shape[self.axis] // self.count
        at = pl.ds(pl.multiple_of(i * size, size), size)
        return (at, slice(None)) if self.axis == 0 else (slice(None), at)

    def copy(self, i):
        at = self.part(i)
        return pltpu.make_async_copy(self.ref.at[at], self.result.at[at], self.sems.at[i])

    def save(self, i):
        self.copy(i).start()

    def finish(self):
        def one(i, carry):
            self.copy(i).wait()
            return carry

        lax.fori_loop(0, self.count, one, 0)


def run_jobs(n_tp, line, jobs, collective, megabytes, name, alias=None):
    rows, width = line[2], line[3]
    dma = pltpu.SemaphoreType.DMA
    line_scratch = [VMEM((rows, width), BF16)] * 5 + [dma((2, CHUNKS)), dma((2, CHUNKS))]
    parts = [(line[0], line[1], line_scratch)] + [job[:3] for job in jobs]
    arrays = [source(array) for part in parts for array, unused in part[0]]
    spec = lambda how: pl.BlockSpec(memory_space=VMEM if how is VMEM else ANY)
    scratch_shapes, plan = [], []
    for ins, outs, scratch in parts:
        at = len(scratch_shapes)
        scratch_shapes += scratch
        plan.append([range(at, len(scratch_shapes)), {}, {}])
        for i, (array, how) in enumerate(ins):
            if how is LOAD:
                plan[-1][1][i] = len(scratch_shapes)
                scratch_shapes += [VMEM(array.shape[-2:], array.dtype), dma]
        for i, (out, how) in enumerate(outs):
            if isinstance(how, tuple):
                plan[-1][2][i] = len(scratch_shapes)
                scratch_shapes += [VMEM(out.shape, out.dtype), dma((how[1],))]
    n_ins = sum(len(part[0]) for part in parts)
    n_outs = sum(len(part[1]) for part in parts)

    def kernel(*refs):
        ins, outs, scratch = refs[:n_ins], refs[n_ins : n_ins + n_outs], refs[n_ins + n_outs :]
        groups, loads, saves = [], [], []
        in_at = out_at = 0
        for (own_ins, own_outs, unused), (own_scratch, loaded, saved) in zip(parts, plan):
            in_refs = list(ins[in_at : in_at + len(own_ins)])
            out_refs = list(outs[out_at : out_at + len(own_outs)])
            in_at += len(own_ins)
            out_at += len(own_outs)
            for i, k in loaded.items():
                which = own_ins[i][0]
                at = in_refs[i].at[which.index] if isinstance(which, One) else in_refs[i]
                in_refs[i] = Loaded(at, scratch[k], scratch[k + 1])
                loads.append(in_refs[i])
            for i, k in saved.items():
                out_refs[i] = Saved(scratch[k], out_refs[i], scratch[k + 1], own_outs[i][1][2])
                saves.append(out_refs[i])
            groups.append((in_refs, out_refs, [scratch[k] for k in own_scratch]))
        for item in loads:
            item.start()
        bound = [job[3](*groups[i + 1]) for i, job in enumerate(jobs)]
        line_sum(n_tp, groups[0][2], line[4](*groups[0][:2]), bound)
        for item in saves:
            item.finish()

    return pl.pallas_call(
        kernel,
        out_shape=[out[0] for part in parts for out in part[1]],
        in_specs=[spec(how) for part in parts for unused, how in part[0]],
        out_specs=[spec(how) for part in parts for unused, how in part[1]],
        scratch_shapes=scratch_shapes,
        input_output_aliases=alias or {},
        compiler_params=params(megabytes, collective),
        name=name,
    )(*arrays)


def piece(c, rows):
    return pl.ds(pl.multiple_of(c * rows, rows), rows)


def line_sum(n_tp, scratch, main, jobs):
    part, from_left, from_right, to_right, to_left, send_sem, recv_sem = scratch
    produce_ready, consume_ready, produce, consume = main
    chunks = CHUNKS
    size = part.shape[0] // chunks
    groups = part.shape[0] // GROUP
    place = lax.axis_index("tp")
    line = lax.axis_index("ctx")
    has_left, has_right = place > 0, place < n_tp - 1
    barrier = pltpu.get_barrier_semaphore()
    peers = [peer for job in jobs for peer in job[0]]
    for peer in peers:
        pl.semaphore_signal(barrier, inc=1, device_id=peer, device_id_type=MESH)

    @pl.when(has_left)
    def _():
        pl.semaphore_signal(barrier, inc=1, device_id=(line, place - 1), device_id_type=MESH)

    @pl.when(has_right)
    def _():
        pl.semaphore_signal(barrier, inc=1, device_id=(line, place + 1), device_id_type=MESH)

    def fill(g):
        part[piece(g, GROUP), :] = produce(g).astype(BF16)

    for item in produce_ready:
        item.wait()
    fill(0)
    pl.semaphore_wait(
        barrier, has_left.astype(jnp.int32) + has_right.astype(jnp.int32) + len(peers)
    )
    for job in jobs:
        job[1]()

    def right(c):
        return pltpu.make_async_remote_copy(
            src_ref=to_right.at[piece(c, size)],
            dst_ref=from_left.at[piece(c, size)],
            send_sem=send_sem.at[0, c],
            recv_sem=recv_sem.at[0, c],
            device_id=(line, place + 1),
            device_id_type=MESH,
        )

    def left(c):
        return pltpu.make_async_remote_copy(
            src_ref=to_left.at[piece(c, size)],
            dst_ref=from_right.at[piece(c, size)],
            send_sem=send_sem.at[1, c],
            recv_sem=recv_sem.at[1, c],
            device_id=(line, place - 1),
            device_id_type=MESH,
        )

    def plus(a, b):
        return (a.astype(F32) + b.astype(F32)).astype(BF16)

    late = LAG * jnp.maximum(place, n_tp - 1 - place)

    def step(s, carry):
        c_right = s - LAG * place
        c_left = s - LAG * (n_tp - 1 - place)
        c_out = s - late

        @pl.when((c_right >= 0) & (c_right < chunks))
        def _():
            at = piece(c_right, size)

            @pl.when(jnp.logical_not(has_left))
            def _():
                to_right[at, :] = part[at, :]

            @pl.when(has_left)
            def _():
                right(c_right).wait_recv()
                to_right[at, :] = plus(part[at, :], from_left[at, :])

            @pl.when(has_right)
            def _():
                right(c_right).start()

        @pl.when((c_left >= 0) & (c_left < chunks))
        def _():
            at = piece(c_left, size)

            @pl.when(jnp.logical_not(has_right))
            def _():
                to_left[at, :] = part[at, :]

            @pl.when(has_right)
            def _():
                left(c_left).wait_recv()
                to_left[at, :] = plus(part[at, :], from_right[at, :])

            @pl.when(has_left)
            def _():
                left(c_left).start()

        @pl.when((s + 1 < groups))
        def _():
            fill(s + 1)

        @pl.when(s == 1)
        def _():
            for item in consume_ready:
                item.wait()

        @pl.when((c_out >= 0) & (c_out < chunks))
        def _():
            at = piece(c_out, size)

            @pl.when(has_right)
            def _():
                consume(c_out, to_right[at, :].astype(F32) + from_right[at, :].astype(F32))

            @pl.when(jnp.logical_not(has_right))
            def _():
                consume(c_out, to_right[at, :].astype(F32))

        for job in jobs:
            job[2](s)
        return carry

    lax.fori_loop(0, chunks + LAG * (n_tp - 1), step, 0)

    for job in jobs:
        job[3]()

    def finish(c, carry):
        @pl.when(has_right)
        def _():
            right(c).wait_send()

        @pl.when(has_left)
        def _():
            left(c).wait_send()

        return carry

    lax.fori_loop(0, chunks, finish, 0)


def mean_square(values):
    return jnp.mean(values * values, axis=-1, keepdims=True)


def shape(rows, width, dtype=BF16):
    return jax.ShapeDtypeStruct((rows, width), dtype)


def attn_out_line(mixed, place, weight, inputs, gain):
    rows, width = inputs.shape
    size = rows // CHUNKS
    groups = rows // GROUP

    def bind(ins, outs):
        mixed_in, place_in, w_in, x_in, gain_ref = ins
        own_out, middle_out, normed_out = outs

        def produce(g):
            own = nn(place_in.ref[piece(g, GROUP), :], mixed_in.ref[...].astype(BF16)).astype(BF16)
            own_out.ref[piece(g, GROUP), :] = own
            own_out.save(g)
            return nt(own, w_in.ref[...])

        def consume(c, total):
            at = piece(c, size)
            middle = x_in.ref[at, :].astype(F32) + total
            middle_out.ref[at, :] = middle.astype(BF16)
            middle_out.save(c)
            unit = middle * lax.rsqrt(mean_square(middle) + EPSILON)
            normed_out.ref[at, :] = (unit * gain_ref[...]).astype(BF16)
            normed_out.save(c)

        return [mixed_in, place_in, w_in], [x_in], produce, consume

    return (
        [(mixed, LOAD), (place, LOAD), (weight, LOAD), (inputs, LOAD), (gain, VMEM)],
        [
            (shape(*mixed.shape), (SAVE, groups, 0)),
            (shape(rows, width), (SAVE, CHUNKS, 0)),
            (shape(rows, width), (SAVE, CHUNKS, 0)),
        ],
        rows,
        width,
        bind,
    )


def middle_back_line(part, grad, middle, gain, weight):
    rows, width = grad.shape
    size = rows // CHUNKS
    groups = rows // GROUP
    each = GROUP // size

    def bind(ins, outs):
        part_in, g_in, middle_in, gain_ref, w_in = ins
        low_out, mixed_out, dgain_ref = outs
        dgain_ref[...] = jnp.zeros_like(dgain_ref)

        def produce(g):
            return part_in.ref[piece(g, GROUP), :]

        def consume(c, total):
            at = piece(c, size)
            middle = middle_in.ref[at, :].astype(F32)
            inverse = lax.rsqrt(mean_square(middle) + EPSILON)
            unit = middle * inverse
            dgain_ref[...] += jnp.sum(total * unit, axis=0, keepdims=True)
            grad = g_in.ref[at, :].astype(F32) + back(total, unit, inverse, gain_ref[...])
            low_out.ref[at, :] = grad.astype(BF16)
            low_out.save(c)

            @pl.when(lax.rem(c, each) == each - 1)
            def _():
                g = c // each
                at = piece(g, GROUP)
                mixed_out.ref[at, :] = nn(low_out.ref[at, :], w_in.ref[...]).astype(BF16)
                mixed_out.save(g)

        return [part_in], [g_in, middle_in, w_in], produce, consume

    return (
        [(part, LOAD), (grad, LOAD), (middle, LOAD), (gain, VMEM), (weight, LOAD)],
        [
            (shape(rows, width), (SAVE, CHUNKS, 0)),
            (shape(rows, weight.shape[1]), (SAVE, groups, 0)),
            (shape(1, width, F32), VMEM),
        ],
        rows,
        width,
        bind,
    )


def input_back_line(gq, gkv, place, weight, inputs, mid, gain):
    rows, width = inputs.shape
    size = rows // CHUNKS

    def bind(ins, outs):
        gq_in, gkv_in, place_in, w_in, x_in, mid_in, gain_ref = ins
        out, dgain_ref = outs
        queries = gq.shape[1]
        dgain_ref[...] = jnp.zeros_like(dgain_ref)

        def produce(g):
            slots = place_in.ref[piece(g, GROUP), :]
            own_q = nn(slots, gq_in.ref[...]).astype(BF16)
            own_kv = nn(slots, gkv_in.ref[...]).astype(BF16)
            return nt(own_q, w_in.ref[:, :queries]) + nt(own_kv, w_in.ref[:, queries:])

        def consume(c, total):
            at = piece(c, size)
            x = x_in.ref[at, :].astype(F32)
            inverse = lax.rsqrt(mean_square(x) + EPSILON)
            unit = x * inverse
            dgain_ref[...] += jnp.sum(total * unit, axis=0, keepdims=True)
            grad = mid_in.ref[at, :].astype(F32) + back(total, unit, inverse, gain_ref[...])
            out.ref[at, :] = grad.astype(BF16)
            out.save(c)

        return [gq_in, gkv_in, place_in, w_in], [x_in, mid_in], produce, consume

    return (
        [(item, LOAD) for item in (gq, gkv, place, weight, inputs, mid)] + [(gain, VMEM)],
        [(shape(rows, width), (SAVE, CHUNKS, 0)), (shape(1, width, F32), VMEM)],
        rows,
        width,
        bind,
    )


def gather_job(own, n_ctx):
    chips = n_ctx // 2
    dma = pltpu.SemaphoreType.DMA

    def bind(ins, outs, scratch):
        peers, start, relay, finish = gather_parts(ins, outs, scratch, n_ctx)

        def hook(s):
            for d in range(1, chips):

                @pl.when(s == CHUNKS - 2 * chips + 2 * d)
                def _(d=d):
                    relay(0, d)

        return peers, start, hook, finish

    return (
        [(own, ANY)],
        [(shape(n_ctx * own.shape[0], own.shape[1]), ANY)],
        [dma((1,))] + [dma((1, chips))] * 4,
        bind,
    )


def mlp_job(middle, normed, grad, weight, n_tp):
    rows, width = normed.shape
    units = weight.shape[1] // 3
    tile = 256
    tiles, down_tiles = units // tile, width // tile
    share = 1.0 / n_tp
    every = max(1, CHUNKS // 16)
    dma = pltpu.SemaphoreType.DMA

    def bind(ins, outs, scratch):
        middle_in, x_in, g_in, w_hbm = ins
        hid, gg, gu, down_out, gn_out = outs
        w_ref, sem = scratch

        def load(t, part):
            at = pl.ds(pl.multiple_of(part * units + t * tile, tile), tile)
            return pltpu.make_async_copy(w_hbm.at[:, at], w_ref.at[:, at], sem.at[part, t])

        def start():
            for t in range(tiles):
                for part in range(3):
                    load(t, part).start()

        def first(t):
            for part in range(3):
                load(t, part).wait()
            cols = [
                pl.ds(pl.multiple_of(part * units + t * tile, tile), tile) for part in range(3)
            ]
            gate = nn(x_in.ref[...], w_ref[:, cols[0]])
            up = nn(x_in.ref[...], w_ref[:, cols[1]])
            grad = nn(g_in.ref[...], w_ref[:, cols[2]])
            sigmoid = jax.nn.sigmoid(gate)
            silu = gate * sigmoid
            hid.ref[:, cols[0]] = (silu * up).astype(BF16)
            gu.ref[:, cols[0]] = (grad * silu).astype(BF16)
            gg.ref[:, cols[0]] = (grad * up * sigmoid * (1.0 + gate * (1.0 - sigmoid))).astype(BF16)
            for out in (hid, gu, gg):
                out.save(t)

        def second(t):
            at = pl.ds(pl.multiple_of(t * tile, tile), tile)
            down = nt(hid.ref[...], w_ref[at, 2 * units :])
            down_out.ref[:, at] = (down + middle_in.ref[:, at].astype(F32) * share).astype(BF16)
            gn_out.ref[:, at] = (
                nt(gg.ref[...], w_ref[at, :units]) + nt(gu.ref[...], w_ref[at, units : 2 * units])
            ).astype(BF16)
            down_out.save(t)
            gn_out.save(t)

        def hook(s):
            h = (s - 1) // every
            now = lax.rem(s - 1, every) == 0

            @pl.when(s == 1)
            def _():
                for item in (middle_in, x_in, g_in):
                    item.wait()

            @pl.when(now & (s >= 1) & (h < tiles))
            def _():
                first(h)

            @pl.when(now & (h >= tiles) & (h < tiles + down_tiles))
            def _():
                second(h - tiles)

        return [], start, hook, lambda: None

    return (
        [(middle, LOAD), (normed, LOAD), (grad, LOAD), (weight, ANY)],
        [(shape(rows, units), (SAVE, tiles, 1))] * 3
        + [(shape(rows, width), (SAVE, down_tiles, 1))] * 2,
        [VMEM(weight.shape, BF16), dma((3, tiles))],
        bind,
    )


def weight_job(lefts, groups, tile, every, room):
    rows, width = lefts[0].shape
    rights = [side for unused, sides in groups for side in sides]
    counts = [sides[0].shape[1] // tile for unused, sides in groups]
    total = sum(counts)
    dma = pltpu.SemaphoreType.DMA
    sources = list(lefts) + rights

    def bind(ins, outs, scratch):
        (out_hbm,) = outs
        held = [item.ref for item in ins[: len(sources)]]
        out_buf, out_sem = scratch

        def save(h):
            slot = lax.rem(h, 2)
            return pltpu.make_async_copy(
                out_buf.at[slot],
                out_hbm.at[:, pl.ds(pl.multiple_of(h * tile, tile), tile)],
                out_sem.at[slot],
            )

        def hook(s):
            @pl.when(s == 1)
            def _():
                for item in ins[: len(sources)]:
                    item.wait()

            h = (s - 1) // every
            now = (s >= 1) & (lax.rem(s - 1, every) == 0) & (h < total)

            @pl.when(now & (h >= 2))
            def _():
                save(h - 2).wait()

            first, at = 0, len(lefts)
            for (indices, sides), count in zip(groups, counts):
                left_refs = [held[i] for i in indices]
                right_refs = held[at : at + len(sides)]
                at += len(sides)

                @pl.when(now & (h >= first) & (h < first + count))
                def _(left_refs=left_refs, right_refs=right_refs, first=first):
                    cols = pl.ds(pl.multiple_of((h - first) * tile, tile), tile)
                    grads = tn(left_refs[0][...], right_refs[0][:, cols])
                    for left_ref, right_ref in zip(left_refs[1:], right_refs[1:]):
                        grads = grads + tn(left_ref[...], right_ref[:, cols])
                    out_buf[lax.rem(h, 2)] = grads.astype(BF16)

                first += count

            @pl.when(now)
            def _():
                save(h).start()

        def finish():
            save(total - 2).wait()
            save(total - 1).wait()

        return [], lambda: None, hook, finish

    return (
        [(item, LOAD) for item in sources] + [(room, ANY)],
        [(shape(width, total * tile), ANY)],
        [VMEM((2, width, tile), BF16), dma((2,))],
        bind,
    )


def scatter_job(whole_rows, n_ctx, dtype, first, second):
    total, width = whole_rows.shape
    rows = total // n_ctx
    chips = n_ctx // 2
    dma = pltpu.SemaphoreType.DMA

    def bind(ins, outs, scratch):
        (source,), (out_ref,) = ins, outs
        mine, near, far, load_sem, near_send, near_recv, far_send, far_recv = scratch
        me, column = lax.axis_index("ctx"), lax.axis_index("tp")
        chip, core = me // 2, lax.rem(me, 2)

        def block(d, which):
            at = (jnp.bitwise_xor(chip, d) * 2 + which) * rows
            return source.at[pl.ds(pl.multiple_of(at, rows), rows)]

        def load(d):
            return pltpu.make_async_copy(block(d, core), mine.at[d], load_sem.at[d])

        def beside(d):
            return pltpu.make_async_remote_copy(
                src_ref=block(d, 1 - core),
                dst_ref=near.at[d],
                send_sem=near_send.at[d],
                recv_sem=near_recv.at[d],
                device_id=(chip * 2 + 1 - core, column),
                device_id_type=MESH,
            )

        def across(d):
            return pltpu.make_async_remote_copy(
                src_ref=mine.at[d],
                dst_ref=far.at[d - 1],
                send_sem=far_send.at[d],
                recv_sem=far_recv.at[d],
                device_id=(jnp.bitwise_xor(chip, d) * 2 + core, column),
                device_id_type=MESH,
            )

        peers = [(chip * 2 + 1 - core, column)] + [
            (jnp.bitwise_xor(chip, d) * 2 + core, column) for d in range(1, chips)
        ]
        order = list(range(chips - 1, -1, -1))

        def start():
            for d in order:
                load(d).start()
                beside(d).start()

        def near_sum():
            for d in order:
                load(d).wait()
                beside(d).wait_recv()
                mine[d] = (mine[d].astype(F32) + near[d].astype(F32)).astype(BF16)
                if d > 0:
                    across(d).start()

        def far_sum():
            for d in range(1, chips):
                across(d).wait_recv()
            result = mine[0].astype(F32)
            for d in range(1, chips):
                result = result + far[d - 1].astype(F32)
            out_ref[...] = result.astype(dtype)

        def hook(s):
            @pl.when(s == first)
            def _():
                near_sum()

            @pl.when(s == second)
            def _():
                far_sum()

        def finish():
            for d in range(chips):
                beside(d).wait_send()
                if d > 0:
                    across(d).wait_send()

        return peers, start, hook, finish

    return (
        [(whole_rows, ANY)],
        [(shape(rows, width, dtype), VMEM)],
        [
            VMEM((chips, rows, width), BF16),
            VMEM((chips, rows, width), BF16),
            VMEM((chips - 1, rows, width), BF16),
        ]
        + [dma((chips,))] * 5,
        bind,
    )


def weight_kernel(starts, parts, *refs):
    out_ref = refs[-1]
    step = pl.program_id(0)
    at = 0
    for index, (lefts, first, last) in enumerate(starts):
        left_refs = [refs[i] for i in lefts]
        right_refs = refs[parts + at : parts + at + len(lefts)]
        at += len(lefts)

        @pl.when((step >= first) & (step < last))
        def _(left_refs=left_refs, right_refs=right_refs):
            total = tn(left_refs[0][...], right_refs[0][...])
            for left_ref, right_ref in zip(left_refs[1:], right_refs[1:]):
                total = total + tn(left_ref[...], right_ref[...])
            out_ref[...] = total.astype(BF16)


def weight_grads(lefts, groups, tile):
    rows, width = lefts[0].shape
    starts, specs, rights, at = [], [], [], 0
    for indices, sides in groups:
        tiles = sides[0].shape[1] // tile
        starts.append((indices, at, at + tiles))
        for side in sides:
            rights.append(side)
            specs.append(
                pl.BlockSpec(
                    (rows, tile), lambda j, at=at, tiles=tiles: (0, jnp.clip(j - at, 0, tiles - 1))
                )
            )
        at += tiles
    return pl.pallas_call(
        functools.partial(weight_kernel, starts, len(lefts)),
        grid=(at,),
        out_shape=jax.ShapeDtypeStruct((width, at * tile), BF16),
        in_specs=[whole((rows, width))] * len(lefts) + specs,
        out_specs=pl.BlockSpec((width, tile), lambda j: (0, j)),
        compiler_params=params(60),
        name="weight_grads",
    )(*lefts, *rights)


def gains_kernel(n_ctx, n_tp, x_ref, out_ref, got, send_sem, recv_sem, line_got, line_send, line_recv):
    me, place = lax.axis_index("ctx"), lax.axis_index("tp")
    barrier = pltpu.get_barrier_semaphore()
    others = [lax.rem(me + d, n_ctx) for d in range(1, n_ctx)]
    members = [lax.rem(place + d, n_tp) for d in range(1, n_tp)]
    for other in others:
        pl.semaphore_signal(barrier, inc=1, device_id=(other, place), device_id_type=MESH)
    for member in members:
        pl.semaphore_signal(barrier, inc=1, device_id=(me, member), device_id_type=MESH)
    pl.semaphore_wait(barrier, n_ctx + n_tp - 2)
    copies = [
        pltpu.make_async_remote_copy(
            src_ref=x_ref.at[other],
            dst_ref=got.at[d],
            send_sem=send_sem.at[d],
            recv_sem=recv_sem.at[d],
            device_id=(other, place),
            device_id_type=MESH,
        )
        for d, other in enumerate(others)
    ]
    for copy in copies:
        copy.start()
    total = x_ref[me]
    for d, copy in enumerate(copies):
        copy.wait()
        total = total + got[d]
    out_ref[...] = total
    copies = [
        pltpu.make_async_remote_copy(
            src_ref=out_ref,
            dst_ref=line_got.at[d],
            send_sem=line_send.at[d],
            recv_sem=line_recv.at[d],
            device_id=(me, member),
            device_id_type=MESH,
        )
        for d, member in enumerate(members)
    ]
    for copy in copies:
        copy.start()
    low = total[4:]
    for d, copy in enumerate(copies):
        copy.wait()
        low = low + line_got[d, 4:, :]
    out_ref[4:, :] = low


def sum_gains(blocks, n_ctx, n_tp, collective):
    dma = pltpu.SemaphoreType.DMA
    return pl.pallas_call(
        functools.partial(gains_kernel, n_ctx, n_tp),
        out_shape=jax.ShapeDtypeStruct((8, 128), F32),
        in_specs=[pl.BlockSpec(memory_space=VMEM)],
        out_specs=pl.BlockSpec(memory_space=VMEM),
        scratch_shapes=[
            VMEM((n_ctx - 1, 8, 128), F32),
            dma((n_ctx - 1,)),
            dma((n_ctx - 1,)),
            VMEM((n_tp - 1, 8, 128), F32),
            dma((n_tp - 1,)),
            dma((n_tp - 1,)),
        ],
        compiler_params=params(16, collective),
        name="sum_gains",
    )(blocks)


def sort_runs(packed_runs):
    place = jnp.sum((packed_runs[:, None, :] < packed_runs[:, :, None]).astype(jnp.int32), axis=2)
    slots = jnp.arange(packed_runs.shape[1], dtype=jnp.int32)
    in_order = jnp.sum(
        jnp.where(place[:, :, None] == slots[None, None, :], packed_runs[:, :, None], 0), axis=1
    )
    return place, in_order


def layout(lengths_row, order_row, rank, n_ctx, head, group):
    runs = order_row.reshape(n_ctx, -1)
    rows = runs.shape[1]
    place, in_order = sort_runs(runs)
    own_place = lax.dynamic_index_in_dim(place, rank, 0, keepdims=False)
    packed = lax.dynamic_index_in_dim(in_order, rank, 0, keepdims=False)
    starts = jnp.cumsum(lengths_row) - lengths_row
    first = jnp.max(jnp.where(starts[None, :] <= packed[:, None], starts[None, :], 0), axis=1)
    position = packed - first
    inverse = jnp.exp(jnp.arange(head // 2, dtype=F32) * (-2.0 * math.log(THETA) / head))
    angles = position.astype(F32)[:, None] * inverse[None, :]
    cosine, sine = jnp.cos(angles), jnp.sin(angles)
    cosine = jnp.concatenate([cosine, cosine], axis=1)
    sine = jnp.concatenate([-sine, sine], axis=1)
    slots = jnp.arange(rows, dtype=jnp.int32)
    to_slot = (own_place[:, None] == slots[None, :]).astype(BF16)
    to_sorted = (own_place[None, :] == slots[:, None]).astype(BF16)
    blocks = rows // SUB
    grouped = in_order.reshape(n_ctx, blocks, SUB)
    smallest = jnp.min(grouped[:, :, 0], axis=0)
    largest = jnp.max(grouped[:, :, SUB - 1], axis=0)
    oldest = first.reshape(-1, QROWS)[:, 0]
    newest = packed.reshape(-1, QROWS)[:, QROWS - 1]
    lo = jnp.sum((largest[None, :] < oldest[:, None]).astype(jnp.int32), axis=1)
    hi = jnp.sum((smallest[None, :] <= newest[:, None]).astype(jnp.int32), axis=1)
    keys = grouped.transpose(1, 0, 2).reshape(blocks, n_ctx * SUB)
    of_group = lambda row: jnp.tile(row.reshape(-1, 1, QROWS), (1, 1, group))
    marks = (
        lo,
        hi,
        keys[:, None, :],
        packed[:, None],
        first[:, None],
        of_group(packed),
        of_group(first),
    )
    return to_slot, to_sorted, cosine, sine, marks


def on_device(
    n_ctx,
    n_tp,
    hidden_in,
    seq_lengths,
    token_order,
    attn_gain,
    w_query,
    w_key,
    w_value,
    query_gain,
    key_gain,
    w_out,
    mlp_gain,
    w_gate,
    w_up,
    w_down,
    cotangent,
):
    micro_count, rows, width = hidden_in.shape
    head = query_gain.shape[0]
    heads, kv_heads = w_query.shape[1] // head, w_key.shape[1] // head
    rank = lax.axis_index("ctx")
    queries = heads * head
    units = w_gate.shape[1]
    q_gain, k_gain = query_gain[None, :], key_gain[None, :]
    a_gain, m_gain = attn_gain[None, :], mlp_gain[None, :]

    pieces = [w_query]
    for n in range(kv_heads):
        at = slice(n * head, (n + 1) * head)
        pieces += [w_key[:, at], w_value[:, at]]
    qkv_w, out_w = gather_ctx([jnp.concatenate(pieces, axis=1), w_out.T], n_ctx, 0)
    mlp_own = jnp.concatenate([w_gate, w_up, w_down.T], axis=1)
    orders = [layout(seq_lengths[b], token_order[b], rank, n_ctx, head, heads // kv_heads) for b in range(micro_count)]
    inputs = hidden_in.astype(F32)
    inverse = lax.rsqrt(jnp.mean(inputs * inputs, axis=-1, keepdims=True) + EPSILON)
    normed = (inputs * inverse * attn_gain).astype(BF16)
    both = range(micro_count)
    last = micro_count - 1
    sorted_normed = [nn(orders[b][1], normed[b]).astype(BF16) for b in both]
    projected = [
        project_qkv(
            sorted_normed[b], qkv_w, orders[b][2], orders[b][3], q_gain, k_gain, heads, kv_heads
        )
        for b in both
    ]
    kv_own = after([p[1] for p in projected], projected[last][0])
    (kv_first,) = gather_ctx([kv_own[0]], n_ctx, 1)
    kv_all = [kv_first.reshape(n_ctx, rows, -1)]
    mlp_w = lax.all_gather(after(mlp_own, kv_first), "ctx", axis=0, tiled=True)

    def forward(b):
        return attend_forward(projected[b][0], kv_all[b], orders[b][4], head, kv_heads)

    def out_line(b):
        return attn_out_line(attended[b][0], orders[b][0], out_w, One(hidden_in, b), m_gain)

    def middle_line(b):
        return middle_back_line(fed[b][4], One(cotangent, b), middles[b][1], m_gain, out_w)

    def feed(b):
        return mlp_job(middles[b][1], middles[b][2], One(cotangent, b), mlp_w, n_tp)

    attended, middles, fed, mids, backs = [], [], [], [], []
    attended.append(forward(0))
    results = run_jobs(n_tp, out_line(0), [gather_job(kv_own[1], n_ctx)], 2, 40, "attn_out_gather")
    middles.append(results[:3])
    kv_all.append(results[3].reshape(n_ctx, rows, -1))
    attended.append(forward(1))
    results = run_jobs(n_tp, out_line(1), [feed(0)], 3, 60, "attn_out_mlp")
    middles.append(results[:3])
    fed.append(results[3:])
    results = run_jobs(n_tp, middle_line(0), [feed(1)], 4, 60, "middle_back_mlp")
    mids.append(results[:3])
    fed.append(results[3:])

    layer_out = jnp.stack(lax.psum([fed[b][3] for b in both], "tp"))

    def backward(b, grad):
        q, unused, raw = projected[b]
        to_slot, to_sorted, cosine, sine, marks = orders[b]
        g_mixed = nn(to_sorted, grad).astype(BF16)
        mixed_full, mass = attended[b]
        return attend_backward(
            q, kv_all[b], marks, g_mixed, mixed_full, mass, raw, cosine, sine, q_gain, head, kv_heads
        )

    backs.append(backward(0, mids[0][1]))
    tile = 512 if units % 512 == 0 else 256
    line = middle_line(1)
    line[0][0] = (after(line[0][0][0], backs[0][0]), LOAD)
    results = run_jobs(
        n_tp,
        line,
        [
            weight_job(
                [middles[b][2] for b in both] + [One(cotangent, b) for b in both],
                [
                    (tuple(both), [fed[b][1] for b in both]),
                    (tuple(both), [fed[b][2] for b in both]),
                    (tuple(micro_count + b for b in both), [fed[b][0] for b in both]),
                ],
                tile,
                2 * max(1, CHUNKS // 16),
                mlp_w,
            ),
            scatter_job(backs[0][1].reshape(n_ctx * rows, -1), n_ctx, BF16, CHUNKS // 4, CHUNKS),
        ],
        5,
        60,
        "middle_back_weights",
        {5 + 5 * micro_count: 3},
    )
    mids.append(results[:3])
    mlp_grads = lax.psum_scatter(results[3], "ctx", scatter_dimension=0, tiled=True)
    dkv_first = results[4]
    backs.append(backward(1, mids[1][1]))

    def key_part(b, dkv):
        return key_back(dkv, projected[b][2], orders[b][2], orders[b][3], k_gain, kv_heads)

    def in_line(b, gkv):
        return input_back_line(
            backs[b][0], gkv, orders[b][0], qkv_w, One(hidden_in, b), mids[b][0], a_gain
        )

    gkv_first, dk_gain_first = key_part(0, after(dkv_first, backs[1][0]))
    results = run_jobs(
        n_tp,
        in_line(0, gkv_first),
        [scatter_job(backs[1][1].reshape(n_ctx * rows, -1), n_ctx, BF16, CHUNKS // 4, CHUNKS)],
        6,
        60,
        "input_back_keys",
    )
    grad_in_first, da_gain_first, dkv_last = results
    gkv_last, dk_gain_last = key_part(1, dkv_last)
    tile = min(512, 2 * kv_heads * head, queries)
    gkvs = [gkv_first, gkv_last]
    attn_grads = weight_grads(
        [sorted_normed[b] for b in both] + [mids[b][0] for b in both],
        [
            (tuple(both), [backs[b][0] for b in both]),
            (tuple(both), [gkvs[b] for b in both]),
            (tuple(micro_count + b for b in both), [middles[b][0] for b in both]),
        ],
        tile,
    )
    results = run_jobs(
        n_tp,
        in_line(1, gkv_last),
        [scatter_job(attn_grads, n_ctx, F32, CHUNKS // 4, CHUNKS + 2)],
        7,
        60,
        "input_back_weights",
    )
    grad_in_last, da_gain_last, attn_grads = results
    grads_in = [grad_in_first, grad_in_last]
    d_attn_gain = [da_gain_first, da_gain_last]
    d_key_gain = [dk_gain_first, dk_gain_last]

    share = width // n_ctx // 128
    own = lambda gain: sum(gain).reshape(n_ctx, share, 128)
    spread = lambda gain: jnp.broadcast_to(sum(gain)[None], (n_ctx, 1, 128))
    blank = jnp.zeros((n_ctx, 4 - 2 * share, 128), F32)
    low_blank = jnp.zeros((n_ctx, 2, 128), F32)
    gains = sum_gains(
        jnp.concatenate(
            [
                own(d_attn_gain),
                own([mids[b][2] for b in both]),
                blank,
                spread([backs[b][2] for b in both]),
                spread(d_key_gain),
                low_blank,
            ],
            axis=1,
        ),
        n_ctx,
        n_tp,
        8,
    )

    mlp_grads = mlp_grads.astype(F32)
    at = queries
    keys, values = [], []
    for n in range(kv_heads):
        keys.append(attn_grads[:, at : at + head])
        values.append(attn_grads[:, at + head : at + 2 * head])
        at += 2 * head
    return (
        layer_out,
        jnp.stack(grads_in).astype(F32),
        gains[:share].reshape(-1),
        attn_grads[:, :queries],
        jnp.concatenate(keys, axis=1),
        jnp.concatenate(values, axis=1),
        gains[4],
        gains[5],
        attn_grads[:, at:].T,
        gains[share : 2 * share].reshape(-1),
        mlp_grads[:, :units],
        mlp_grads[:, units : 2 * units],
        mlp_grads[:, 2 * units :].T,
    )


def solution(mesh):
    rows = P("ctx", "tp")
    columns = P("tp", "ctx")
    tokens = P(None, "ctx", None)
    in_specs = (
        tokens,
        P(),
        P(),
        P(),
        rows,
        rows,
        rows,
        P(),
        P(),
        columns,
        P(),
        rows,
        rows,
        columns,
        tokens,
    )
    out_specs = (
        tokens,
        tokens,
        P("ctx"),
        rows,
        rows,
        rows,
        P(),
        P(),
        columns,
        P("ctx"),
        rows,
        rows,
        columns,
    )
    return jax.shard_map(
        functools.partial(on_device, mesh.shape["ctx"], mesh.shape["tp"]),
        mesh=mesh,
        in_specs=in_specs,
        out_specs=out_specs,
        check_vma=False,
    )
```

```python
import functools
import math

import jax
import jax.numpy as jnp
from jax import lax
from jax.experimental import pallas as pl
from jax.experimental.pallas import tpu as pltpu
from jax.sharding import PartitionSpec as P

EPSILON = 1e-06
THETA = 1000000.0
F32 = jnp.float32
BF16 = jnp.bfloat16
MESH = pl.DeviceIdType.MESH
VMEM = pltpu.VMEM
ANY = pl.ANY
LOG2E = math.log2(math.e)
SUB = 64
QROWS = 256
CHUNKS = 16
LAG = 2
GROUP = 128


def params(megabytes, collective=None):
    if collective is None:
        return pltpu.CompilerParams(vmem_limit_bytes=megabytes << 20)
    return pltpu.CompilerParams(
        vmem_limit_bytes=megabytes << 20, collective_id=collective, has_side_effects=True
    )


def nt(left_side, right_side):
    return lax.dot_general(
        left_side, right_side, (((1,), (1,)), ((), ())), preferred_element_type=F32
    )


def tn(left_side, right_side):
    return lax.dot_general(
        left_side, right_side, (((0,), (0,)), ((), ())), preferred_element_type=F32
    )


def nn(left_side, right_side):
    return jnp.dot(left_side, right_side, preferred_element_type=F32)


def whole(shape):
    return pl.BlockSpec(shape, lambda *ids: (0,) * len(shape))


def after(value, *others):
    return lax.optimization_barrier((value, others))[0]


def gather_parts(sources, results, sems, n_ctx):
    own_sem, send_sem, recv_sem, pass_sem, take_sem = sems
    count = len(sources)
    me = lax.axis_index("ctx")
    column = lax.axis_index("tp")
    chip, core = me // 2, lax.rem(me, 2)
    chips = n_ctx // 2
    partner = chip * 2 + 1 - core

    def peer(d):
        return jnp.bitwise_xor(chip, d) * 2 + core

    def rows_of(array, owner):
        rows = sources[array].shape[0]
        return results[array].at[pl.ds(pl.multiple_of(owner * rows, rows), rows)]

    def across(array, d):
        return pltpu.make_async_remote_copy(
            src_ref=sources[array],
            dst_ref=rows_of(array, me),
            send_sem=send_sem.at[array, d],
            recv_sem=recv_sem.at[array, d],
            device_id=(peer(d), column),
            device_id_type=MESH,
        )

    def passed(array, d):
        owner = peer(d)
        return pltpu.make_async_remote_copy(
            src_ref=sources[array] if d == 0 else rows_of(array, owner),
            dst_ref=rows_of(array, owner),
            send_sem=pass_sem.at[array, d],
            recv_sem=take_sem.at[array, d],
            device_id=(partner, column),
            device_id_type=MESH,
        )

    def local(array):
        return pltpu.make_async_copy(sources[array], rows_of(array, me), own_sem.at[array])

    def onward(array, d):
        rows = sources[array].shape[0]
        half = rows // 2
        slot = 3 if d == 1 else 0

        def of(owner):
            at = pl.multiple_of(owner * rows + (0 if d == 1 else half), half)
            return results[array].at[pl.ds(at, half)]

        return pltpu.make_async_remote_copy(
            src_ref=of(peer(d)),
            dst_ref=of(peer(d)),
            send_sem=send_sem.at[array, slot],
            recv_sem=recv_sem.at[array, slot],
            device_id=(peer(3 - d), column),
            device_id_type=MESH,
        )

    direct = range(1, chips) if chips != 4 else (1, 2)

    def start():
        for d in direct:
            for array in range(count):
                across(array, d).start()
        for array in range(count):
            passed(array, 0).start()
            local(array).start()

    def relay(array, d):
        if d in direct:
            across(array, d).wait_recv()
            if chips == 4:
                onward(array, d).start()
        else:
            onward(array, 1).wait_recv()
            onward(array, 2).wait_recv()
        passed(array, d).start()

    def finish():
        for array in range(count):
            local(array).wait()
            for d in range(chips):
                if d in direct:
                    across(array, d).wait_send()
                elif d > 0:
                    onward(array, 1).wait_send()
                    onward(array, 2).wait_send()
                passed(array, d).wait_send()
                passed(array, d).wait_recv()

    peers = [(partner, column)] + [(peer(d), column) for d in direct]
    return peers, start, relay, finish


def gather_kernel(index, n_ctx, source_ref, result_ref, *sems):
    peers, start, relay, finish = gather_parts([source_ref.at[index]], [result_ref], sems, n_ctx)
    barrier = pltpu.get_barrier_semaphore()
    for peer in peers:
        pl.semaphore_signal(barrier, inc=1, device_id=peer, device_id_type=MESH)
    pl.semaphore_wait(barrier, len(peers))
    start()
    for d in range(1, n_ctx // 2):
        relay(0, d)
    finish()


def gather_ctx(array, index, n_ctx, collective):
    dma = pltpu.SemaphoreType.DMA
    unused, rows, width = array.shape
    return pl.pallas_call(
        functools.partial(gather_kernel, index, n_ctx),
        out_shape=jax.ShapeDtypeStruct((n_ctx * rows, width), array.dtype),
        in_specs=[pl.BlockSpec(memory_space=ANY)],
        out_specs=pl.BlockSpec(memory_space=ANY),
        scratch_shapes=[dma((1,))] + [dma((1, n_ctx // 2))] * 4,
        compiler_params=params(60, collective),
        name="gather_ctx",
    )(array)


def begin_kernel(
    n_ctx,
    head,
    kv_heads,
    x_hbm,
    order_ref,
    lengths_ref,
    gain_ref,
    frequency_ref,
    wq_ref,
    wk_ref,
    wv_ref,
    wo_ref,
    wg_hbm,
    wu_hbm,
    wd_ref,
    qkv_hbm,
    out_hbm,
    mlp_hbm,
    sorted_ref,
    to_slot_ref,
    to_sorted_ref,
    cos_ref,
    sin_ref,
    keys_ref,
    newest_ref,
    oldest_ref,
    x_ref,
    normed_ref,
    qkv_own,
    wo_turned,
    mlp_own,
    load_sem,
    mlp_sem,
    *gather_sems,
):
    micro_count, rows, width = x_ref.shape
    queries, units = wq_ref.shape[1], wg_hbm.shape[1]
    me = lax.axis_index("ctx")

    def load(b):
        return pltpu.make_async_copy(x_hbm.at[b], x_ref.at[b], load_sem.at[b])

    for b in range(micro_count):
        load(b).start()
    wo_turned[...] = wo_ref[...].T
    qkv_own[:, :queries] = wq_ref[...]
    for n in range(kv_heads):
        at = queries + 2 * n * head
        own = slice(n * head, (n + 1) * head)
        qkv_own[:, at : at + head] = wk_ref[:, own]
        qkv_own[:, at + head : at + 2 * head] = wv_ref[:, own]
    sources = [qkv_own, wo_turned]
    peers, start, relay, finish = gather_parts(sources, [qkv_hbm, out_hbm], gather_sems, n_ctx)
    barrier = pltpu.get_barrier_semaphore()
    for peer in peers:
        pl.semaphore_signal(barrier, inc=1, device_id=peer, device_id_type=MESH)
    pl.semaphore_wait(barrier, len(peers))
    start()
    mlp_loads = [
        pltpu.make_async_copy(item, mlp_own.at[:, slice(i * units, (i + 1) * units)], mlp_sem.at[i])
        for i, item in enumerate((wg_hbm, wu_hbm))
    ]
    for copy in mlp_loads:
        copy.start()
    mlp_own[:, 2 * units :] = wd_ref[...].T

    def relays(low, high):
        for d in range(low, high):
            for item in range(len(sources)):
                relay(item, d)

    across = lax.broadcasted_iota(jnp.int32, (rows, rows), 1)
    down = lax.broadcasted_iota(jnp.int32, (rows, rows), 0)
    column_of = lambda row: jnp.broadcast_to(row, (8, rows)).T[:, :1]

    def in_order(row):
        column = column_of(row)
        place = jnp.sum((row < column).astype(jnp.int32), axis=1, keepdims=True)
        return place, jnp.sum(jnp.where(place == across, column, 0), axis=0, keepdims=True)

    for b in range(micro_count):

        def run(r, carry):
            row = order_ref[pl.ds(b * n_ctx + r, 1), :]
            keys_ref[pl.ds(b * n_ctx + r, 1), :] = in_order(row)[1]
            return carry

        lax.fori_loop(0, n_ctx, run, 0)
        row = order_ref[pl.ds(b * n_ctx + me, 1), :]
        place, packed = in_order(row)
        packed = column_of(packed)
        place_row = jnp.sum((column_of(row) < row).astype(jnp.int32), axis=0, keepdims=True)
        to_slot_ref[b] = (place == across).astype(F32).astype(BF16)
        to_sorted = (place_row == down).astype(F32).astype(BF16)
        to_sorted_ref[b] = to_sorted
        first = jnp.zeros_like(packed)
        begin = lengths_ref[b, 0] * 0
        for i in range(lengths_ref.shape[1]):
            first = jnp.maximum(first, jnp.where(packed >= begin, begin, 0))
            begin = begin + lengths_ref[b, i]
        newest_ref[b] = packed
        oldest_ref[b] = first
        angles = (packed - first).astype(F32) * frequency_ref[0:1, :]
        cos_ref[b] = jnp.cos(angles)
        sin_ref[b] = jnp.sin(angles) * frequency_ref[1:2, :]
        load(b).wait()
        for g in range(rows // GROUP):
            at = slice(g * GROUP, (g + 1) * GROUP)
            x = x_ref[b, at, :].astype(F32)
            inverse = lax.rsqrt(jnp.mean(x * x, axis=-1, keepdims=True) + EPSILON)
            normed_ref[at, :] = (x * inverse * gain_ref[...]).astype(BF16)
        for g in range(rows // GROUP):
            at = slice(g * GROUP, (g + 1) * GROUP)
            sorted_ref[b, at, :] = nn(to_sorted_ref[b, at, :], normed_ref[...]).astype(BF16)
        if b == 0:
            relays(1, min(3, n_ctx // 2))

    for copy in mlp_loads:
        copy.wait()
    mlp_save = pltpu.make_async_copy(mlp_own, mlp_hbm, mlp_sem.at[2])
    mlp_save.start()
    relays(min(3, n_ctx // 2), n_ctx // 2)
    finish()
    mlp_save.wait()


def begin(inputs, order, lengths, gain, frequency, weights, n_ctx, head, kv_heads, collective):
    micro_count, rows, width = inputs.shape
    wq, wk, wv, wo, wg, wu, wd = weights
    dma = pltpu.SemaphoreType.DMA
    chips = n_ctx // 2
    count = 2
    own, queries, units = wq.shape[0], wq.shape[1], wg.shape[1]
    some = lambda *dims: jax.ShapeDtypeStruct(dims, BF16)
    table = lambda *dims: jax.ShapeDtypeStruct(dims, F32)
    ints = lambda *dims: jax.ShapeDtypeStruct(dims, jnp.int32)
    inside, lies = pl.BlockSpec(memory_space=VMEM), pl.BlockSpec(memory_space=ANY)
    return pl.pallas_call(
        functools.partial(begin_kernel, n_ctx, head, kv_heads),
        out_shape=[
            some(n_ctx * own, queries + 2 * wk.shape[1]),
            some(n_ctx * own, wo.shape[0]),
            some(own, 3 * units),
            some(micro_count, rows, width),
            some(micro_count, rows, rows),
            some(micro_count, rows, rows),
            table(micro_count, rows, head),
            table(micro_count, rows, head),
            ints(micro_count * n_ctx, rows),
            ints(micro_count, rows, 1),
            ints(micro_count, rows, 1),
        ],
        in_specs=[lies, inside, pl.BlockSpec(memory_space=pltpu.SMEM), inside, inside]
        + [inside, inside, inside, inside, lies, lies, inside],
        out_specs=[lies] * 3 + [inside] * 8,
        scratch_shapes=[
            VMEM(inputs.shape, BF16),
            VMEM((rows, width), BF16),
            VMEM((own, queries + 2 * wk.shape[1]), BF16),
            VMEM((own, wo.shape[0]), BF16),
            VMEM((own, 3 * units), BF16),
            dma((micro_count,)),
            dma((3,)),
            dma((count,)),
        ]
        + [dma((count, chips))] * 4,
        compiler_params=params(60, collective),
        name="begin",
    )(inputs, order, lengths, gain, frequency, wq, wk, wv, wo, wg, wu, wd)


def qkv_kernel(heads, kv_heads, x_ref, w_ref, cos_ref, sin_ref, qg_ref, kg_ref, q_ref, kv_ref, raw_ref):
    head = qg_ref.shape[1]
    rows = nn(x_ref[...], w_ref[...])
    cosine, sine = cos_ref[...], sin_ref[...]

    def turn(part, gain):
        unit = part * lax.rsqrt(jnp.mean(part * part, axis=-1, keepdims=True) + EPSILON)
        scaled = unit * gain
        return (scaled * cosine + pltpu.roll(scaled, head // 2, 1) * sine).astype(BF16)

    for h in range(heads):
        part = rows[:, h * head : (h + 1) * head]
        raw_ref[:, h * head : (h + 1) * head] = part
        q_ref[:, h * head : (h + 1) * head] = turn(part, qg_ref[...])
    for n in range(kv_heads):
        at = (heads + 2 * n) * head
        part = rows[:, at : at + head]
        raw_ref[:, (heads + n) * head : (heads + n + 1) * head] = part
        kv_ref[:, 2 * n * head : (2 * n + 1) * head] = turn(part, kg_ref[...])
        kv_ref[:, (2 * n + 1) * head : (2 * n + 2) * head] = rows[:, at + head : at + 2 * head].astype(BF16)


def project_qkv(normed, weight, cosine, sine, query_gain, key_gain, heads, kv_heads):
    micro_count, total, width = normed.shape
    head = query_gain.shape[1]
    block = 256
    of = lambda cols: pl.BlockSpec((None, block, cols), lambda b, i: (b, i, 0))
    result = lambda cols, dtype: jax.ShapeDtypeStruct((micro_count, total, cols), dtype)
    return pl.pallas_call(
        functools.partial(qkv_kernel, heads, kv_heads),
        grid=(micro_count, total // block),
        out_shape=[
            result(heads * head, BF16),
            result(2 * kv_heads * head, BF16),
            result((heads + kv_heads) * head, F32),
        ],
        in_specs=[
            of(width),
            whole(weight.shape),
            of(head),
            of(head),
            whole((1, head)),
            whole((1, head)),
        ],
        out_specs=[of(heads * head), of(2 * kv_heads * head), of((heads + kv_heads) * head)],
        compiler_params=params(60),
        name="project_qkv",
    )(normed, weight, cosine, sine, query_gain, key_gain)


def heads_to_rows(block, head):
    return jnp.concatenate(
        [block[:, g * head : (g + 1) * head] for g in range(block.shape[1] // head)], axis=0
    )


def rows_to_heads(block, rows):
    return jnp.concatenate(
        [block[g * rows : (g + 1) * rows] for g in range(block.shape[0] // rows)], axis=1
    )


def head_parts(block, head, kv_heads):
    wide = block.shape[1] // kv_heads
    return [heads_to_rows(block[:, n * wide : (n + 1) * wide], head) for n in range(kv_heads)]


def keys_and_values(kv_ref, at, n, head):
    runs = kv_ref.shape[0]
    take = lambda i: kv_ref[:, at, i * head : (i + 1) * head].reshape(runs * SUB, head)
    return take(2 * n), take(2 * n + 1)


def forward_kernel(head, kv_heads, lo_ref, hi_ref, q_ref, kv_ref, pk_ref, pq_ref, sq_ref, out_ref, mass_ref):
    block = pl.program_id(0)
    rows = q_ref.shape[0]
    wide = q_ref.shape[1] // kv_heads
    group = wide // head
    scale = head ** (-0.5) * LOG2E
    queries = head_parts(q_ref[...], head, kv_heads)
    newest, oldest = pq_ref[...], sq_ref[...]

    def step(j, carry):
        at = pl.ds(pl.multiple_of(j * SUB, SUB), SUB)
        packed = pk_ref[j]
        allowed = (packed <= newest) & (packed >= oldest)
        allowed = jnp.concatenate([allowed] * group, axis=0)
        result = []
        for n, (total, mass) in enumerate(carry):
            keys, values = keys_and_values(kv_ref, at, n, head)
            probs = jnp.where(allowed, jnp.exp2(nt(queries[n], keys) * scale), 0.0)
            for i in range(probs.shape[1] // 128):
                mass = mass + probs[:, i * 128 : (i + 1) * 128]
            result.append((total + nn(probs.astype(BF16), values), mass))
        return tuple(result)

    zero = (jnp.zeros((group * rows, head), F32), jnp.zeros((group * rows, 128), F32))
    results = lax.fori_loop(lo_ref[block], hi_ref[block], step, (zero,) * kv_heads)
    for n, (total, mass) in enumerate(results):
        mass = jnp.sum(mass, axis=1, keepdims=True)
        out_ref[:, n * wide : (n + 1) * wide] = rows_to_heads(total / mass, rows)
        mass_ref[0, n : n + 1] = jnp.broadcast_to(jnp.log2(mass), (group * rows, 128)).T[0:1]


def attend_forward(query, index, kv, marks, head, kv_heads):
    lo, hi, pk_row, pq_col, sq_col = marks[:5]
    unused, rows, width = query.shape
    group = width // (kv_heads * head)
    blocks = rows // QROWS
    own = lambda i, *s: (i, 0)
    return pl.pallas_call(
        functools.partial(forward_kernel, head, kv_heads),
        grid_spec=pltpu.PrefetchScalarGridSpec(
            num_scalar_prefetch=2,
            grid=(blocks,),
            in_specs=[
                pl.BlockSpec((None, QROWS, width), lambda i, *s: (index, i, 0)),
                whole(kv.shape),
                whole(pk_row.shape),
                pl.BlockSpec((QROWS, 1), own),
                pl.BlockSpec((QROWS, 1), own),
            ],
            out_specs=[
                pl.BlockSpec((QROWS, width), own),
                pl.BlockSpec((1, kv_heads, group * QROWS), lambda i, *s: (i, 0, 0)),
            ],
        ),
        out_shape=[
            jax.ShapeDtypeStruct((rows, width), F32),
            jax.ShapeDtypeStruct((blocks, kv_heads, group * QROWS), F32),
        ],
        compiler_params=params(60),
        name="attend_forward",
    )(lo, hi, query, kv, pk_row, pq_col, sq_col)


def back(grad, unit, inverse, gain):
    scaled = grad * gain
    return inverse * (scaled - unit * jnp.mean(scaled * unit, axis=-1, keepdims=True))


def unturn(grad, cosine, sine):
    return grad * cosine - pltpu.roll(grad, grad.shape[1] // 2, 1) * sine


def backward_kernel(
    head,
    kv_heads,
    lo_ref,
    hi_ref,
    q_ref,
    kv_ref,
    pk_ref,
    pq_ref,
    sq_ref,
    g_ref,
    out_ref,
    mass_ref,
    raw_ref,
    cos_ref,
    sin_ref,
    gain_ref,
    dq_ref,
    dkv_ref,
    dgain_ref,
    acc,
):
    block = pl.program_id(0)
    runs = kv_ref.shape[0]
    rows = q_ref.shape[0]
    group = q_ref.shape[1] // (kv_heads * head)
    scale = head ** (-0.5)
    queries = head_parts(q_ref[...], head, kv_heads)
    grads = head_parts(g_ref[...], head, kv_heads)
    mixed = head_parts(out_ref[...], head, kv_heads)
    dots = []
    for grad, own in zip(grads, mixed):
        dot = jnp.sum(grad.astype(F32) * own, axis=1, keepdims=True)
        dots.append(jnp.broadcast_to(dot, (group * rows, 128)).T[0:1])
    newest, oldest = pq_ref[0], sq_ref[0]

    @pl.when(block == 0)
    def _():
        acc[...] = jnp.zeros_like(acc)
        dgain_ref[...] = jnp.zeros_like(dgain_ref)

    def step(j, dqs):
        at = pl.ds(pl.multiple_of(j * SUB, SUB), SUB)
        packed = jnp.broadcast_to(pk_ref[j], (8, pk_ref.shape[2])).T[:, :1]
        allowed = (packed <= newest) & (packed >= oldest)
        result = []
        for n, dq in enumerate(dqs):
            keys, values = keys_and_values(kv_ref, at, n, head)
            scores = nt(keys, queries[n]) * (scale * LOG2E) - mass_ref[0, n : n + 1]
            probs = jnp.where(allowed, jnp.exp2(scores), 0.0)
            dscores = (probs * (nt(values, grads[n]) - dots[n])).astype(BF16)
            key_cols = slice(2 * n * head, (2 * n + 1) * head)
            value_cols = slice((2 * n + 1) * head, (2 * n + 2) * head)
            acc[:, at, key_cols] += nn(dscores, queries[n]).reshape(runs, SUB, head)
            acc[:, at, value_cols] += nn(probs.astype(BF16), grads[n]).reshape(runs, SUB, head)
            result.append(dq + tn(dscores, keys))
        return tuple(result)

    zero = jnp.zeros((group * rows, head), F32)
    dqs = lax.fori_loop(lo_ref[block], hi_ref[block], step, (zero,) * kv_heads)
    cosine, sine = cos_ref[...], sin_ref[...]
    for n in range(kv_heads):
        for g in range(group):
            own = unturn(dqs[n][g * rows : (g + 1) * rows] * scale, cosine, sine)
            cols = slice((n * group + g) * head, (n * group + g + 1) * head)
            raw = raw_ref[:, cols]
            inverse = lax.rsqrt(jnp.mean(raw * raw, axis=-1, keepdims=True) + EPSILON)
            unit = raw * inverse
            dgain_ref[...] += jnp.sum(own * unit, axis=0, keepdims=True)
            dq_ref[:, cols] = back(own, unit, inverse, gain_ref[...]).astype(BF16)

    @pl.when(block == pl.num_programs(0) - 1)
    def _():
        for n in range(kv_heads):
            key_cols = slice(2 * n * head, (2 * n + 1) * head)
            value_cols = slice((2 * n + 1) * head, (2 * n + 2) * head)
            dkv_ref[:, :, key_cols] = (acc[:, :, key_cols] * scale).astype(BF16)
            dkv_ref[:, :, value_cols] = acc[:, :, value_cols].astype(BF16)


def attend_backward(query, index, kv, marks, grad, out, mass, raw, cosine, sine, gain, head, kv_heads):
    lo, hi, pk_row, unused, unused_too, pq_row, sq_row = marks
    unused, rows, width = query.shape
    group = width // (kv_heads * head)
    blocks = rows // QROWS
    own = lambda i, *s: (i, 0)
    line = lambda i, *s: (i, 0, 0)
    of = lambda cols: pl.BlockSpec((None, QROWS, cols), lambda i, *s: (index, i, 0))
    return pl.pallas_call(
        functools.partial(backward_kernel, head, kv_heads),
        grid_spec=pltpu.PrefetchScalarGridSpec(
            num_scalar_prefetch=2,
            grid=(blocks,),
            in_specs=[
                of(width),
                whole(kv.shape),
                whole(pk_row.shape),
                pl.BlockSpec((1, 1, group * QROWS), line),
                pl.BlockSpec((1, 1, group * QROWS), line),
                pl.BlockSpec((QROWS, width), own),
                pl.BlockSpec((QROWS, width), own),
                pl.BlockSpec((1, kv_heads, group * QROWS), line),
                of(width),
                of(head),
                of(head),
                whole((1, head)),
            ],
            out_specs=[pl.BlockSpec((QROWS, width), own), whole(kv.shape), whole((1, head))],
            scratch_shapes=[VMEM(kv.shape, F32)],
        ),
        out_shape=[
            jax.ShapeDtypeStruct((rows, width), BF16),
            jax.ShapeDtypeStruct(kv.shape, BF16),
            jax.ShapeDtypeStruct((1, head), F32),
        ],
        compiler_params=params(56),
        name="attend_backward",
    )(lo, hi, query, kv, pk_row, pq_row, sq_row, grad, out, mass, raw, cosine, sine, gain)


def key_back_kernel(head, kv_heads, grad_ref, raw_ref, cos_ref, sin_ref, gain_ref, out_ref, dgain_ref):
    cosine, sine = cos_ref[...], sin_ref[...]
    total = jnp.zeros((1, head), F32)
    for n in range(kv_heads):
        at = 2 * n * head
        own = unturn(grad_ref[:, at : at + head].astype(F32), cosine, sine)
        raw = raw_ref[:, n * head : (n + 1) * head]
        inverse = lax.rsqrt(jnp.mean(raw * raw, axis=-1, keepdims=True) + EPSILON)
        unit = raw * inverse
        total = total + jnp.sum(own * unit, axis=0, keepdims=True)
        out_ref[:, at : at + head] = back(own, unit, inverse, gain_ref[...]).astype(BF16)
        out_ref[:, at + head : at + 2 * head] = grad_ref[:, at + head : at + 2 * head]
    dgain_ref[...] = total


def key_back(grad, index, raw, cosine, sine, gain, kv_heads):
    rows = grad.shape[0]
    head = gain.shape[1]
    keys = pl.BlockSpec(
        (None, rows, kv_heads * head), lambda i: (index, 0, raw.shape[2] // (kv_heads * head) - 1)
    )
    turns = pl.BlockSpec((None, rows, head), lambda i: (index, 0, 0))
    return pl.pallas_call(
        functools.partial(key_back_kernel, head, kv_heads),
        grid=(1,),
        out_shape=[jax.ShapeDtypeStruct(grad.shape, BF16), jax.ShapeDtypeStruct((1, head), F32)],
        in_specs=[whole(grad.shape), keys, turns, turns, whole((1, head))],
        out_specs=[whole(grad.shape), whole((1, head))],
        compiler_params=params(32),
        name="key_back",
    )(grad, raw, cosine, sine, gain)


LOAD, SAVE = "load", "save"


class One:
    def __init__(self, array, index):
        self.array, self.index = array, index
        self.shape, self.dtype = array.shape[1:], array.dtype


def source(item):
    return item.array if isinstance(item, One) else item


class Loaded:
    def __init__(self, source, held, sem):
        self.ref = held
        self.copy = lambda: pltpu.make_async_copy(source, held, sem)

    def start(self):
        self.copy().start()

    def wait(self):
        self.copy().wait()


class Saved:
    def __init__(self, held, result, sems, axis):
        self.ref, self.result, self.sems, self.axis = held, result, sems, axis
        self.count = sems.shape[0]

    def part(self, i):
        size = self.ref.shape[self.axis] // self.count
        at = pl.ds(pl.multiple_of(i * size, size), size)
        return (at, slice(None)) if self.axis == 0 else (slice(None), at)

    def copy(self, i):
        at = self.part(i)
        return pltpu.make_async_copy(self.ref.at[at], self.result.at[at], self.sems.at[i])

    def save(self, i):
        self.copy(i).start()

    def finish(self):
        def one(i, carry):
            self.copy(i).wait()
            return carry

        lax.fori_loop(0, self.count, one, 0)


def run_jobs(n_tp, line, jobs, collective, megabytes, name, alias=None):
    rows, width = line[2], line[3]
    dma = pltpu.SemaphoreType.DMA
    line_scratch = [VMEM((rows, width), BF16)] * 5 + [dma((2, CHUNKS)), dma((2, CHUNKS))]
    parts = [(line[0], line[1], line_scratch)] + [job[:3] for job in jobs]
    arrays = [source(array) for part in parts for array, unused in part[0]]
    spec = lambda how: pl.BlockSpec(memory_space=VMEM if how is VMEM else ANY)
    scratch_shapes, plan = [], []
    for ins, outs, scratch in parts:
        at = len(scratch_shapes)
        scratch_shapes += scratch
        plan.append([range(at, len(scratch_shapes)), {}, {}])
        for i, (array, how) in enumerate(ins):
            if how is LOAD:
                plan[-1][1][i] = len(scratch_shapes)
                scratch_shapes += [VMEM(array.shape[-2:], array.dtype), dma]
        for i, (out, how) in enumerate(outs):
            if isinstance(how, tuple):
                plan[-1][2][i] = len(scratch_shapes)
                scratch_shapes += [VMEM(out.shape, out.dtype), dma((how[1],))]
    n_ins = sum(len(part[0]) for part in parts)
    n_outs = sum(len(part[1]) for part in parts)

    def kernel(*refs):
        ins, outs, scratch = refs[:n_ins], refs[n_ins : n_ins + n_outs], refs[n_ins + n_outs :]
        groups, loads, saves = [], [], []
        in_at = out_at = 0
        for (own_ins, own_outs, unused), (own_scratch, loaded, saved) in zip(parts, plan):
            in_refs = list(ins[in_at : in_at + len(own_ins)])
            out_refs = list(outs[out_at : out_at + len(own_outs)])
            in_at += len(own_ins)
            out_at += len(own_outs)
            for i, k in loaded.items():
                which = own_ins[i][0]
                at = in_refs[i].at[which.index] if isinstance(which, One) else in_refs[i]
                in_refs[i] = Loaded(at, scratch[k], scratch[k + 1])
                loads.append(in_refs[i])
            for i, k in saved.items():
                out_refs[i] = Saved(scratch[k], out_refs[i], scratch[k + 1], own_outs[i][1][2])
                saves.append(out_refs[i])
            groups.append((in_refs, out_refs, [scratch[k] for k in own_scratch]))
        for item in loads:
            item.start()
        bound = [job[3](*groups[i + 1]) for i, job in enumerate(jobs)]
        line_sum(n_tp, groups[0][2], line[4](*groups[0][:2]), bound)
        for item in saves:
            item.finish()

    return pl.pallas_call(
        kernel,
        out_shape=[out[0] for part in parts for out in part[1]],
        in_specs=[spec(how) for part in parts for unused, how in part[0]],
        out_specs=[spec(how) for part in parts for unused, how in part[1]],
        scratch_shapes=scratch_shapes,
        input_output_aliases=alias or {},
        compiler_params=params(megabytes, collective),
        name=name,
    )(*arrays)


def piece(c, rows):
    return pl.ds(pl.multiple_of(c * rows, rows), rows)


def line_sum(n_tp, scratch, main, jobs):
    part, from_left, from_right, to_right, to_left, send_sem, recv_sem = scratch
    produce_ready, consume_ready, produce, consume = main
    chunks = CHUNKS
    size = part.shape[0] // chunks
    groups = part.shape[0] // GROUP
    place = lax.axis_index("tp")
    line = lax.axis_index("ctx")
    has_left, has_right = place > 0, place < n_tp - 1
    barrier = pltpu.get_barrier_semaphore()
    peers = [peer for job in jobs for peer in job[0]]
    for peer in peers:
        pl.semaphore_signal(barrier, inc=1, device_id=peer, device_id_type=MESH)

    @pl.when(has_left)
    def _():
        pl.semaphore_signal(barrier, inc=1, device_id=(line, place - 1), device_id_type=MESH)

    @pl.when(has_right)
    def _():
        pl.semaphore_signal(barrier, inc=1, device_id=(line, place + 1), device_id_type=MESH)

    def fill(g):
        part[piece(g, GROUP), :] = produce(g).astype(BF16)

    for item in produce_ready:
        item.wait()
    fill(0)
    pl.semaphore_wait(
        barrier, has_left.astype(jnp.int32) + has_right.astype(jnp.int32) + len(peers)
    )
    for job in jobs:
        job[1]()

    def right(c):
        return pltpu.make_async_remote_copy(
            src_ref=to_right.at[piece(c, size)],
            dst_ref=from_left.at[piece(c, size)],
            send_sem=send_sem.at[0, c],
            recv_sem=recv_sem.at[0, c],
            device_id=(line, place + 1),
            device_id_type=MESH,
        )

    def left(c):
        return pltpu.make_async_remote_copy(
            src_ref=to_left.at[piece(c, size)],
            dst_ref=from_right.at[piece(c, size)],
            send_sem=send_sem.at[1, c],
            recv_sem=recv_sem.at[1, c],
            device_id=(line, place - 1),
            device_id_type=MESH,
        )

    def plus(a, b):
        return (a.astype(F32) + b.astype(F32)).astype(BF16)

    late = LAG * jnp.maximum(place, n_tp - 1 - place)

    def step(s, carry):
        c_right = s - LAG * place
        c_left = s - LAG * (n_tp - 1 - place)
        c_out = s - late

        @pl.when((c_right >= 0) & (c_right < chunks))
        def _():
            at = piece(c_right, size)

            @pl.when(jnp.logical_not(has_left))
            def _():
                to_right[at, :] = part[at, :]

            @pl.when(has_left)
            def _():
                right(c_right).wait_recv()
                to_right[at, :] = plus(part[at, :], from_left[at, :])

            @pl.when(has_right)
            def _():
                right(c_right).start()

        @pl.when((c_left >= 0) & (c_left < chunks))
        def _():
            at = piece(c_left, size)

            @pl.when(jnp.logical_not(has_right))
            def _():
                to_left[at, :] = part[at, :]

            @pl.when(has_right)
            def _():
                left(c_left).wait_recv()
                to_left[at, :] = plus(part[at, :], from_right[at, :])

            @pl.when(has_left)
            def _():
                left(c_left).start()

        @pl.when((s + 1 < groups))
        def _():
            fill(s + 1)

        @pl.when(s == 1)
        def _():
            for item in consume_ready:
                item.wait()

        @pl.when((c_out >= 0) & (c_out < chunks))
        def _():
            at = piece(c_out, size)

            @pl.when(has_right)
            def _():
                consume(c_out, to_right[at, :].astype(F32) + from_right[at, :].astype(F32))

            @pl.when(jnp.logical_not(has_right))
            def _():
                consume(c_out, to_right[at, :].astype(F32))

        for job in jobs:
            job[2](s)
        return carry

    lax.fori_loop(0, chunks + LAG * (n_tp - 1), step, 0)

    for job in jobs:
        job[3]()

    def finish(c, carry):
        @pl.when(has_right)
        def _():
            right(c).wait_send()

        @pl.when(has_left)
        def _():
            left(c).wait_send()

        return carry

    lax.fori_loop(0, chunks, finish, 0)


def mean_square(values):
    return jnp.mean(values * values, axis=-1, keepdims=True)


def shape(rows, width, dtype=BF16):
    return jax.ShapeDtypeStruct((rows, width), dtype)


def attn_out_line(mixed, place, weight, inputs, gain):
    rows, width = inputs.shape
    size = rows // CHUNKS
    groups = rows // GROUP

    def bind(ins, outs):
        mixed_in, place_in, w_in, x_in, gain_ref = ins
        own_out, middle_out, normed_out = outs

        def produce(g):
            own = nn(place_in.ref[piece(g, GROUP), :], mixed_in.ref[...].astype(BF16)).astype(BF16)
            own_out.ref[piece(g, GROUP), :] = own
            own_out.save(g)
            return nt(own, w_in.ref[...])

        def consume(c, total):
            at = piece(c, size)
            middle = x_in.ref[at, :].astype(F32) + total
            middle_out.ref[at, :] = middle.astype(BF16)
            middle_out.save(c)
            unit = middle * lax.rsqrt(mean_square(middle) + EPSILON)
            normed_out.ref[at, :] = (unit * gain_ref[...]).astype(BF16)
            normed_out.save(c)

        return [mixed_in, place_in, w_in], [x_in], produce, consume

    return (
        [(mixed, LOAD), (place, LOAD), (weight, LOAD), (inputs, LOAD), (gain, VMEM)],
        [
            (shape(*mixed.shape), (SAVE, groups, 0)),
            (shape(rows, width), (SAVE, CHUNKS, 0)),
            (shape(rows, width), (SAVE, CHUNKS, 0)),
        ],
        rows,
        width,
        bind,
    )


def middle_back_line(part, grad, middle, gain, weight):
    rows, width = grad.shape
    size = rows // CHUNKS
    groups = rows // GROUP
    each = GROUP // size

    def bind(ins, outs):
        part_in, g_in, middle_in, gain_ref, w_in = ins
        low_out, mixed_out, dgain_ref = outs
        dgain_ref[...] = jnp.zeros_like(dgain_ref)

        def produce(g):
            return part_in.ref[piece(g, GROUP), :]

        def consume(c, total):
            at = piece(c, size)
            middle = middle_in.ref[at, :].astype(F32)
            inverse = lax.rsqrt(mean_square(middle) + EPSILON)
            unit = middle * inverse
            dgain_ref[...] += jnp.sum(total * unit, axis=0, keepdims=True)
            grad = g_in.ref[at, :].astype(F32) + back(total, unit, inverse, gain_ref[...])
            low_out.ref[at, :] = grad.astype(BF16)
            low_out.save(c)

            @pl.when(lax.rem(c, each) == each - 1)
            def _():
                g = c // each
                at = piece(g, GROUP)
                mixed_out.ref[at, :] = nn(low_out.ref[at, :], w_in.ref[...]).astype(BF16)
                mixed_out.save(g)

        return [part_in], [g_in, middle_in, w_in], produce, consume

    return (
        [(part, LOAD), (grad, LOAD), (middle, LOAD), (gain, VMEM), (weight, LOAD)],
        [
            (shape(rows, width), (SAVE, CHUNKS, 0)),
            (shape(rows, weight.shape[1]), (SAVE, groups, 0)),
            (shape(1, width, F32), VMEM),
        ],
        rows,
        width,
        bind,
    )


def input_back_line(gq, gkv, place, weight, inputs, mid, gain):
    rows, width = inputs.shape
    size = rows // CHUNKS

    def bind(ins, outs):
        gq_in, gkv_in, place_in, w_in, x_in, mid_in, gain_ref = ins
        out, dgain_ref = outs
        queries = gq.shape[1]
        dgain_ref[...] = jnp.zeros_like(dgain_ref)

        def produce(g):
            slots = place_in.ref[piece(g, GROUP), :]
            own_q = nn(slots, gq_in.ref[...]).astype(BF16)
            own_kv = nn(slots, gkv_in.ref[...]).astype(BF16)
            return nt(own_q, w_in.ref[:, :queries]) + nt(own_kv, w_in.ref[:, queries:])

        def consume(c, total):
            at = piece(c, size)
            x = x_in.ref[at, :].astype(F32)
            inverse = lax.rsqrt(mean_square(x) + EPSILON)
            unit = x * inverse
            dgain_ref[...] += jnp.sum(total * unit, axis=0, keepdims=True)
            grad = mid_in.ref[at, :].astype(F32) + back(total, unit, inverse, gain_ref[...])
            out.ref[at, :] = grad.astype(BF16)
            out.save(c)

        return [gq_in, gkv_in, place_in, w_in], [x_in, mid_in], produce, consume

    return (
        [(item, LOAD) for item in (gq, gkv, place, weight, inputs, mid)] + [(gain, VMEM)],
        [(shape(rows, width), (SAVE, CHUNKS, 0)), (shape(1, width, F32), VMEM)],
        rows,
        width,
        bind,
    )


def gather_job(own, n_ctx):
    chips = n_ctx // 2
    dma = pltpu.SemaphoreType.DMA

    def bind(ins, outs, scratch):
        peers, start, relay, finish = gather_parts([ins[0].at[own.index]], outs, scratch, n_ctx)

        def hook(s):
            for d in range(1, chips):

                @pl.when(s == CHUNKS - 2 * chips + 2 * d)
                def _(d=d):
                    relay(0, d)

        return peers, start, hook, finish

    return (
        [(own, ANY)],
        [(shape(n_ctx * own.shape[0], own.shape[1]), ANY)],
        [dma((1,))] + [dma((1, chips))] * 4,
        bind,
    )


def mlp_job(middle, normed, grad, weight, n_tp):
    rows, width = normed.shape
    units = weight.shape[1] // 3
    tile = 256
    tiles, down_tiles = units // tile, width // tile
    share = 1.0 / n_tp
    every = max(1, CHUNKS // 16)
    dma = pltpu.SemaphoreType.DMA

    def bind(ins, outs, scratch):
        middle_in, x_in, g_in, w_hbm = ins
        hid, gg, gu, down_out, gn_out = outs
        w_ref, sem = scratch

        def load(t, part):
            at = pl.ds(pl.multiple_of(part * units + t * tile, tile), tile)
            return pltpu.make_async_copy(w_hbm.at[:, at], w_ref.at[:, at], sem.at[part, t])

        def start():
            for t in range(tiles):
                for part in range(3):
                    load(t, part).start()

        def first(t):
            for part in range(3):
                load(t, part).wait()
            cols = [
                pl.ds(pl.multiple_of(part * units + t * tile, tile), tile) for part in range(3)
            ]
            gate = nn(x_in.ref[...], w_ref[:, cols[0]])
            up = nn(x_in.ref[...], w_ref[:, cols[1]])
            grad = nn(g_in.ref[...], w_ref[:, cols[2]])
            sigmoid = jax.nn.sigmoid(gate)
            silu = gate * sigmoid
            hid.ref[:, cols[0]] = (silu * up).astype(BF16)
            gu.ref[:, cols[0]] = (grad * silu).astype(BF16)
            gg.ref[:, cols[0]] = (grad * up * sigmoid * (1.0 + gate * (1.0 - sigmoid))).astype(BF16)
            for out in (hid, gu, gg):
                out.save(t)

        def second(t):
            at = pl.ds(pl.multiple_of(t * tile, tile), tile)
            down = nt(hid.ref[...], w_ref[at, 2 * units :])
            down_out.ref[:, at] = (down + middle_in.ref[:, at].astype(F32) * share).astype(BF16)
            gn_out.ref[:, at] = (
                nt(gg.ref[...], w_ref[at, :units]) + nt(gu.ref[...], w_ref[at, units : 2 * units])
            ).astype(BF16)
            down_out.save(t)
            gn_out.save(t)

        def hook(s):
            h = (s - 1) // every
            now = lax.rem(s - 1, every) == 0

            @pl.when(s == 1)
            def _():
                for item in (middle_in, x_in, g_in):
                    item.wait()

            @pl.when(now & (s >= 1) & (h < tiles))
            def _():
                first(h)

            @pl.when(now & (h >= tiles) & (h < tiles + down_tiles))
            def _():
                second(h - tiles)

        return [], start, hook, lambda: None

    return (
        [(middle, LOAD), (normed, LOAD), (grad, LOAD), (weight, ANY)],
        [(shape(rows, units), (SAVE, tiles, 1))] * 3
        + [(shape(rows, width), (SAVE, down_tiles, 1))] * 2,
        [VMEM(weight.shape, BF16), dma((3, tiles))],
        bind,
    )


def weight_job(lefts, groups, tile, every, room):
    rows, width = lefts[0].shape
    rights = [side for unused, sides in groups for side in sides]
    counts = [sides[0].shape[1] // tile for unused, sides in groups]
    total = sum(counts)
    dma = pltpu.SemaphoreType.DMA
    sources = list(lefts) + rights

    def bind(ins, outs, scratch):
        (out_hbm,) = outs
        held = [item.ref for item in ins[: len(sources)]]
        out_buf, out_sem = scratch

        def save(h):
            slot = lax.rem(h, 2)
            return pltpu.make_async_copy(
                out_buf.at[slot],
                out_hbm.at[:, pl.ds(pl.multiple_of(h * tile, tile), tile)],
                out_sem.at[slot],
            )

        def hook(s):
            @pl.when(s == 1)
            def _():
                for item in ins[: len(sources)]:
                    item.wait()

            h = (s - 1) // every
            now = (s >= 1) & (lax.rem(s - 1, every) == 0) & (h < total)

            @pl.when(now & (h >= 2))
            def _():
                save(h - 2).wait()

            first, at = 0, len(lefts)
            for (indices, sides), count in zip(groups, counts):
                left_refs = [held[i] for i in indices]
                right_refs = held[at : at + len(sides)]
                at += len(sides)

                @pl.when(now & (h >= first) & (h < first + count))
                def _(left_refs=left_refs, right_refs=right_refs, first=first):
                    cols = pl.ds(pl.multiple_of((h - first) * tile, tile), tile)
                    grads = tn(left_refs[0][...], right_refs[0][:, cols])
                    for left_ref, right_ref in zip(left_refs[1:], right_refs[1:]):
                        grads = grads + tn(left_ref[...], right_ref[:, cols])
                    out_buf[lax.rem(h, 2)] = grads.astype(BF16)

                first += count

            @pl.when(now)
            def _():
                save(h).start()

        def finish():
            save(total - 2).wait()
            save(total - 1).wait()

        return [], lambda: None, hook, finish

    return (
        [(item, LOAD) for item in sources] + [(room, ANY)],
        [(shape(width, total * tile), ANY)],
        [VMEM((2, width, tile), BF16), dma((2,))],
        bind,
    )


def scatter_job(whole_rows, n_ctx, dtype, first, second):
    total, width = whole_rows.shape
    rows = total // n_ctx
    chips = n_ctx // 2
    dma = pltpu.SemaphoreType.DMA

    def bind(ins, outs, scratch):
        (source,), (out_ref,) = ins, outs
        mine, near, far, load_sem, near_send, near_recv, far_send, far_recv = scratch
        me, column = lax.axis_index("ctx"), lax.axis_index("tp")
        chip, core = me // 2, lax.rem(me, 2)

        def block(d, which):
            at = (jnp.bitwise_xor(chip, d) * 2 + which) * rows
            return source.at[pl.ds(pl.multiple_of(at, rows), rows)]

        def load(d):
            return pltpu.make_async_copy(block(d, core), mine.at[d], load_sem.at[d])

        def beside(d):
            return pltpu.make_async_remote_copy(
                src_ref=block(d, 1 - core),
                dst_ref=near.at[d],
                send_sem=near_send.at[d],
                recv_sem=near_recv.at[d],
                device_id=(chip * 2 + 1 - core, column),
                device_id_type=MESH,
            )

        def across(d):
            return pltpu.make_async_remote_copy(
                src_ref=mine.at[d],
                dst_ref=far.at[d - 1],
                send_sem=far_send.at[d],
                recv_sem=far_recv.at[d],
                device_id=(jnp.bitwise_xor(chip, d) * 2 + core, column),
                device_id_type=MESH,
            )

        peers = [(chip * 2 + 1 - core, column)] + [
            (jnp.bitwise_xor(chip, d) * 2 + core, column) for d in range(1, chips)
        ]
        order = list(range(chips - 1, -1, -1))

        def start():
            for d in order:
                load(d).start()
                beside(d).start()

        def near_sum():
            for d in order:
                load(d).wait()
                beside(d).wait_recv()
                mine[d] = (mine[d].astype(F32) + near[d].astype(F32)).astype(BF16)
                if d > 0:
                    across(d).start()

        def far_sum():
            for d in range(1, chips):
                across(d).wait_recv()
            result = mine[0].astype(F32)
            for d in range(1, chips):
                result = result + far[d - 1].astype(F32)
            out_ref[...] = result.astype(dtype)

        def hook(s):
            @pl.when(s == first)
            def _():
                near_sum()

            @pl.when(s == second)
            def _():
                far_sum()

        def finish():
            for d in range(chips):
                beside(d).wait_send()
                if d > 0:
                    across(d).wait_send()

        return peers, start, hook, finish

    return (
        [(whole_rows, ANY)],
        [(shape(rows, width, dtype), VMEM)],
        [
            VMEM((chips, rows, width), BF16),
            VMEM((chips, rows, width), BF16),
            VMEM((chips - 1, rows, width), BF16),
        ]
        + [dma((chips,))] * 5,
        bind,
    )


def weight_kernel(starts, parts, *refs):
    out_ref = refs[-1]
    step = pl.program_id(0)
    at = 0
    for index, (lefts, first, last) in enumerate(starts):
        left_refs = [refs[i] for i in lefts]
        right_refs = refs[parts + at : parts + at + len(lefts)]
        at += len(lefts)

        @pl.when((step >= first) & (step < last))
        def _(left_refs=left_refs, right_refs=right_refs):
            total = tn(left_refs[0][...], right_refs[0][...])
            for left_ref, right_ref in zip(left_refs[1:], right_refs[1:]):
                total = total + tn(left_ref[...], right_ref[...])
            out_ref[...] = total.astype(BF16)


def weight_grads(lefts, groups, tile):
    rows, width = lefts[0].shape
    starts, specs, rights, at = [], [], [], 0
    for indices, sides in groups:
        tiles = sides[0].shape[1] // tile
        starts.append((indices, at, at + tiles))
        for side in sides:
            rights.append(side)
            specs.append(
                pl.BlockSpec(
                    (rows, tile), lambda j, at=at, tiles=tiles: (0, jnp.clip(j - at, 0, tiles - 1))
                )
            )
        at += tiles
    return pl.pallas_call(
        functools.partial(weight_kernel, starts, len(lefts)),
        grid=(at,),
        out_shape=jax.ShapeDtypeStruct((width, at * tile), BF16),
        in_specs=[
            pl.BlockSpec((None, rows, width), lambda j, at=left.index: (at, 0, 0))
            if isinstance(left, One)
            else whole((rows, width))
            for left in lefts
        ]
        + specs,
        out_specs=pl.BlockSpec((width, tile), lambda j: (0, j)),
        compiler_params=params(60),
        name="weight_grads",
    )(*[source(left) for left in lefts], *rights)


def gains_kernel(n_ctx, n_tp, x_ref, out_ref, got, send_sem, recv_sem, line_got, line_send, line_recv):
    me, place = lax.axis_index("ctx"), lax.axis_index("tp")
    barrier = pltpu.get_barrier_semaphore()
    others = [lax.rem(me + d, n_ctx) for d in range(1, n_ctx)]
    members = [lax.rem(place + d, n_tp) for d in range(1, n_tp)]
    for other in others:
        pl.semaphore_signal(barrier, inc=1, device_id=(other, place), device_id_type=MESH)
    for member in members:
        pl.semaphore_signal(barrier, inc=1, device_id=(me, member), device_id_type=MESH)
    pl.semaphore_wait(barrier, n_ctx + n_tp - 2)
    copies = [
        pltpu.make_async_remote_copy(
            src_ref=x_ref.at[other],
            dst_ref=got.at[d],
            send_sem=send_sem.at[d],
            recv_sem=recv_sem.at[d],
            device_id=(other, place),
            device_id_type=MESH,
        )
        for d, other in enumerate(others)
    ]
    for copy in copies:
        copy.start()
    total = x_ref[me]
    for d, copy in enumerate(copies):
        copy.wait()
        total = total + got[d]
    out_ref[...] = total
    copies = [
        pltpu.make_async_remote_copy(
            src_ref=out_ref,
            dst_ref=line_got.at[d],
            send_sem=line_send.at[d],
            recv_sem=line_recv.at[d],
            device_id=(me, member),
            device_id_type=MESH,
        )
        for d, member in enumerate(members)
    ]
    for copy in copies:
        copy.start()
    low = total[4:]
    for d, copy in enumerate(copies):
        copy.wait()
        low = low + line_got[d, 4:, :]
    out_ref[4:, :] = low


def sum_gains(blocks, n_ctx, n_tp, collective):
    dma = pltpu.SemaphoreType.DMA
    return pl.pallas_call(
        functools.partial(gains_kernel, n_ctx, n_tp),
        out_shape=jax.ShapeDtypeStruct((8, 128), F32),
        in_specs=[pl.BlockSpec(memory_space=VMEM)],
        out_specs=pl.BlockSpec(memory_space=VMEM),
        scratch_shapes=[
            VMEM((n_ctx - 1, 8, 128), F32),
            dma((n_ctx - 1,)),
            dma((n_ctx - 1,)),
            VMEM((n_tp - 1, 8, 128), F32),
            dma((n_tp - 1,)),
            dma((n_tp - 1,)),
        ],
        compiler_params=params(16, collective),
        name="sum_gains",
    )(blocks)


def attention_marks(in_order, newest, oldest, n_ctx, group):
    rows = newest.shape[0]
    blocks = rows // SUB
    grouped = in_order.reshape(n_ctx, blocks, SUB)
    smallest = jnp.min(grouped[:, :, 0], axis=0)
    largest = jnp.max(grouped[:, :, SUB - 1], axis=0)
    first = oldest.reshape(-1, QROWS)[:, 0]
    last = newest.reshape(-1, QROWS)[:, QROWS - 1]
    lo = jnp.sum((largest[None, :] < first[:, None]).astype(jnp.int32), axis=1)
    hi = jnp.sum((smallest[None, :] <= last[:, None]).astype(jnp.int32), axis=1)
    keys = grouped.transpose(1, 0, 2).reshape(blocks, 1, n_ctx * SUB)
    of_group = lambda column: jnp.tile(column.reshape(-1, 1, QROWS), (1, 1, group))
    return lo, hi, keys, newest, oldest, of_group(newest), of_group(oldest)


def on_device(
    n_ctx,
    n_tp,
    hidden_in,
    seq_lengths,
    token_order,
    attn_gain,
    w_query,
    w_key,
    w_value,
    query_gain,
    key_gain,
    w_out,
    mlp_gain,
    w_gate,
    w_up,
    w_down,
    cotangent,
):
    micro_count, rows, width = hidden_in.shape
    head = query_gain.shape[0]
    heads, kv_heads = w_query.shape[1] // head, w_key.shape[1] // head
    rank = lax.axis_index("ctx")
    queries = heads * head
    units = w_gate.shape[1]
    q_gain, k_gain = query_gain[None, :], key_gain[None, :]
    a_gain, m_gain = attn_gain[None, :], mlp_gain[None, :]

    frequency = jnp.exp(jnp.arange(head // 2, dtype=F32) * (-2.0 * math.log(THETA) / head))
    one = jnp.ones((head // 2,), F32)
    frequency = jnp.stack([jnp.tile(frequency, 2), jnp.concatenate([-one, one])])
    (
        qkv_w,
        out_w,
        mlp_own,
        sorted_normed,
        to_slot,
        to_sorted,
        cosine,
        sine,
        in_order,
        newest,
        oldest,
    ) = begin(
        hidden_in,
        token_order.reshape(micro_count * n_ctx, rows),
        seq_lengths,
        a_gain,
        frequency,
        (w_query, w_key, w_value, w_out, w_gate, w_up, w_down),
        n_ctx,
        head,
        kv_heads,
        0,
    )
    both = range(micro_count)
    last = micro_count - 1
    orders = [
        (
            to_slot[b],
            to_sorted[b],
            attention_marks(
                in_order[b * n_ctx : (b + 1) * n_ctx], newest[b], oldest[b], n_ctx, heads // kv_heads
            ),
        )
        for b in both
    ]
    query, kv_own, raw = project_qkv(
        sorted_normed, qkv_w, cosine, sine, q_gain, k_gain, heads, kv_heads
    )
    kv_first = gather_ctx(kv_own, 0, n_ctx, 1)
    kv_all = [kv_first.reshape(n_ctx, rows, -1)]
    mlp_w = lax.all_gather(after(mlp_own, kv_first), "ctx", axis=0, tiled=True)

    def forward(b):
        return attend_forward(query, b, kv_all[b], orders[b][2], head, kv_heads)

    def out_line(b):
        return attn_out_line(attended[b][0], One(to_slot, b), out_w, One(hidden_in, b), m_gain)

    def middle_line(b):
        return middle_back_line(fed[b][4], One(cotangent, b), middles[b][1], m_gain, out_w)

    def feed(b):
        return mlp_job(middles[b][1], middles[b][2], One(cotangent, b), mlp_w, n_tp)

    attended, middles, fed, mids, backs = [], [], [], [], []
    attended.append(forward(0))
    results = run_jobs(n_tp, out_line(0), [gather_job(One(kv_own, 1), n_ctx)], 2, 40, "attn_out_gather")
    middles.append(results[:3])
    kv_all.append(results[3].reshape(n_ctx, rows, -1))
    attended.append(forward(1))
    results = run_jobs(n_tp, out_line(1), [feed(0)], 3, 60, "attn_out_mlp")
    middles.append(results[:3])
    fed.append(results[3:])
    results = run_jobs(n_tp, middle_line(0), [feed(1)], 4, 60, "middle_back_mlp")
    mids.append(results[:3])
    fed.append(results[3:])

    layer_out = jnp.stack(lax.psum([fed[b][3] for b in both], "tp"))

    def backward(b, grad):
        unused, sorting, marks = orders[b]
        g_mixed = nn(sorting, grad).astype(BF16)
        mixed_full, mass = attended[b]
        return attend_backward(
            query, b, kv_all[b], marks, g_mixed, mixed_full, mass, raw, cosine, sine, q_gain, head, kv_heads
        )

    backs.append(backward(0, mids[0][1]))
    tile = 512 if units % 512 == 0 else 256
    line = middle_line(1)
    line[0][0] = (after(line[0][0][0], backs[0][0]), LOAD)
    results = run_jobs(
        n_tp,
        line,
        [
            weight_job(
                [middles[b][2] for b in both] + [One(cotangent, b) for b in both],
                [
                    (tuple(both), [fed[b][1] for b in both]),
                    (tuple(both), [fed[b][2] for b in both]),
                    (tuple(micro_count + b for b in both), [fed[b][0] for b in both]),
                ],
                tile,
                2 * max(1, CHUNKS // 16),
                mlp_w,
            ),
            scatter_job(backs[0][1].reshape(n_ctx * rows, -1), n_ctx, BF16, CHUNKS // 4, CHUNKS),
        ],
        5,
        60,
        "middle_back_weights",
        {5 + 5 * micro_count: 3},
    )
    mids.append(results[:3])
    mlp_grads = lax.psum_scatter(results[3], "ctx", scatter_dimension=0, tiled=True)
    dkv_first = results[4]
    backs.append(backward(1, mids[1][1]))

    def key_part(b, dkv):
        return key_back(dkv, b, raw, cosine, sine, k_gain, kv_heads)

    def in_line(b, gkv):
        return input_back_line(
            backs[b][0], gkv, One(to_slot, b), qkv_w, One(hidden_in, b), mids[b][0], a_gain
        )

    gkv_first, dk_gain_first = key_part(0, after(dkv_first, backs[1][0]))
    results = run_jobs(
        n_tp,
        in_line(0, gkv_first),
        [scatter_job(backs[1][1].reshape(n_ctx * rows, -1), n_ctx, BF16, CHUNKS // 4, CHUNKS)],
        6,
        60,
        "input_back_keys",
    )
    grad_in_first, da_gain_first, dkv_last = results
    gkv_last, dk_gain_last = key_part(1, dkv_last)
    tile = min(512, 2 * kv_heads * head, queries)
    gkvs = [gkv_first, gkv_last]
    attn_grads = weight_grads(
        [One(sorted_normed, b) for b in both] + [mids[b][0] for b in both],
        [
            (tuple(both), [backs[b][0] for b in both]),
            (tuple(both), [gkvs[b] for b in both]),
            (tuple(micro_count + b for b in both), [middles[b][0] for b in both]),
        ],
        tile,
    )
    results = run_jobs(
        n_tp,
        in_line(1, gkv_last),
        [scatter_job(attn_grads, n_ctx, F32, CHUNKS // 4, CHUNKS + 2)],
        7,
        60,
        "input_back_weights",
    )
    grad_in_last, da_gain_last, attn_grads = results
    grads_in = [grad_in_first, grad_in_last]
    d_attn_gain = [da_gain_first, da_gain_last]
    d_key_gain = [dk_gain_first, dk_gain_last]

    share = width // n_ctx // 128
    own = lambda gain: sum(gain).reshape(n_ctx, share, 128)
    spread = lambda gain: jnp.broadcast_to(sum(gain)[None], (n_ctx, 1, 128))
    blank = jnp.zeros((n_ctx, 4 - 2 * share, 128), F32)
    low_blank = jnp.zeros((n_ctx, 2, 128), F32)
    gains = sum_gains(
        jnp.concatenate(
            [
                own(d_attn_gain),
                own([mids[b][2] for b in both]),
                blank,
                spread([backs[b][2] for b in both]),
                spread(d_key_gain),
                low_blank,
            ],
            axis=1,
        ),
        n_ctx,
        n_tp,
        8,
    )

    mlp_grads = mlp_grads.astype(F32)
    at = queries
    keys, values = [], []
    for n in range(kv_heads):
        keys.append(attn_grads[:, at : at + head])
        values.append(attn_grads[:, at + head : at + 2 * head])
        at += 2 * head
    return (
        layer_out,
        jnp.stack(grads_in).astype(F32),
        gains[:share].reshape(-1),
        attn_grads[:, :queries],
        jnp.concatenate(keys, axis=1),
        jnp.concatenate(values, axis=1),
        gains[4],
        gains[5],
        attn_grads[:, at:].T,
        gains[share : 2 * share].reshape(-1),
        mlp_grads[:, :units],
        mlp_grads[:, units : 2 * units],
        mlp_grads[:, 2 * units :].T,
    )


def solution(mesh):
    rows = P("ctx", "tp")
    columns = P("tp", "ctx")
    tokens = P(None, "ctx", None)
    in_specs = (
        tokens,
        P(),
        P(),
        P(),
        rows,
        rows,
        rows,
        P(),
        P(),
        columns,
        P(),
        rows,
        rows,
        columns,
        tokens,
    )
    out_specs = (
        tokens,
        tokens,
        P("ctx"),
        rows,
        rows,
        rows,
        P(),
        P(),
        columns,
        P("ctx"),
        rows,
        rows,
        columns,
    )
    return jax.shard_map(
        functools.partial(on_device, mesh.shape["ctx"], mesh.shape["tp"]),
        mesh=mesh,
        in_specs=in_specs,
        out_specs=out_specs,
        check_vma=False,
    )
```

```python
import functools
import math

import jax
import jax.numpy as jnp
from jax import lax
from jax.experimental import pallas as pl
from jax.experimental.pallas import tpu as pltpu
from jax.sharding import PartitionSpec as P

EPSILON = 1e-06
THETA = 1000000.0
F32 = jnp.float32
BF16 = jnp.bfloat16
MESH = pl.DeviceIdType.MESH
VMEM = pltpu.VMEM
ANY = pl.ANY
LOG2E = math.log2(math.e)
SUB = 64
QROWS = 256
CHUNKS = 16
LAG = 2
GROUP = 128


def params(megabytes, collective=None):
    if collective is None:
        return pltpu.CompilerParams(vmem_limit_bytes=megabytes << 20)
    return pltpu.CompilerParams(
        vmem_limit_bytes=megabytes << 20, collective_id=collective, has_side_effects=True
    )


def nt(left_side, right_side):
    return lax.dot_general(
        left_side, right_side, (((1,), (1,)), ((), ())), preferred_element_type=F32
    )


def tn(left_side, right_side):
    return lax.dot_general(
        left_side, right_side, (((0,), (0,)), ((), ())), preferred_element_type=F32
    )


def nn(left_side, right_side):
    return jnp.dot(left_side, right_side, preferred_element_type=F32)


def whole(shape):
    return pl.BlockSpec(shape, lambda *ids: (0,) * len(shape))


def after(value, *others):
    return lax.optimization_barrier((value, others))[0]


def gather_parts(sources, results, sems, n_ctx):
    own_sem, send_sem, recv_sem, pass_sem, take_sem = sems
    count = len(sources)
    me = lax.axis_index("ctx")
    column = lax.axis_index("tp")
    chip, core = me // 2, lax.rem(me, 2)
    chips = n_ctx // 2
    partner = chip * 2 + 1 - core

    def peer(d):
        return jnp.bitwise_xor(chip, d) * 2 + core

    def rows_of(array, owner):
        rows = sources[array].shape[0]
        return results[array].at[pl.ds(pl.multiple_of(owner * rows, rows), rows)]

    def across(array, d):
        return pltpu.make_async_remote_copy(
            src_ref=sources[array],
            dst_ref=rows_of(array, me),
            send_sem=send_sem.at[array, d],
            recv_sem=recv_sem.at[array, d],
            device_id=(peer(d), column),
            device_id_type=MESH,
        )

    def passed(array, d):
        owner = peer(d)
        return pltpu.make_async_remote_copy(
            src_ref=sources[array] if d == 0 else rows_of(array, owner),
            dst_ref=rows_of(array, owner),
            send_sem=pass_sem.at[array, d],
            recv_sem=take_sem.at[array, d],
            device_id=(partner, column),
            device_id_type=MESH,
        )

    def local(array):
        return pltpu.make_async_copy(sources[array], rows_of(array, me), own_sem.at[array])

    def onward(array, d):
        rows = sources[array].shape[0]
        half = rows // 2
        slot = 3 if d == 1 else 0

        def of(owner):
            at = pl.multiple_of(owner * rows + (0 if d == 1 else half), half)
            return results[array].at[pl.ds(at, half)]

        return pltpu.make_async_remote_copy(
            src_ref=of(peer(d)),
            dst_ref=of(peer(d)),
            send_sem=send_sem.at[array, slot],
            recv_sem=recv_sem.at[array, slot],
            device_id=(peer(3 - d), column),
            device_id_type=MESH,
        )

    direct = range(1, chips) if chips != 4 else (1, 2)

    def start():
        for d in direct:
            for array in range(count):
                across(array, d).start()
        for array in range(count):
            passed(array, 0).start()
            local(array).start()

    def relay(array, d):
        if d in direct:
            across(array, d).wait_recv()
            if chips == 4:
                onward(array, d).start()
        else:
            onward(array, 1).wait_recv()
            onward(array, 2).wait_recv()
        passed(array, d).start()

    def finish():
        for array in range(count):
            local(array).wait()
            for d in range(chips):
                if d in direct:
                    across(array, d).wait_send()
                elif d > 0:
                    onward(array, 1).wait_send()
                    onward(array, 2).wait_send()
                passed(array, d).wait_send()
                passed(array, d).wait_recv()

    peers = [(partner, column)] + [(peer(d), column) for d in direct]
    return peers, start, relay, finish


def gather_kernel(index, n_ctx, source_ref, result_ref, *sems):
    peers, start, relay, finish = gather_parts([source_ref.at[index]], [result_ref], sems, n_ctx)
    barrier = pltpu.get_barrier_semaphore()
    for peer in peers:
        pl.semaphore_signal(barrier, inc=1, device_id=peer, device_id_type=MESH)
    pl.semaphore_wait(barrier, len(peers))
    start()
    for d in range(1, n_ctx // 2):
        relay(0, d)
    finish()


def gather_ctx(array, index, n_ctx, collective):
    dma = pltpu.SemaphoreType.DMA
    unused, rows, width = array.shape
    return pl.pallas_call(
        functools.partial(gather_kernel, index, n_ctx),
        out_shape=jax.ShapeDtypeStruct((n_ctx * rows, width), array.dtype),
        in_specs=[pl.BlockSpec(memory_space=ANY)],
        out_specs=pl.BlockSpec(memory_space=ANY),
        scratch_shapes=[dma((1,))] + [dma((1, n_ctx // 2))] * 4,
        compiler_params=params(60, collective),
        name="gather_ctx",
    )(array)


def begin_kernel(
    n_ctx,
    head,
    kv_heads,
    x_hbm,
    order_ref,
    lengths_ref,
    gain_ref,
    frequency_ref,
    wq_ref,
    wk_ref,
    wv_ref,
    wo_ref,
    wg_hbm,
    wu_hbm,
    wd_ref,
    qkv_hbm,
    out_hbm,
    mlp_hbm,
    sorted_ref,
    to_slot_ref,
    to_sorted_ref,
    cos_ref,
    sin_ref,
    keys_ref,
    newest_ref,
    oldest_ref,
    x_ref,
    normed_ref,
    qkv_own,
    wo_turned,
    mlp_own,
    load_sem,
    mlp_sem,
    *gather_sems,
):
    micro_count, rows, width = x_ref.shape
    queries, units = wq_ref.shape[1], wg_hbm.shape[1]
    me = lax.axis_index("ctx")

    def load(b):
        return pltpu.make_async_copy(x_hbm.at[b], x_ref.at[b], load_sem.at[b])

    for b in range(micro_count):
        load(b).start()
    wo_turned[...] = wo_ref[...].T
    qkv_own[:, :queries] = wq_ref[...]
    for n in range(kv_heads):
        at = queries + 2 * n * head
        own = slice(n * head, (n + 1) * head)
        qkv_own[:, at : at + head] = wk_ref[:, own]
        qkv_own[:, at + head : at + 2 * head] = wv_ref[:, own]
    sources = [qkv_own, wo_turned]
    peers, start, relay, finish = gather_parts(sources, [qkv_hbm, out_hbm], gather_sems, n_ctx)
    barrier = pltpu.get_barrier_semaphore()
    for peer in peers:
        pl.semaphore_signal(barrier, inc=1, device_id=peer, device_id_type=MESH)
    pl.semaphore_wait(barrier, len(peers))
    start()
    mlp_loads = [
        pltpu.make_async_copy(item, mlp_own.at[:, slice(i * units, (i + 1) * units)], mlp_sem.at[i])
        for i, item in enumerate((wg_hbm, wu_hbm))
    ]
    for copy in mlp_loads:
        copy.start()
    mlp_own[:, 2 * units :] = wd_ref[...].T

    def relays(low, high):
        for d in range(low, high):
            for item in range(len(sources)):
                relay(item, d)

    across = lax.broadcasted_iota(jnp.int32, (rows, rows), 1)
    down = lax.broadcasted_iota(jnp.int32, (rows, rows), 0)
    column_of = lambda row: jnp.broadcast_to(row, (8, rows)).T[:, :1]

    def in_order(row):
        column = column_of(row)
        place = jnp.sum((row < column).astype(jnp.int32), axis=1, keepdims=True)
        return place, jnp.sum(jnp.where(place == across, column, 0), axis=0, keepdims=True)

    for b in range(micro_count):

        def run(r, carry):
            row = order_ref[pl.ds(b * n_ctx + r, 1), :]
            keys_ref[pl.ds(b * n_ctx + r, 1), :] = in_order(row)[1]
            return carry

        lax.fori_loop(0, n_ctx, run, 0)
        row = order_ref[pl.ds(b * n_ctx + me, 1), :]
        place, packed = in_order(row)
        packed = column_of(packed)
        place_row = jnp.sum((column_of(row) < row).astype(jnp.int32), axis=0, keepdims=True)
        to_slot_ref[b] = (place == across).astype(F32).astype(BF16)
        to_sorted = (place_row == down).astype(F32).astype(BF16)
        to_sorted_ref[b] = to_sorted
        first = jnp.zeros_like(packed)
        begin = lengths_ref[b, 0] * 0
        for i in range(lengths_ref.shape[1]):
            first = jnp.maximum(first, jnp.where(packed >= begin, begin, 0))
            begin = begin + lengths_ref[b, i]
        newest_ref[b] = packed
        oldest_ref[b] = first
        angles = (packed - first).astype(F32) * frequency_ref[0:1, :]
        cos_ref[b] = jnp.cos(angles)
        sin_ref[b] = jnp.sin(angles) * frequency_ref[1:2, :]
        load(b).wait()
        for g in range(rows // GROUP):
            at = slice(g * GROUP, (g + 1) * GROUP)
            x = x_ref[b, at, :].astype(F32)
            inverse = lax.rsqrt(jnp.mean(x * x, axis=-1, keepdims=True) + EPSILON)
            normed_ref[at, :] = (x * inverse * gain_ref[...]).astype(BF16)
        for g in range(rows // GROUP):
            at = slice(g * GROUP, (g + 1) * GROUP)
            sorted_ref[b, at, :] = nn(to_sorted_ref[b, at, :], normed_ref[...]).astype(BF16)
        if b == 0:
            relays(1, min(3, n_ctx // 2))

    for copy in mlp_loads:
        copy.wait()
    mlp_save = pltpu.make_async_copy(mlp_own, mlp_hbm, mlp_sem.at[2])
    mlp_save.start()
    relays(min(3, n_ctx // 2), n_ctx // 2)
    finish()
    mlp_save.wait()


def begin(inputs, order, lengths, gain, frequency, weights, n_ctx, head, kv_heads, collective):
    micro_count, rows, width = inputs.shape
    wq, wk, wv, wo, wg, wu, wd = weights
    dma = pltpu.SemaphoreType.DMA
    chips = n_ctx // 2
    count = 2
    own, queries, units = wq.shape[0], wq.shape[1], wg.shape[1]
    some = lambda *dims: jax.ShapeDtypeStruct(dims, BF16)
    table = lambda *dims: jax.ShapeDtypeStruct(dims, F32)
    ints = lambda *dims: jax.ShapeDtypeStruct(dims, jnp.int32)
    inside, lies = pl.BlockSpec(memory_space=VMEM), pl.BlockSpec(memory_space=ANY)
    return pl.pallas_call(
        functools.partial(begin_kernel, n_ctx, head, kv_heads),
        out_shape=[
            some(n_ctx * own, queries + 2 * wk.shape[1]),
            some(n_ctx * own, wo.shape[0]),
            some(own, 3 * units),
            some(micro_count, rows, width),
            some(micro_count, rows, rows),
            some(micro_count, rows, rows),
            table(micro_count, rows, head),
            table(micro_count, rows, head),
            ints(micro_count * n_ctx, rows),
            ints(micro_count, rows, 1),
            ints(micro_count, rows, 1),
        ],
        in_specs=[lies, inside, pl.BlockSpec(memory_space=pltpu.SMEM), inside, inside]
        + [inside, inside, inside, inside, lies, lies, inside],
        out_specs=[lies] * 3 + [inside] * 8,
        scratch_shapes=[
            VMEM(inputs.shape, BF16),
            VMEM((rows, width), BF16),
            VMEM((own, queries + 2 * wk.shape[1]), BF16),
            VMEM((own, wo.shape[0]), BF16),
            VMEM((own, 3 * units), BF16),
            dma((micro_count,)),
            dma((3,)),
            dma((count,)),
        ]
        + [dma((count, chips))] * 4,
        compiler_params=params(60, collective),
        name="begin",
    )(inputs, order, lengths, gain, frequency, wq, wk, wv, wo, wg, wu, wd)


def qkv_kernel(heads, kv_heads, x_ref, w_ref, cos_ref, sin_ref, qg_ref, kg_ref, q_ref, kv_ref, raw_ref):
    head = qg_ref.shape[1]
    rows = nn(x_ref[...], w_ref[...])
    cosine, sine = cos_ref[...], sin_ref[...]

    def turn(part, gain):
        unit = part * lax.rsqrt(jnp.mean(part * part, axis=-1, keepdims=True) + EPSILON)
        scaled = unit * gain
        return (scaled * cosine + pltpu.roll(scaled, head // 2, 1) * sine).astype(BF16)

    for h in range(heads):
        part = rows[:, h * head : (h + 1) * head]
        raw_ref[:, h * head : (h + 1) * head] = part
        q_ref[:, h * head : (h + 1) * head] = turn(part, qg_ref[...])
    for n in range(kv_heads):
        at = (heads + 2 * n) * head
        part = rows[:, at : at + head]
        raw_ref[:, (heads + n) * head : (heads + n + 1) * head] = part
        kv_ref[:, 2 * n * head : (2 * n + 1) * head] = turn(part, kg_ref[...])
        kv_ref[:, (2 * n + 1) * head : (2 * n + 2) * head] = rows[:, at + head : at + 2 * head].astype(BF16)


def project_qkv(normed, weight, cosine, sine, query_gain, key_gain, heads, kv_heads):
    micro_count, total, width = normed.shape
    head = query_gain.shape[1]
    block = 256
    of = lambda cols: pl.BlockSpec((None, block, cols), lambda b, i: (b, i, 0))
    result = lambda cols, dtype: jax.ShapeDtypeStruct((micro_count, total, cols), dtype)
    return pl.pallas_call(
        functools.partial(qkv_kernel, heads, kv_heads),
        grid=(micro_count, total // block),
        out_shape=[
            result(heads * head, BF16),
            result(2 * kv_heads * head, BF16),
            result((heads + kv_heads) * head, F32),
        ],
        in_specs=[
            of(width),
            whole(weight.shape),
            of(head),
            of(head),
            whole((1, head)),
            whole((1, head)),
        ],
        out_specs=[of(heads * head), of(2 * kv_heads * head), of((heads + kv_heads) * head)],
        compiler_params=params(60),
        name="project_qkv",
    )(normed, weight, cosine, sine, query_gain, key_gain)


def heads_to_rows(block, head):
    return jnp.concatenate(
        [block[:, g * head : (g + 1) * head] for g in range(block.shape[1] // head)], axis=0
    )


def rows_to_heads(block, rows):
    return jnp.concatenate(
        [block[g * rows : (g + 1) * rows] for g in range(block.shape[0] // rows)], axis=1
    )


def head_parts(block, head, kv_heads):
    wide = block.shape[1] // kv_heads
    return [heads_to_rows(block[:, n * wide : (n + 1) * wide], head) for n in range(kv_heads)]


def keys_and_values(kv_ref, at, n, head):
    runs = kv_ref.shape[0]
    take = lambda i: kv_ref[:, at, i * head : (i + 1) * head].reshape(runs * SUB, head)
    return take(2 * n), take(2 * n + 1)


def forward_kernel(head, kv_heads, lo_ref, hi_ref, q_ref, kv_ref, pk_ref, pq_ref, sq_ref, out_ref, mass_ref):
    block = pl.program_id(0)
    rows = q_ref.shape[0]
    wide = q_ref.shape[1] // kv_heads
    group = wide // head
    scale = head ** (-0.5) * LOG2E
    queries = head_parts(q_ref[...], head, kv_heads)
    newest, oldest = pq_ref[...], sq_ref[...]

    def step(j, carry):
        at = pl.ds(pl.multiple_of(j * SUB, SUB), SUB)
        packed = pk_ref[j]
        allowed = (packed <= newest) & (packed >= oldest)
        allowed = jnp.concatenate([allowed] * group, axis=0)
        result = []
        for n, (total, mass) in enumerate(carry):
            keys, values = keys_and_values(kv_ref, at, n, head)
            probs = jnp.where(allowed, jnp.exp2(nt(queries[n], keys) * scale), 0.0)
            for i in range(probs.shape[1] // 128):
                mass = mass + probs[:, i * 128 : (i + 1) * 128]
            result.append((total + nn(probs.astype(BF16), values), mass))
        return tuple(result)

    zero = (jnp.zeros((group * rows, head), F32), jnp.zeros((group * rows, 128), F32))
    results = lax.fori_loop(lo_ref[block], hi_ref[block], step, (zero,) * kv_heads)
    for n, (total, mass) in enumerate(results):
        mass = jnp.sum(mass, axis=1, keepdims=True)
        out_ref[:, n * wide : (n + 1) * wide] = rows_to_heads(total / mass, rows)
        mass_ref[0, n : n + 1] = jnp.broadcast_to(jnp.log2(mass), (group * rows, 128)).T[0:1]


def attend_forward(query, index, kv, marks, head, kv_heads):
    lo, hi, pk_row, pq_col, sq_col = marks[:5]
    unused, rows, width = query.shape
    group = width // (kv_heads * head)
    blocks = rows // QROWS
    own = lambda i, *s: (i, 0)
    return pl.pallas_call(
        functools.partial(forward_kernel, head, kv_heads),
        grid_spec=pltpu.PrefetchScalarGridSpec(
            num_scalar_prefetch=2,
            grid=(blocks,),
            in_specs=[
                pl.BlockSpec((None, QROWS, width), lambda i, *s: (index, i, 0)),
                whole(kv.shape),
                whole(pk_row.shape),
                pl.BlockSpec((QROWS, 1), own),
                pl.BlockSpec((QROWS, 1), own),
            ],
            out_specs=[
                pl.BlockSpec((QROWS, width), own),
                pl.BlockSpec((1, kv_heads, group * QROWS), lambda i, *s: (i, 0, 0)),
            ],
        ),
        out_shape=[
            jax.ShapeDtypeStruct((rows, width), F32),
            jax.ShapeDtypeStruct((blocks, kv_heads, group * QROWS), F32),
        ],
        compiler_params=params(60),
        name="attend_forward",
    )(lo, hi, query, kv, pk_row, pq_col, sq_col)


def back(grad, unit, inverse, gain):
    scaled = grad * gain
    return inverse * (scaled - unit * jnp.mean(scaled * unit, axis=-1, keepdims=True))


def unturn(grad, cosine, sine):
    return grad * cosine - pltpu.roll(grad, grad.shape[1] // 2, 1) * sine


def backward_kernel(
    head,
    kv_heads,
    lo_ref,
    hi_ref,
    q_ref,
    kv_ref,
    pk_ref,
    pq_ref,
    sq_ref,
    g_ref,
    out_ref,
    mass_ref,
    raw_ref,
    cos_ref,
    sin_ref,
    gain_ref,
    dq_ref,
    dkv_ref,
    dgain_ref,
    acc,
):
    block = pl.program_id(0)
    runs = kv_ref.shape[0]
    rows = q_ref.shape[0]
    group = q_ref.shape[1] // (kv_heads * head)
    scale = head ** (-0.5)
    queries = head_parts(q_ref[...], head, kv_heads)
    grads = head_parts(g_ref[...], head, kv_heads)
    mixed = head_parts(out_ref[...], head, kv_heads)
    dots = []
    for grad, own in zip(grads, mixed):
        dot = jnp.sum(grad.astype(F32) * own, axis=1, keepdims=True)
        dots.append(jnp.broadcast_to(dot, (group * rows, 128)).T[0:1])
    newest, oldest = pq_ref[0], sq_ref[0]

    @pl.when(block == 0)
    def _():
        acc[...] = jnp.zeros_like(acc)
        dgain_ref[...] = jnp.zeros_like(dgain_ref)

    def step(j, dqs):
        at = pl.ds(pl.multiple_of(j * SUB, SUB), SUB)
        packed = jnp.broadcast_to(pk_ref[j], (8, pk_ref.shape[2])).T[:, :1]
        allowed = (packed <= newest) & (packed >= oldest)
        result = []
        for n, dq in enumerate(dqs):
            keys, values = keys_and_values(kv_ref, at, n, head)
            scores = nt(keys, queries[n]) * (scale * LOG2E) - mass_ref[0, n : n + 1]
            probs = jnp.where(allowed, jnp.exp2(scores), 0.0)
            dscores = (probs * (nt(values, grads[n]) - dots[n])).astype(BF16)
            key_cols = slice(2 * n * head, (2 * n + 1) * head)
            value_cols = slice((2 * n + 1) * head, (2 * n + 2) * head)
            acc[:, at, key_cols] += nn(dscores, queries[n]).reshape(runs, SUB, head)
            acc[:, at, value_cols] += nn(probs.astype(BF16), grads[n]).reshape(runs, SUB, head)
            result.append(dq + tn(dscores, keys))
        return tuple(result)

    zero = jnp.zeros((group * rows, head), F32)
    dqs = lax.fori_loop(lo_ref[block], hi_ref[block], step, (zero,) * kv_heads)
    cosine, sine = cos_ref[...], sin_ref[...]
    for n in range(kv_heads):
        for g in range(group):
            own = unturn(dqs[n][g * rows : (g + 1) * rows] * scale, cosine, sine)
            cols = slice((n * group + g) * head, (n * group + g + 1) * head)
            raw = raw_ref[:, cols]
            inverse = lax.rsqrt(jnp.mean(raw * raw, axis=-1, keepdims=True) + EPSILON)
            unit = raw * inverse
            dgain_ref[...] += jnp.sum(own * unit, axis=0, keepdims=True)
            dq_ref[:, cols] = back(own, unit, inverse, gain_ref[...]).astype(BF16)

    @pl.when(block == pl.num_programs(0) - 1)
    def _():
        for n in range(kv_heads):
            key_cols = slice(2 * n * head, (2 * n + 1) * head)
            value_cols = slice((2 * n + 1) * head, (2 * n + 2) * head)
            dkv_ref[:, :, key_cols] = (acc[:, :, key_cols] * scale).astype(BF16)
            dkv_ref[:, :, value_cols] = acc[:, :, value_cols].astype(BF16)


def attend_backward(query, index, kv, marks, grad, out, mass, raw, cosine, sine, gain, head, kv_heads):
    lo, hi, pk_row, unused, unused_too, pq_row, sq_row = marks
    unused, rows, width = query.shape
    group = width // (kv_heads * head)
    blocks = rows // QROWS
    own = lambda i, *s: (i, 0)
    line = lambda i, *s: (i, 0, 0)
    of = lambda cols: pl.BlockSpec((None, QROWS, cols), lambda i, *s: (index, i, 0))
    return pl.pallas_call(
        functools.partial(backward_kernel, head, kv_heads),
        grid_spec=pltpu.PrefetchScalarGridSpec(
            num_scalar_prefetch=2,
            grid=(blocks,),
            in_specs=[
                of(width),
                whole(kv.shape),
                whole(pk_row.shape),
                pl.BlockSpec((1, 1, group * QROWS), line),
                pl.BlockSpec((1, 1, group * QROWS), line),
                pl.BlockSpec((QROWS, width), own),
                pl.BlockSpec((QROWS, width), own),
                pl.BlockSpec((1, kv_heads, group * QROWS), line),
                of(width),
                of(head),
                of(head),
                whole((1, head)),
            ],
            out_specs=[pl.BlockSpec((QROWS, width), own), whole(kv.shape), whole((1, head))],
            scratch_shapes=[VMEM(kv.shape, F32)],
        ),
        out_shape=[
            jax.ShapeDtypeStruct((rows, width), BF16),
            jax.ShapeDtypeStruct(kv.shape, BF16),
            jax.ShapeDtypeStruct((1, head), F32),
        ],
        compiler_params=params(56),
        name="attend_backward",
    )(lo, hi, query, kv, pk_row, pq_row, sq_row, grad, out, mass, raw, cosine, sine, gain)


def key_back_kernel(head, kv_heads, grad_ref, raw_ref, cos_ref, sin_ref, gain_ref, out_ref, dgain_ref):
    cosine, sine = cos_ref[...], sin_ref[...]
    total = jnp.zeros((1, head), F32)
    for n in range(kv_heads):
        at = 2 * n * head
        own = unturn(grad_ref[:, at : at + head].astype(F32), cosine, sine)
        raw = raw_ref[:, n * head : (n + 1) * head]
        inverse = lax.rsqrt(jnp.mean(raw * raw, axis=-1, keepdims=True) + EPSILON)
        unit = raw * inverse
        total = total + jnp.sum(own * unit, axis=0, keepdims=True)
        out_ref[:, at : at + head] = back(own, unit, inverse, gain_ref[...]).astype(BF16)
        out_ref[:, at + head : at + 2 * head] = grad_ref[:, at + head : at + 2 * head]
    dgain_ref[...] = total


def key_back(grad, index, raw, cosine, sine, gain, kv_heads):
    rows = grad.shape[0]
    head = gain.shape[1]
    keys = pl.BlockSpec(
        (None, rows, kv_heads * head), lambda i: (index, 0, raw.shape[2] // (kv_heads * head) - 1)
    )
    turns = pl.BlockSpec((None, rows, head), lambda i: (index, 0, 0))
    return pl.pallas_call(
        functools.partial(key_back_kernel, head, kv_heads),
        grid=(1,),
        out_shape=[jax.ShapeDtypeStruct(grad.shape, BF16), jax.ShapeDtypeStruct((1, head), F32)],
        in_specs=[whole(grad.shape), keys, turns, turns, whole((1, head))],
        out_specs=[whole(grad.shape), whole((1, head))],
        compiler_params=params(32),
        name="key_back",
    )(grad, raw, cosine, sine, gain)


LOAD, SAVE = "load", "save"


class One:
    def __init__(self, array, index):
        self.array, self.index = array, index
        self.shape, self.dtype = array.shape[1:], array.dtype


def source(item):
    return item.array if isinstance(item, One) else item


class Loaded:
    def __init__(self, source, held, sem):
        self.ref = held
        self.copy = lambda: pltpu.make_async_copy(source, held, sem)

    def start(self):
        self.copy().start()

    def wait(self):
        self.copy().wait()


class Saved:
    def __init__(self, held, result, sems, axis):
        self.ref, self.result, self.sems, self.axis = held, result, sems, axis
        self.count = sems.shape[0]

    def part(self, i):
        size = self.ref.shape[self.axis] // self.count
        at = pl.ds(pl.multiple_of(i * size, size), size)
        return (at, slice(None)) if self.axis == 0 else (slice(None), at)

    def copy(self, i):
        at = self.part(i)
        return pltpu.make_async_copy(self.ref.at[at], self.result.at[at], self.sems.at[i])

    def save(self, i):
        self.copy(i).start()

    def finish(self):
        def one(i, carry):
            self.copy(i).wait()
            return carry

        lax.fori_loop(0, self.count, one, 0)


def run_jobs(n_tp, line, jobs, collective, megabytes, name, alias=None):
    rows, width = line[2], line[3]
    dma = pltpu.SemaphoreType.DMA
    line_scratch = [VMEM((rows, width), BF16)] * 5 + [dma((2, CHUNKS)), dma((2, CHUNKS))]
    parts = [(line[0], line[1], line_scratch)] + [job[:3] for job in jobs]
    arrays = [source(array) for part in parts for array, unused in part[0]]
    spec = lambda how: pl.BlockSpec(memory_space=VMEM if how is VMEM else ANY)
    scratch_shapes, plan = [], []
    for ins, outs, scratch in parts:
        at = len(scratch_shapes)
        scratch_shapes += scratch
        plan.append([range(at, len(scratch_shapes)), {}, {}])
        for i, (array, how) in enumerate(ins):
            if how is LOAD:
                plan[-1][1][i] = len(scratch_shapes)
                scratch_shapes += [VMEM(array.shape[-2:], array.dtype), dma]
        for i, (out, how) in enumerate(outs):
            if isinstance(how, tuple):
                plan[-1][2][i] = len(scratch_shapes)
                scratch_shapes += [VMEM(out.shape, out.dtype), dma((how[1],))]
    n_ins = sum(len(part[0]) for part in parts)
    n_outs = sum(len(part[1]) for part in parts)

    def kernel(*refs):
        ins, outs, scratch = refs[:n_ins], refs[n_ins : n_ins + n_outs], refs[n_ins + n_outs :]
        groups, loads, saves = [], [], []
        in_at = out_at = 0
        for (own_ins, own_outs, unused), (own_scratch, loaded, saved) in zip(parts, plan):
            in_refs = list(ins[in_at : in_at + len(own_ins)])
            out_refs = list(outs[out_at : out_at + len(own_outs)])
            in_at += len(own_ins)
            out_at += len(own_outs)
            for i, k in loaded.items():
                which = own_ins[i][0]
                at = in_refs[i].at[which.index] if isinstance(which, One) else in_refs[i]
                in_refs[i] = Loaded(at, scratch[k], scratch[k + 1])
                loads.append(in_refs[i])
            for i, k in saved.items():
                out_refs[i] = Saved(scratch[k], out_refs[i], scratch[k + 1], own_outs[i][1][2])
                saves.append(out_refs[i])
            groups.append((in_refs, out_refs, [scratch[k] for k in own_scratch]))
        for item in loads:
            item.start()
        bound = [job[3](*groups[i + 1]) for i, job in enumerate(jobs)]
        line_sum(n_tp, groups[0][2], line[4](*groups[0][:2]), bound)
        for item in saves:
            item.finish()

    return pl.pallas_call(
        kernel,
        out_shape=[out[0] for part in parts for out in part[1]],
        in_specs=[spec(how) for part in parts for unused, how in part[0]],
        out_specs=[spec(how) for part in parts for unused, how in part[1]],
        scratch_shapes=scratch_shapes,
        input_output_aliases=alias or {},
        compiler_params=params(megabytes, collective),
        name=name,
    )(*arrays)


def piece(c, rows):
    return pl.ds(pl.multiple_of(c * rows, rows), rows)


def line_sum(n_tp, scratch, main, jobs):
    part, from_left, from_right, to_right, to_left, send_sem, recv_sem = scratch
    produce_ready, consume_ready, produce, consume = main
    chunks = CHUNKS
    size = part.shape[0] // chunks
    groups = part.shape[0] // GROUP
    place = lax.axis_index("tp")
    line = lax.axis_index("ctx")
    has_left, has_right = place > 0, place < n_tp - 1
    barrier = pltpu.get_barrier_semaphore()
    peers = [peer for job in jobs for peer in job[0]]
    for peer in peers:
        pl.semaphore_signal(barrier, inc=1, device_id=peer, device_id_type=MESH)

    @pl.when(has_left)
    def _():
        pl.semaphore_signal(barrier, inc=1, device_id=(line, place - 1), device_id_type=MESH)

    @pl.when(has_right)
    def _():
        pl.semaphore_signal(barrier, inc=1, device_id=(line, place + 1), device_id_type=MESH)

    def fill(g):
        part[piece(g, GROUP), :] = produce(g).astype(BF16)

    for item in produce_ready:
        item.wait()
    fill(0)
    pl.semaphore_wait(
        barrier, has_left.astype(jnp.int32) + has_right.astype(jnp.int32) + len(peers)
    )
    for job in jobs:
        job[1]()

    def right(c):
        return pltpu.make_async_remote_copy(
            src_ref=to_right.at[piece(c, size)],
            dst_ref=from_left.at[piece(c, size)],
            send_sem=send_sem.at[0, c],
            recv_sem=recv_sem.at[0, c],
            device_id=(line, place + 1),
            device_id_type=MESH,
        )

    def left(c):
        return pltpu.make_async_remote_copy(
            src_ref=to_left.at[piece(c, size)],
            dst_ref=from_right.at[piece(c, size)],
            send_sem=send_sem.at[1, c],
            recv_sem=recv_sem.at[1, c],
            device_id=(line, place - 1),
            device_id_type=MESH,
        )

    def plus(a, b):
        return (a.astype(F32) + b.astype(F32)).astype(BF16)

    late = LAG * jnp.maximum(place, n_tp - 1 - place)

    def step(s, carry):
        c_right = s - LAG * place
        c_left = s - LAG * (n_tp - 1 - place)
        c_out = s - late

        @pl.when((c_right >= 0) & (c_right < chunks))
        def _():
            at = piece(c_right, size)

            @pl.when(jnp.logical_not(has_left))
            def _():
                to_right[at, :] = part[at, :]

            @pl.when(has_left)
            def _():
                right(c_right).wait_recv()
                to_right[at, :] = plus(part[at, :], from_left[at, :])

            @pl.when(has_right)
            def _():
                right(c_right).start()

        @pl.when((c_left >= 0) & (c_left < chunks))
        def _():
            at = piece(c_left, size)

            @pl.when(jnp.logical_not(has_right))
            def _():
                to_left[at, :] = part[at, :]

            @pl.when(has_right)
            def _():
                left(c_left).wait_recv()
                to_left[at, :] = plus(part[at, :], from_right[at, :])

            @pl.when(has_left)
            def _():
                left(c_left).start()

        @pl.when((s + 1 < groups))
        def _():
            fill(s + 1)

        @pl.when(s == 1)
        def _():
            for item in consume_ready:
                item.wait()

        @pl.when((c_out >= 0) & (c_out < chunks))
        def _():
            at = piece(c_out, size)

            @pl.when(has_right)
            def _():
                consume(c_out, to_right[at, :].astype(F32) + from_right[at, :].astype(F32))

            @pl.when(jnp.logical_not(has_right))
            def _():
                consume(c_out, to_right[at, :].astype(F32))

        for job in jobs:
            job[2](s)
        return carry

    lax.fori_loop(0, chunks + LAG * (n_tp - 1), step, 0)

    for job in jobs:
        job[3]()

    def finish(c, carry):
        @pl.when(has_right)
        def _():
            right(c).wait_send()

        @pl.when(has_left)
        def _():
            left(c).wait_send()

        return carry

    lax.fori_loop(0, chunks, finish, 0)


def mean_square(values):
    return jnp.mean(values * values, axis=-1, keepdims=True)


def shape(rows, width, dtype=BF16):
    return jax.ShapeDtypeStruct((rows, width), dtype)


def attn_out_line(mixed, place, weight, inputs, gain):
    rows, width = inputs.shape
    size = rows // CHUNKS
    groups = rows // GROUP

    def bind(ins, outs):
        mixed_in, place_in, w_in, x_in, gain_ref = ins
        own_out, middle_out, normed_out = outs

        def produce(g):
            own = nn(place_in.ref[piece(g, GROUP), :], mixed_in.ref[...].astype(BF16)).astype(BF16)
            own_out.ref[piece(g, GROUP), :] = own
            own_out.save(g)
            return nt(own, w_in.ref[...])

        def consume(c, total):
            at = piece(c, size)
            middle = x_in.ref[at, :].astype(F32) + total
            middle_out.ref[at, :] = middle.astype(BF16)
            middle_out.save(c)
            unit = middle * lax.rsqrt(mean_square(middle) + EPSILON)
            normed_out.ref[at, :] = (unit * gain_ref[...]).astype(BF16)
            normed_out.save(c)

        return [mixed_in, place_in, w_in], [x_in], produce, consume

    return (
        [(mixed, LOAD), (place, LOAD), (weight, LOAD), (inputs, LOAD), (gain, VMEM)],
        [
            (shape(*mixed.shape), (SAVE, groups, 0)),
            (shape(rows, width), (SAVE, CHUNKS, 0)),
            (shape(rows, width), (SAVE, CHUNKS, 0)),
        ],
        rows,
        width,
        bind,
    )


def middle_back_line(part, grad, middle, gain, weight):
    rows, width = grad.shape
    size = rows // CHUNKS
    groups = rows // GROUP
    each = GROUP // size

    def bind(ins, outs):
        part_in, g_in, middle_in, gain_ref, w_in = ins
        low_out, mixed_out, dgain_ref = outs
        dgain_ref[...] = jnp.zeros_like(dgain_ref)

        def produce(g):
            return part_in.ref[piece(g, GROUP), :]

        def consume(c, total):
            at = piece(c, size)
            middle = middle_in.ref[at, :].astype(F32)
            inverse = lax.rsqrt(mean_square(middle) + EPSILON)
            unit = middle * inverse
            dgain_ref[...] += jnp.sum(total * unit, axis=0, keepdims=True)
            grad = g_in.ref[at, :].astype(F32) + back(total, unit, inverse, gain_ref[...])
            low_out.ref[at, :] = grad.astype(BF16)
            low_out.save(c)

            @pl.when(lax.rem(c, each) == each - 1)
            def _():
                g = c // each
                at = piece(g, GROUP)
                mixed_out.ref[at, :] = nn(low_out.ref[at, :], w_in.ref[...]).astype(BF16)
                mixed_out.save(g)

        return [part_in], [g_in, middle_in, w_in], produce, consume

    return (
        [(part, LOAD), (grad, LOAD), (middle, LOAD), (gain, VMEM), (weight, LOAD)],
        [
            (shape(rows, width), (SAVE, CHUNKS, 0)),
            (shape(rows, weight.shape[1]), (SAVE, groups, 0)),
            (shape(1, width, F32), VMEM),
        ],
        rows,
        width,
        bind,
    )


def input_back_line(gq, gkv, place, weight, inputs, mid, gain):
    rows, width = inputs.shape
    size = rows // CHUNKS

    def bind(ins, outs):
        gq_in, gkv_in, place_in, w_in, x_in, mid_in, gain_ref = ins
        out, dgain_ref = outs
        queries = gq.shape[1]
        dgain_ref[...] = jnp.zeros_like(dgain_ref)

        def produce(g):
            slots = place_in.ref[piece(g, GROUP), :]
            own_q = nn(slots, gq_in.ref[...]).astype(BF16)
            own_kv = nn(slots, gkv_in.ref[...]).astype(BF16)
            return nt(own_q, w_in.ref[:, :queries]) + nt(own_kv, w_in.ref[:, queries:])

        def consume(c, total):
            at = piece(c, size)
            x = x_in.ref[at, :].astype(F32)
            inverse = lax.rsqrt(mean_square(x) + EPSILON)
            unit = x * inverse
            dgain_ref[...] += jnp.sum(total * unit, axis=0, keepdims=True)
            grad = mid_in.ref[at, :].astype(F32) + back(total, unit, inverse, gain_ref[...])
            out.ref[at, :] = grad.astype(BF16)
            out.save(c)

        return [gq_in, gkv_in, place_in, w_in], [x_in, mid_in], produce, consume

    return (
        [(item, LOAD) for item in (gq, gkv, place, weight, inputs, mid)] + [(gain, VMEM)],
        [(shape(rows, width), (SAVE, CHUNKS, 0)), (shape(1, width, F32), VMEM)],
        rows,
        width,
        bind,
    )


def gather_job(own, n_ctx):
    chips = n_ctx // 2
    dma = pltpu.SemaphoreType.DMA

    def bind(ins, outs, scratch):
        peers, start, relay, finish = gather_parts([ins[0].at[own.index]], outs, scratch, n_ctx)

        def hook(s):
            for d in range(1, chips):

                @pl.when(s == CHUNKS - 2 * chips + 2 * d)
                def _(d=d):
                    relay(0, d)

        return peers, start, hook, finish

    return (
        [(own, ANY)],
        [(shape(n_ctx * own.shape[0], own.shape[1]), ANY)],
        [dma((1,))] + [dma((1, chips))] * 4,
        bind,
    )


def mlp_job(middle, normed, grad, weight, n_tp):
    rows, width = normed.shape
    units = weight.shape[1] // 3
    tile = 256
    tiles, down_tiles = units // tile, width // tile
    share = 1.0 / n_tp
    every = max(1, CHUNKS // 16)
    dma = pltpu.SemaphoreType.DMA

    def bind(ins, outs, scratch):
        middle_in, x_in, g_in, w_hbm = ins
        hid, gg, gu, down_out, gn_out = outs
        w_ref, sem = scratch

        def load(t, part):
            at = pl.ds(pl.multiple_of(part * units + t * tile, tile), tile)
            return pltpu.make_async_copy(w_hbm.at[:, at], w_ref.at[:, at], sem.at[part, t])

        def start():
            for t in range(tiles):
                for part in range(3):
                    load(t, part).start()

        def first(t):
            for part in range(3):
                load(t, part).wait()
            cols = [
                pl.ds(pl.multiple_of(part * units + t * tile, tile), tile) for part in range(3)
            ]
            gate = nn(x_in.ref[...], w_ref[:, cols[0]])
            up = nn(x_in.ref[...], w_ref[:, cols[1]])
            grad = nn(g_in.ref[...], w_ref[:, cols[2]])
            sigmoid = jax.nn.sigmoid(gate)
            silu = gate * sigmoid
            hid.ref[:, cols[0]] = (silu * up).astype(BF16)
            gu.ref[:, cols[0]] = (grad * silu).astype(BF16)
            gg.ref[:, cols[0]] = (grad * up * sigmoid * (1.0 + gate * (1.0 - sigmoid))).astype(BF16)
            for out in (hid, gu, gg):
                out.save(t)

        def second(t):
            at = pl.ds(pl.multiple_of(t * tile, tile), tile)
            down = nt(hid.ref[...], w_ref[at, 2 * units :])
            down_out.ref[:, at] = (down + middle_in.ref[:, at].astype(F32) * share).astype(BF16)
            gn_out.ref[:, at] = (
                nt(gg.ref[...], w_ref[at, :units]) + nt(gu.ref[...], w_ref[at, units : 2 * units])
            ).astype(BF16)
            down_out.save(t)
            gn_out.save(t)

        def hook(s):
            h = (s - 1) // every
            now = lax.rem(s - 1, every) == 0

            @pl.when(s == 1)
            def _():
                for item in (middle_in, x_in, g_in):
                    item.wait()

            @pl.when(now & (s >= 1) & (h < tiles))
            def _():
                first(h)

            @pl.when(now & (h >= tiles) & (h < tiles + down_tiles))
            def _():
                second(h - tiles)

        return [], start, hook, lambda: None

    return (
        [(middle, LOAD), (normed, LOAD), (grad, LOAD), (weight, ANY)],
        [(shape(rows, units), (SAVE, tiles, 1))] * 3
        + [(shape(rows, width), (SAVE, down_tiles, 1))] * 2,
        [VMEM(weight.shape, BF16), dma((3, tiles))],
        bind,
    )


def weight_job(lefts, groups, tile, every, room):
    rows, width = lefts[0].shape
    rights = [side for unused, sides in groups for side in sides]
    counts = [sides[0].shape[1] // tile for unused, sides in groups]
    total = sum(counts)
    dma = pltpu.SemaphoreType.DMA
    sources = list(lefts) + rights

    def bind(ins, outs, scratch):
        (out_hbm,) = outs
        held = [item.ref for item in ins[: len(sources)]]
        out_buf, out_sem = scratch

        def save(h):
            slot = lax.rem(h, 2)
            return pltpu.make_async_copy(
                out_buf.at[slot],
                out_hbm.at[:, pl.ds(pl.multiple_of(h * tile, tile), tile)],
                out_sem.at[slot],
            )

        def hook(s):
            @pl.when(s == 1)
            def _():
                for item in ins[: len(sources)]:
                    item.wait()

            h = (s - 1) // every
            now = (s >= 1) & (lax.rem(s - 1, every) == 0) & (h < total)

            @pl.when(now & (h >= 2))
            def _():
                save(h - 2).wait()

            first, at = 0, len(lefts)
            for (indices, sides), count in zip(groups, counts):
                left_refs = [held[i] for i in indices]
                right_refs = held[at : at + len(sides)]
                at += len(sides)

                @pl.when(now & (h >= first) & (h < first + count))
                def _(left_refs=left_refs, right_refs=right_refs, first=first):
                    cols = pl.ds(pl.multiple_of((h - first) * tile, tile), tile)
                    grads = tn(left_refs[0][...], right_refs[0][:, cols])
                    for left_ref, right_ref in zip(left_refs[1:], right_refs[1:]):
                        grads = grads + tn(left_ref[...], right_ref[:, cols])
                    out_buf[lax.rem(h, 2)] = grads.astype(BF16)

                first += count

            @pl.when(now)
            def _():
                save(h).start()

        def finish():
            save(total - 2).wait()
            save(total - 1).wait()

        return [], lambda: None, hook, finish

    return (
        [(item, LOAD) for item in sources] + [(room, ANY)],
        [(shape(width, total * tile), ANY)],
        [VMEM((2, width, tile), BF16), dma((2,))],
        bind,
    )


def scatter_job(whole_rows, n_ctx, dtype, first, second):
    total, width = whole_rows.shape
    rows = total // n_ctx
    chips = n_ctx // 2
    dma = pltpu.SemaphoreType.DMA

    def bind(ins, outs, scratch):
        (source,), (out_ref,) = ins, outs
        mine, near, far, load_sem, near_send, near_recv, far_send, far_recv = scratch
        me, column = lax.axis_index("ctx"), lax.axis_index("tp")
        chip, core = me // 2, lax.rem(me, 2)

        def block(d, which):
            at = (jnp.bitwise_xor(chip, d) * 2 + which) * rows
            return source.at[pl.ds(pl.multiple_of(at, rows), rows)]

        def load(d):
            return pltpu.make_async_copy(block(d, core), mine.at[d], load_sem.at[d])

        def beside(d):
            return pltpu.make_async_remote_copy(
                src_ref=block(d, 1 - core),
                dst_ref=near.at[d],
                send_sem=near_send.at[d],
                recv_sem=near_recv.at[d],
                device_id=(chip * 2 + 1 - core, column),
                device_id_type=MESH,
            )

        def across(d):
            return pltpu.make_async_remote_copy(
                src_ref=mine.at[d],
                dst_ref=far.at[d - 1],
                send_sem=far_send.at[d],
                recv_sem=far_recv.at[d],
                device_id=(jnp.bitwise_xor(chip, d) * 2 + core, column),
                device_id_type=MESH,
            )

        peers = [(chip * 2 + 1 - core, column)] + [
            (jnp.bitwise_xor(chip, d) * 2 + core, column) for d in range(1, chips)
        ]
        order = list(range(chips - 1, -1, -1))

        def start():
            for d in order:
                load(d).start()
                beside(d).start()

        def near_sum():
            for d in order:
                load(d).wait()
                beside(d).wait_recv()
                mine[d] = (mine[d].astype(F32) + near[d].astype(F32)).astype(BF16)
                if d > 0:
                    across(d).start()

        def far_sum():
            for d in range(1, chips):
                across(d).wait_recv()
            result = mine[0].astype(F32)
            for d in range(1, chips):
                result = result + far[d - 1].astype(F32)
            out_ref[...] = result.astype(dtype)

        def hook(s):
            @pl.when(s == first)
            def _():
                near_sum()

            @pl.when(s == second)
            def _():
                far_sum()

        def finish():
            for d in range(chips):
                beside(d).wait_send()
                if d > 0:
                    across(d).wait_send()

        return peers, start, hook, finish

    return (
        [(whole_rows, ANY)],
        [(shape(rows, width, dtype), VMEM)],
        [
            VMEM((chips, rows, width), BF16),
            VMEM((chips, rows, width), BF16),
            VMEM((chips - 1, rows, width), BF16),
        ]
        + [dma((chips,))] * 5,
        bind,
    )


def weight_kernel(starts, parts, *refs):
    out_ref = refs[-1]
    step = pl.program_id(0)
    at = 0
    for index, (lefts, first, last) in enumerate(starts):
        left_refs = [refs[i] for i in lefts]
        right_refs = refs[parts + at : parts + at + len(lefts)]
        at += len(lefts)

        @pl.when((step >= first) & (step < last))
        def _(left_refs=left_refs, right_refs=right_refs):
            total = tn(left_refs[0][...], right_refs[0][...])
            for left_ref, right_ref in zip(left_refs[1:], right_refs[1:]):
                total = total + tn(left_ref[...], right_ref[...])
            out_ref[...] = total.astype(BF16)


def weight_grads(lefts, groups, tile):
    rows, width = lefts[0].shape
    starts, specs, rights, at = [], [], [], 0
    for indices, sides in groups:
        tiles = sides[0].shape[1] // tile
        starts.append((indices, at, at + tiles))
        for side in sides:
            rights.append(side)
            specs.append(
                pl.BlockSpec(
                    (rows, tile), lambda j, at=at, tiles=tiles: (0, jnp.clip(j - at, 0, tiles - 1))
                )
            )
        at += tiles
    return pl.pallas_call(
        functools.partial(weight_kernel, starts, len(lefts)),
        grid=(at,),
        out_shape=jax.ShapeDtypeStruct((width, at * tile), BF16),
        in_specs=[
            pl.BlockSpec((None, rows, width), lambda j, at=left.index: (at, 0, 0))
            if isinstance(left, One)
            else whole((rows, width))
            for left in lefts
        ]
        + specs,
        out_specs=pl.BlockSpec((width, tile), lambda j: (0, j)),
        compiler_params=params(60),
        name="weight_grads",
    )(*[source(left) for left in lefts], *rights)


def mlp_results_kernel(grads_ref, gate_ref, up_ref, down_ref):
    units = gate_ref.shape[1]
    gate_ref[...] = grads_ref[:, :units].astype(F32)
    up_ref[...] = grads_ref[:, units : 2 * units].astype(F32)
    down_ref[...] = grads_ref[:, 2 * units :].astype(F32).T


def mlp_results(grads):
    rows, units = grads.shape[0], grads.shape[1] // 3
    shapes = [(rows, units), (rows, units), (units, rows)]
    return pl.pallas_call(
        mlp_results_kernel,
        grid=(1,),
        out_shape=[jax.ShapeDtypeStruct(item, F32) for item in shapes],
        in_specs=[whole(grads.shape)],
        out_specs=[whole(item) for item in shapes],
        compiler_params=params(60),
        name="mlp_results",
    )(grads)


def attn_results_kernel(head, grads_ref, query_ref, key_ref, value_ref, out_ref):
    at = query_ref.shape[1]
    query_ref[...] = grads_ref[:, :at]
    for n in range(key_ref.shape[1] // head):
        own = slice(n * head, (n + 1) * head)
        key_ref[:, own] = grads_ref[:, at : at + head]
        value_ref[:, own] = grads_ref[:, at + head : at + 2 * head]
        at += 2 * head
    out_ref[...] = grads_ref[:, at:].T


def attn_results(grads, head, queries, keys):
    rows = grads.shape[0]
    shapes = [(rows, queries), (rows, keys), (rows, keys), (queries, rows)]
    return pl.pallas_call(
        functools.partial(attn_results_kernel, head),
        grid=(1,),
        out_shape=[jax.ShapeDtypeStruct(item, F32) for item in shapes],
        in_specs=[whole(grads.shape)],
        out_specs=[whole(item) for item in shapes],
        compiler_params=params(60),
        name="attn_results",
    )(grads)


def gains_kernel(n_ctx, n_tp, x_ref, out_ref, got, send_sem, recv_sem, line_got, line_send, line_recv):
    me, place = lax.axis_index("ctx"), lax.axis_index("tp")
    barrier = pltpu.get_barrier_semaphore()
    others = [lax.rem(me + d, n_ctx) for d in range(1, n_ctx)]
    members = [lax.rem(place + d, n_tp) for d in range(1, n_tp)]
    for other in others:
        pl.semaphore_signal(barrier, inc=1, device_id=(other, place), device_id_type=MESH)
    for member in members:
        pl.semaphore_signal(barrier, inc=1, device_id=(me, member), device_id_type=MESH)
    pl.semaphore_wait(barrier, n_ctx + n_tp - 2)
    copies = [
        pltpu.make_async_remote_copy(
            src_ref=x_ref.at[other],
            dst_ref=got.at[d],
            send_sem=send_sem.at[d],
            recv_sem=recv_sem.at[d],
            device_id=(other, place),
            device_id_type=MESH,
        )
        for d, other in enumerate(others)
    ]
    for copy in copies:
        copy.start()
    total = x_ref[me]
    for d, copy in enumerate(copies):
        copy.wait()
        total = total + got[d]
    out_ref[...] = total
    copies = [
        pltpu.make_async_remote_copy(
            src_ref=out_ref,
            dst_ref=line_got.at[d],
            send_sem=line_send.at[d],
            recv_sem=line_recv.at[d],
            device_id=(me, member),
            device_id_type=MESH,
        )
        for d, member in enumerate(members)
    ]
    for copy in copies:
        copy.start()
    low = total[4:]
    for d, copy in enumerate(copies):
        copy.wait()
        low = low + line_got[d, 4:, :]
    out_ref[4:, :] = low


def sum_gains(blocks, n_ctx, n_tp, collective):
    dma = pltpu.SemaphoreType.DMA
    return pl.pallas_call(
        functools.partial(gains_kernel, n_ctx, n_tp),
        out_shape=jax.ShapeDtypeStruct((8, 128), F32),
        in_specs=[pl.BlockSpec(memory_space=VMEM)],
        out_specs=pl.BlockSpec(memory_space=VMEM),
        scratch_shapes=[
            VMEM((n_ctx - 1, 8, 128), F32),
            dma((n_ctx - 1,)),
            dma((n_ctx - 1,)),
            VMEM((n_tp - 1, 8, 128), F32),
            dma((n_tp - 1,)),
            dma((n_tp - 1,)),
        ],
        compiler_params=params(16, collective),
        name="sum_gains",
    )(blocks)


def attention_marks(in_order, newest, oldest, n_ctx, group):
    rows = newest.shape[0]
    blocks = rows // SUB
    grouped = in_order.reshape(n_ctx, blocks, SUB)
    smallest = jnp.min(grouped[:, :, 0], axis=0)
    largest = jnp.max(grouped[:, :, SUB - 1], axis=0)
    first = oldest.reshape(-1, QROWS)[:, 0]
    last = newest.reshape(-1, QROWS)[:, QROWS - 1]
    lo = jnp.sum((largest[None, :] < first[:, None]).astype(jnp.int32), axis=1)
    hi = jnp.sum((smallest[None, :] <= last[:, None]).astype(jnp.int32), axis=1)
    keys = grouped.transpose(1, 0, 2).reshape(blocks, 1, n_ctx * SUB)
    of_group = lambda column: jnp.tile(column.reshape(-1, 1, QROWS), (1, 1, group))
    return lo, hi, keys, newest, oldest, of_group(newest), of_group(oldest)


def on_device(
    n_ctx,
    n_tp,
    hidden_in,
    seq_lengths,
    token_order,
    attn_gain,
    w_query,
    w_key,
    w_value,
    query_gain,
    key_gain,
    w_out,
    mlp_gain,
    w_gate,
    w_up,
    w_down,
    cotangent,
):
    micro_count, rows, width = hidden_in.shape
    head = query_gain.shape[0]
    heads, kv_heads = w_query.shape[1] // head, w_key.shape[1] // head
    rank = lax.axis_index("ctx")
    queries = heads * head
    units = w_gate.shape[1]
    q_gain, k_gain = query_gain[None, :], key_gain[None, :]
    a_gain, m_gain = attn_gain[None, :], mlp_gain[None, :]

    frequency = jnp.exp(jnp.arange(head // 2, dtype=F32) * (-2.0 * math.log(THETA) / head))
    one = jnp.ones((head // 2,), F32)
    frequency = jnp.stack([jnp.tile(frequency, 2), jnp.concatenate([-one, one])])
    (
        qkv_w,
        out_w,
        mlp_own,
        sorted_normed,
        to_slot,
        to_sorted,
        cosine,
        sine,
        in_order,
        newest,
        oldest,
    ) = begin(
        hidden_in,
        token_order.reshape(micro_count * n_ctx, rows),
        seq_lengths,
        a_gain,
        frequency,
        (w_query, w_key, w_value, w_out, w_gate, w_up, w_down),
        n_ctx,
        head,
        kv_heads,
        0,
    )
    both = range(micro_count)
    last = micro_count - 1
    orders = [
        (
            to_slot[b],
            to_sorted[b],
            attention_marks(
                in_order[b * n_ctx : (b + 1) * n_ctx], newest[b], oldest[b], n_ctx, heads // kv_heads
            ),
        )
        for b in both
    ]
    query, kv_own, raw = project_qkv(
        sorted_normed, qkv_w, cosine, sine, q_gain, k_gain, heads, kv_heads
    )
    kv_first = gather_ctx(kv_own, 0, n_ctx, 1)
    kv_all = [kv_first.reshape(n_ctx, rows, -1)]
    mlp_w = lax.all_gather(after(mlp_own, kv_first), "ctx", axis=0, tiled=True)

    def forward(b):
        return attend_forward(query, b, kv_all[b], orders[b][2], head, kv_heads)

    def out_line(b):
        return attn_out_line(attended[b][0], One(to_slot, b), out_w, One(hidden_in, b), m_gain)

    def middle_line(b):
        return middle_back_line(fed[b][4], One(cotangent, b), middles[b][1], m_gain, out_w)

    def feed(b):
        return mlp_job(middles[b][1], middles[b][2], One(cotangent, b), mlp_w, n_tp)

    attended, middles, fed, mids, backs = [], [], [], [], []
    attended.append(forward(0))
    results = run_jobs(n_tp, out_line(0), [gather_job(One(kv_own, 1), n_ctx)], 2, 60, "attn_out_gather")
    middles.append(results[:3])
    kv_all.append(results[3].reshape(n_ctx, rows, -1))
    attended.append(forward(1))
    results = run_jobs(n_tp, out_line(1), [feed(0)], 3, 60, "attn_out_mlp")
    middles.append(results[:3])
    fed.append(results[3:])
    results = run_jobs(n_tp, middle_line(0), [feed(1)], 4, 60, "middle_back_mlp")
    mids.append(results[:3])
    fed.append(results[3:])

    layer_out = jnp.stack(lax.psum([fed[b][3] for b in both], "tp"))

    def backward(b, grad):
        unused, sorting, marks = orders[b]
        g_mixed = nn(sorting, grad).astype(BF16)
        mixed_full, mass = attended[b]
        return attend_backward(
            query, b, kv_all[b], marks, g_mixed, mixed_full, mass, raw, cosine, sine, q_gain, head, kv_heads
        )

    backs.append(backward(0, mids[0][1]))
    tile = 512 if units % 512 == 0 else 256
    line = middle_line(1)
    line[0][0] = (after(line[0][0][0], backs[0][0]), LOAD)
    results = run_jobs(
        n_tp,
        line,
        [
            weight_job(
                [middles[b][2] for b in both] + [One(cotangent, b) for b in both],
                [
                    (tuple(both), [fed[b][1] for b in both]),
                    (tuple(both), [fed[b][2] for b in both]),
                    (tuple(micro_count + b for b in both), [fed[b][0] for b in both]),
                ],
                tile,
                2 * max(1, CHUNKS // 16),
                mlp_w,
            ),
            scatter_job(backs[0][1].reshape(n_ctx * rows, -1), n_ctx, BF16, CHUNKS // 4, CHUNKS),
        ],
        5,
        60,
        "middle_back_weights",
        {5 + 5 * micro_count: 3},
    )
    mids.append(results[:3])
    mlp_grads = lax.psum_scatter(results[3], "ctx", scatter_dimension=0, tiled=True)
    dkv_first = results[4]
    backs.append(backward(1, mids[1][1]))

    def key_part(b, dkv):
        return key_back(dkv, b, raw, cosine, sine, k_gain, kv_heads)

    def in_line(b, gkv):
        return input_back_line(
            backs[b][0], gkv, One(to_slot, b), qkv_w, One(hidden_in, b), mids[b][0], a_gain
        )

    gkv_first, dk_gain_first = key_part(0, after(dkv_first, backs[1][0]))
    results = run_jobs(
        n_tp,
        in_line(0, gkv_first),
        [scatter_job(backs[1][1].reshape(n_ctx * rows, -1), n_ctx, BF16, CHUNKS // 4, CHUNKS)],
        6,
        60,
        "input_back_keys",
    )
    grad_in_first, da_gain_first, dkv_last = results
    gkv_last, dk_gain_last = key_part(1, dkv_last)
    tile = min(512, 2 * kv_heads * head, queries)
    gkvs = [gkv_first, gkv_last]
    attn_grads = weight_grads(
        [One(sorted_normed, b) for b in both] + [mids[b][0] for b in both],
        [
            (tuple(both), [backs[b][0] for b in both]),
            (tuple(both), [gkvs[b] for b in both]),
            (tuple(micro_count + b for b in both), [middles[b][0] for b in both]),
        ],
        tile,
    )
    results = run_jobs(
        n_tp,
        in_line(1, gkv_last),
        [scatter_job(attn_grads, n_ctx, F32, CHUNKS // 4, CHUNKS + 2)],
        7,
        60,
        "input_back_weights",
    )
    grad_in_last, da_gain_last, attn_grads = results
    grads_in = [grad_in_first, grad_in_last]
    d_attn_gain = [da_gain_first, da_gain_last]
    d_key_gain = [dk_gain_first, dk_gain_last]

    share = width // n_ctx // 128
    own = lambda gain: sum(gain).reshape(n_ctx, share, 128)
    spread = lambda gain: jnp.broadcast_to(sum(gain)[None], (n_ctx, 1, 128))
    blank = jnp.zeros((n_ctx, 4 - 2 * share, 128), F32)
    low_blank = jnp.zeros((n_ctx, 2, 128), F32)
    gains = sum_gains(
        jnp.concatenate(
            [
                own(d_attn_gain),
                own([mids[b][2] for b in both]),
                blank,
                spread([backs[b][2] for b in both]),
                spread(d_key_gain),
                low_blank,
            ],
            axis=1,
        ),
        n_ctx,
        n_tp,
        8,
    )

    grad_query, grad_key, grad_value, grad_out = attn_results(
        attn_grads, head, queries, kv_heads * head
    )
    grad_gate, grad_up, grad_down = mlp_results(mlp_grads)
    return (
        layer_out,
        jnp.stack(grads_in).astype(F32),
        gains[:share].reshape(-1),
        grad_query,
        grad_key,
        grad_value,
        gains[4],
        gains[5],
        grad_out,
        gains[share : 2 * share].reshape(-1),
        grad_gate,
        grad_up,
        grad_down,
    )


def solution(mesh):
    rows = P("ctx", "tp")
    columns = P("tp", "ctx")
    tokens = P(None, "ctx", None)
    in_specs = (
        tokens,
        P(),
        P(),
        P(),
        rows,
        rows,
        rows,
        P(),
        P(),
        columns,
        P(),
        rows,
        rows,
        columns,
        tokens,
    )
    out_specs = (
        tokens,
        tokens,
        P("ctx"),
        rows,
        rows,
        rows,
        P(),
        P(),
        columns,
        P("ctx"),
        rows,
        rows,
        columns,
    )
    return jax.shard_map(
        functools.partial(on_device, mesh.shape["ctx"], mesh.shape["tp"]),
        mesh=mesh,
        in_specs=in_specs,
        out_specs=out_specs,
        check_vma=False,
    )
```

```python
import functools
import math

import jax
import jax.numpy as jnp
from jax import lax
from jax.experimental import pallas as pl
from jax.experimental.pallas import tpu as pltpu
from jax.sharding import PartitionSpec as P

EPSILON = 1e-06
THETA = 1000000.0
F32 = jnp.float32
BF16 = jnp.bfloat16
MESH = pl.DeviceIdType.MESH
VMEM = pltpu.VMEM
ANY = pl.ANY
LOG2E = math.log2(math.e)
SUB = 64
QROWS = 256
CHUNKS = 16
LAG = 2
GROUP = 128


def params(megabytes, collective=None):
    if collective is None:
        return pltpu.CompilerParams(vmem_limit_bytes=megabytes << 20)
    return pltpu.CompilerParams(
        vmem_limit_bytes=megabytes << 20, collective_id=collective, has_side_effects=True
    )


def nt(left_side, right_side):
    return lax.dot_general(
        left_side, right_side, (((1,), (1,)), ((), ())), preferred_element_type=F32
    )


def tn(left_side, right_side):
    return lax.dot_general(
        left_side, right_side, (((0,), (0,)), ((), ())), preferred_element_type=F32
    )


def nn(left_side, right_side):
    return jnp.dot(left_side, right_side, preferred_element_type=F32)


def whole(shape):
    return pl.BlockSpec(shape, lambda *ids: (0,) * len(shape))


def after(value, *others):
    return lax.optimization_barrier((value, others))[0]


def gather_parts(sources, results, sems, n_ctx):
    own_sem, send_sem, recv_sem, pass_sem, take_sem = sems
    count = len(sources)
    me = lax.axis_index("ctx")
    column = lax.axis_index("tp")
    chip, core = me // 2, lax.rem(me, 2)
    chips = n_ctx // 2
    partner = chip * 2 + 1 - core

    def peer(d):
        return jnp.bitwise_xor(chip, d) * 2 + core

    def rows_of(array, owner):
        rows = sources[array].shape[0]
        return results[array].at[pl.ds(pl.multiple_of(owner * rows, rows), rows)]

    def across(array, d):
        return pltpu.make_async_remote_copy(
            src_ref=sources[array],
            dst_ref=rows_of(array, me),
            send_sem=send_sem.at[array, d],
            recv_sem=recv_sem.at[array, d],
            device_id=(peer(d), column),
            device_id_type=MESH,
        )

    def passed(array, d):
        owner = peer(d)
        return pltpu.make_async_remote_copy(
            src_ref=sources[array] if d == 0 else rows_of(array, owner),
            dst_ref=rows_of(array, owner),
            send_sem=pass_sem.at[array, d],
            recv_sem=take_sem.at[array, d],
            device_id=(partner, column),
            device_id_type=MESH,
        )

    def local(array):
        return pltpu.make_async_copy(sources[array], rows_of(array, me), own_sem.at[array])

    def onward(array, d):
        rows = sources[array].shape[0]
        half = rows // 2
        slot = 3 if d == 1 else 0

        def of(owner):
            at = pl.multiple_of(owner * rows + (0 if d == 1 else half), half)
            return results[array].at[pl.ds(at, half)]

        return pltpu.make_async_remote_copy(
            src_ref=of(peer(d)),
            dst_ref=of(peer(d)),
            send_sem=send_sem.at[array, slot],
            recv_sem=recv_sem.at[array, slot],
            device_id=(peer(3 - d), column),
            device_id_type=MESH,
        )

    direct = range(1, chips) if chips != 4 else (1, 2)

    def start():
        for d in direct:
            for array in range(count):
                across(array, d).start()
        for array in range(count):
            passed(array, 0).start()
            local(array).start()

    def relay(array, d):
        if d in direct:
            across(array, d).wait_recv()
            if chips == 4:
                onward(array, d).start()
        else:
            onward(array, 1).wait_recv()
            onward(array, 2).wait_recv()
        passed(array, d).start()

    def finish():
        for array in range(count):
            local(array).wait()
            for d in range(chips):
                if d in direct:
                    across(array, d).wait_send()
                elif d > 0:
                    onward(array, 1).wait_send()
                    onward(array, 2).wait_send()
                passed(array, d).wait_send()
                passed(array, d).wait_recv()

    peers = [(partner, column)] + [(peer(d), column) for d in direct]
    return peers, start, relay, finish


def gather_kernel(index, n_ctx, source_ref, result_ref, *sems):
    peers, start, relay, finish = gather_parts([source_ref.at[index]], [result_ref], sems, n_ctx)
    barrier = pltpu.get_barrier_semaphore()
    for peer in peers:
        pl.semaphore_signal(barrier, inc=1, device_id=peer, device_id_type=MESH)
    pl.semaphore_wait(barrier, len(peers))
    start()
    for d in range(1, n_ctx // 2):
        relay(0, d)
    finish()


def gather_ctx(array, index, n_ctx, collective):
    dma = pltpu.SemaphoreType.DMA
    unused, rows, width = array.shape
    return pl.pallas_call(
        functools.partial(gather_kernel, index, n_ctx),
        out_shape=jax.ShapeDtypeStruct((n_ctx * rows, width), array.dtype),
        in_specs=[pl.BlockSpec(memory_space=ANY)],
        out_specs=pl.BlockSpec(memory_space=ANY),
        scratch_shapes=[dma((1,))] + [dma((1, n_ctx // 2))] * 4,
        compiler_params=params(60, collective),
        name="gather_ctx",
    )(array)


def begin_kernel(
    n_ctx,
    head,
    kv_heads,
    x_hbm,
    order_ref,
    lengths_ref,
    gain_ref,
    frequency_ref,
    wq_ref,
    wk_ref,
    wv_ref,
    wo_ref,
    wg_hbm,
    wu_hbm,
    wd_ref,
    qkv_hbm,
    out_hbm,
    mlp_hbm,
    sorted_ref,
    to_slot_ref,
    to_sorted_ref,
    cos_ref,
    sin_ref,
    keys_ref,
    newest_ref,
    oldest_ref,
    x_ref,
    normed_ref,
    qkv_own,
    wo_turned,
    mlp_own,
    load_sem,
    mlp_sem,
    *gather_sems,
):
    micro_count, rows, width = x_ref.shape
    queries, units = wq_ref.shape[1], wg_hbm.shape[1]
    me = lax.axis_index("ctx")

    def load(b):
        return pltpu.make_async_copy(x_hbm.at[b], x_ref.at[b], load_sem.at[b])

    for b in range(micro_count):
        load(b).start()
    wo_turned[...] = wo_ref[...].T
    qkv_own[:, :queries] = wq_ref[...]
    for n in range(kv_heads):
        at = queries + 2 * n * head
        own = slice(n * head, (n + 1) * head)
        qkv_own[:, at : at + head] = wk_ref[:, own]
        qkv_own[:, at + head : at + 2 * head] = wv_ref[:, own]
    sources = [qkv_own, wo_turned]
    peers, start, relay, finish = gather_parts(sources, [qkv_hbm, out_hbm], gather_sems, n_ctx)
    barrier = pltpu.get_barrier_semaphore()
    for peer in peers:
        pl.semaphore_signal(barrier, inc=1, device_id=peer, device_id_type=MESH)
    pl.semaphore_wait(barrier, len(peers))
    start()
    mlp_loads = [
        pltpu.make_async_copy(item, mlp_own.at[:, slice(i * units, (i + 1) * units)], mlp_sem.at[i])
        for i, item in enumerate((wg_hbm, wu_hbm))
    ]
    for copy in mlp_loads:
        copy.start()
    mlp_own[:, 2 * units :] = wd_ref[...].T

    def relays(low, high):
        for d in range(low, high):
            for item in range(len(sources)):
                relay(item, d)

    across = lax.broadcasted_iota(jnp.int32, (rows, rows), 1)
    down = lax.broadcasted_iota(jnp.int32, (rows, rows), 0)
    column_of = lambda row: jnp.broadcast_to(row, (8, rows)).T[:, :1]

    def in_order(row):
        column = column_of(row)
        place = jnp.sum((row < column).astype(jnp.int32), axis=1, keepdims=True)
        return place, jnp.sum(jnp.where(place == across, column, 0), axis=0, keepdims=True)

    for b in range(micro_count):

        def run(r, carry):
            row = order_ref[pl.ds(b * n_ctx + r, 1), :]
            keys_ref[pl.ds(b * n_ctx + r, 1), :] = in_order(row)[1]
            return carry

        lax.fori_loop(0, n_ctx, run, 0)
        row = order_ref[pl.ds(b * n_ctx + me, 1), :]
        place, packed = in_order(row)
        packed = column_of(packed)
        place_row = jnp.sum((column_of(row) < row).astype(jnp.int32), axis=0, keepdims=True)
        to_slot_ref[b] = (place == across).astype(F32).astype(BF16)
        to_sorted = (place_row == down).astype(F32).astype(BF16)
        to_sorted_ref[b] = to_sorted
        first = jnp.zeros_like(packed)
        begin = lengths_ref[b, 0] * 0
        for i in range(lengths_ref.shape[1]):
            first = jnp.maximum(first, jnp.where(packed >= begin, begin, 0))
            begin = begin + lengths_ref[b, i]
        newest_ref[b] = packed
        oldest_ref[b] = first
        angles = (packed - first).astype(F32) * frequency_ref[0:1, :]
        cos_ref[b] = jnp.cos(angles)
        sin_ref[b] = jnp.sin(angles) * frequency_ref[1:2, :]
        load(b).wait()
        for g in range(rows // GROUP):
            at = slice(g * GROUP, (g + 1) * GROUP)
            x = x_ref[b, at, :].astype(F32)
            inverse = lax.rsqrt(jnp.mean(x * x, axis=-1, keepdims=True) + EPSILON)
            normed_ref[at, :] = (x * inverse * gain_ref[...]).astype(BF16)
        for g in range(rows // GROUP):
            at = slice(g * GROUP, (g + 1) * GROUP)
            sorted_ref[b, at, :] = nn(to_sorted_ref[b, at, :], normed_ref[...]).astype(BF16)
        if b == 0:
            relays(1, min(3, n_ctx // 2))

    for copy in mlp_loads:
        copy.wait()
    mlp_save = pltpu.make_async_copy(mlp_own, mlp_hbm, mlp_sem.at[2])
    mlp_save.start()
    relays(min(3, n_ctx // 2), n_ctx // 2)
    finish()
    mlp_save.wait()


def begin(inputs, order, lengths, gain, frequency, weights, n_ctx, head, kv_heads, collective):
    micro_count, rows, width = inputs.shape
    wq, wk, wv, wo, wg, wu, wd = weights
    dma = pltpu.SemaphoreType.DMA
    chips = n_ctx // 2
    count = 2
    own, queries, units = wq.shape[0], wq.shape[1], wg.shape[1]
    some = lambda *dims: jax.ShapeDtypeStruct(dims, BF16)
    table = lambda *dims: jax.ShapeDtypeStruct(dims, F32)
    ints = lambda *dims: jax.ShapeDtypeStruct(dims, jnp.int32)
    inside, lies = pl.BlockSpec(memory_space=VMEM), pl.BlockSpec(memory_space=ANY)
    return pl.pallas_call(
        functools.partial(begin_kernel, n_ctx, head, kv_heads),
        out_shape=[
            some(n_ctx * own, queries + 2 * wk.shape[1]),
            some(n_ctx * own, wo.shape[0]),
            some(own, 3 * units),
            some(micro_count, rows, width),
            some(micro_count, rows, rows),
            some(micro_count, rows, rows),
            table(micro_count, rows, head),
            table(micro_count, rows, head),
            ints(micro_count * n_ctx, rows),
            ints(micro_count, rows, 1),
            ints(micro_count, rows, 1),
        ],
        in_specs=[lies, inside, pl.BlockSpec(memory_space=pltpu.SMEM), inside, inside]
        + [inside, inside, inside, inside, lies, lies, inside],
        out_specs=[lies] * 3 + [inside] * 8,
        scratch_shapes=[
            VMEM(inputs.shape, BF16),
            VMEM((rows, width), BF16),
            VMEM((own, queries + 2 * wk.shape[1]), BF16),
            VMEM((own, wo.shape[0]), BF16),
            VMEM((own, 3 * units), BF16),
            dma((micro_count,)),
            dma((3,)),
            dma((count,)),
        ]
        + [dma((count, chips))] * 4,
        compiler_params=params(60, collective),
        name="begin",
    )(inputs, order, lengths, gain, frequency, wq, wk, wv, wo, wg, wu, wd)


def qkv_kernel(heads, kv_heads, x_ref, w_ref, cos_ref, sin_ref, qg_ref, kg_ref, q_ref, kv_ref, raw_ref):
    head = qg_ref.shape[1]
    rows = nn(x_ref[...], w_ref[...])
    cosine, sine = cos_ref[...], sin_ref[...]

    def turn(part, gain):
        unit = part * lax.rsqrt(jnp.mean(part * part, axis=-1, keepdims=True) + EPSILON)
        scaled = unit * gain
        return (scaled * cosine + pltpu.roll(scaled, head // 2, 1) * sine).astype(BF16)

    for h in range(heads):
        part = rows[:, h * head : (h + 1) * head]
        raw_ref[:, h * head : (h + 1) * head] = part
        q_ref[:, h * head : (h + 1) * head] = turn(part, qg_ref[...])
    for n in range(kv_heads):
        at = (heads + 2 * n) * head
        part = rows[:, at : at + head]
        raw_ref[:, (heads + n) * head : (heads + n + 1) * head] = part
        kv_ref[:, 2 * n * head : (2 * n + 1) * head] = turn(part, kg_ref[...])
        kv_ref[:, (2 * n + 1) * head : (2 * n + 2) * head] = rows[:, at + head : at + 2 * head].astype(BF16)


def project_qkv(normed, weight, cosine, sine, query_gain, key_gain, heads, kv_heads):
    micro_count, total, width = normed.shape
    head = query_gain.shape[1]
    block = 256
    of = lambda cols: pl.BlockSpec((None, block, cols), lambda b, i: (b, i, 0))
    result = lambda cols, dtype: jax.ShapeDtypeStruct((micro_count, total, cols), dtype)
    return pl.pallas_call(
        functools.partial(qkv_kernel, heads, kv_heads),
        grid=(micro_count, total // block),
        out_shape=[
            result(heads * head, BF16),
            result(2 * kv_heads * head, BF16),
            result((heads + kv_heads) * head, F32),
        ],
        in_specs=[
            of(width),
            whole(weight.shape),
            of(head),
            of(head),
            whole((1, head)),
            whole((1, head)),
        ],
        out_specs=[of(heads * head), of(2 * kv_heads * head), of((heads + kv_heads) * head)],
        compiler_params=params(60),
        name="project_qkv",
    )(normed, weight, cosine, sine, query_gain, key_gain)


def heads_to_rows(block, head):
    return jnp.concatenate(
        [block[:, g * head : (g + 1) * head] for g in range(block.shape[1] // head)], axis=0
    )


def rows_to_heads(block, rows):
    return jnp.concatenate(
        [block[g * rows : (g + 1) * rows] for g in range(block.shape[0] // rows)], axis=1
    )


def head_parts(block, head, kv_heads):
    wide = block.shape[1] // kv_heads
    return [heads_to_rows(block[:, n * wide : (n + 1) * wide], head) for n in range(kv_heads)]


def keys_and_values(kv_ref, at, n, head):
    runs = kv_ref.shape[0]
    take = lambda i: kv_ref[:, at, i * head : (i + 1) * head].reshape(runs * SUB, head)
    return take(2 * n), take(2 * n + 1)


def forward_kernel(head, kv_heads, lo_ref, hi_ref, q_ref, kv_ref, pk_ref, pq_ref, sq_ref, out_ref, mass_ref):
    block = pl.program_id(0)
    rows = q_ref.shape[0]
    wide = q_ref.shape[1] // kv_heads
    group = wide // head
    scale = head ** (-0.5) * LOG2E
    queries = head_parts(q_ref[...], head, kv_heads)
    newest, oldest = pq_ref[...], sq_ref[...]

    def step(j, carry):
        at = pl.ds(pl.multiple_of(j * SUB, SUB), SUB)
        packed = pk_ref[j]
        allowed = (packed <= newest) & (packed >= oldest)
        allowed = jnp.concatenate([allowed] * group, axis=0)
        result = []
        for n, (total, mass) in enumerate(carry):
            keys, values = keys_and_values(kv_ref, at, n, head)
            probs = jnp.where(allowed, jnp.exp2(nt(queries[n], keys) * scale), 0.0)
            for i in range(probs.shape[1] // 128):
                mass = mass + probs[:, i * 128 : (i + 1) * 128]
            result.append((total + nn(probs.astype(BF16), values), mass))
        return tuple(result)

    zero = (jnp.zeros((group * rows, head), F32), jnp.zeros((group * rows, 128), F32))
    results = lax.fori_loop(lo_ref[block], hi_ref[block], step, (zero,) * kv_heads)
    for n, (total, mass) in enumerate(results):
        mass = jnp.sum(mass, axis=1, keepdims=True)
        out_ref[:, n * wide : (n + 1) * wide] = rows_to_heads(total / mass, rows)
        mass_ref[0, n : n + 1] = jnp.broadcast_to(jnp.log2(mass), (group * rows, 128)).T[0:1]


def attend_forward(query, index, kv, marks, head, kv_heads):
    lo, hi, pk_row, pq_col, sq_col = marks[:5]
    unused, rows, width = query.shape
    group = width // (kv_heads * head)
    blocks = rows // QROWS
    own = lambda i, *s: (i, 0)
    return pl.pallas_call(
        functools.partial(forward_kernel, head, kv_heads),
        grid_spec=pltpu.PrefetchScalarGridSpec(
            num_scalar_prefetch=2,
            grid=(blocks,),
            in_specs=[
                pl.BlockSpec((None, QROWS, width), lambda i, *s: (index, i, 0)),
                whole(kv.shape),
                whole(pk_row.shape),
                pl.BlockSpec((QROWS, 1), own),
                pl.BlockSpec((QROWS, 1), own),
            ],
            out_specs=[
                pl.BlockSpec((QROWS, width), own),
                pl.BlockSpec((1, kv_heads, group * QROWS), lambda i, *s: (i, 0, 0)),
            ],
        ),
        out_shape=[
            jax.ShapeDtypeStruct((rows, width), F32),
            jax.ShapeDtypeStruct((blocks, kv_heads, group * QROWS), F32),
        ],
        compiler_params=params(60),
        name="attend_forward",
    )(lo, hi, query, kv, pk_row, pq_col, sq_col)


def back(grad, unit, inverse, gain):
    scaled = grad * gain
    return inverse * (scaled - unit * jnp.mean(scaled * unit, axis=-1, keepdims=True))


def unturn(grad, cosine, sine):
    return grad * cosine - pltpu.roll(grad, grad.shape[1] // 2, 1) * sine


def backward_kernel(
    head,
    kv_heads,
    lo_ref,
    hi_ref,
    q_ref,
    kv_ref,
    pk_ref,
    pq_ref,
    sq_ref,
    g_ref,
    out_ref,
    mass_ref,
    raw_ref,
    cos_ref,
    sin_ref,
    gain_ref,
    dq_ref,
    dkv_ref,
    dgain_ref,
    acc,
):
    block = pl.program_id(0)
    runs = kv_ref.shape[0]
    rows = q_ref.shape[0]
    group = q_ref.shape[1] // (kv_heads * head)
    scale = head ** (-0.5)
    queries = head_parts(q_ref[...], head, kv_heads)
    grads = head_parts(g_ref[...], head, kv_heads)
    mixed = head_parts(out_ref[...], head, kv_heads)
    dots = []
    for grad, own in zip(grads, mixed):
        dot = jnp.sum(grad.astype(F32) * own, axis=1, keepdims=True)
        dots.append(jnp.broadcast_to(dot, (group * rows, 128)).T[0:1])
    newest, oldest = pq_ref[0], sq_ref[0]

    @pl.when(block == 0)
    def _():
        acc[...] = jnp.zeros_like(acc)
        dgain_ref[...] = jnp.zeros_like(dgain_ref)

    def step(j, dqs):
        at = pl.ds(pl.multiple_of(j * SUB, SUB), SUB)
        packed = jnp.broadcast_to(pk_ref[j], (8, pk_ref.shape[2])).T[:, :1]
        allowed = (packed <= newest) & (packed >= oldest)
        result = []
        for n, dq in enumerate(dqs):
            keys, values = keys_and_values(kv_ref, at, n, head)
            scores = nt(keys, queries[n]) * (scale * LOG2E) - mass_ref[0, n : n + 1]
            probs = jnp.where(allowed, jnp.exp2(scores), 0.0)
            dscores = (probs * (nt(values, grads[n]) - dots[n])).astype(BF16)
            key_cols = slice(2 * n * head, (2 * n + 1) * head)
            value_cols = slice((2 * n + 1) * head, (2 * n + 2) * head)
            acc[:, at, key_cols] += nn(dscores, queries[n]).reshape(runs, SUB, head)
            acc[:, at, value_cols] += nn(probs.astype(BF16), grads[n]).reshape(runs, SUB, head)
            result.append(dq + tn(dscores, keys))
        return tuple(result)

    zero = jnp.zeros((group * rows, head), F32)
    dqs = lax.fori_loop(lo_ref[block], hi_ref[block], step, (zero,) * kv_heads)
    cosine, sine = cos_ref[...], sin_ref[...]
    for n in range(kv_heads):
        for g in range(group):
            own = unturn(dqs[n][g * rows : (g + 1) * rows] * scale, cosine, sine)
            cols = slice((n * group + g) * head, (n * group + g + 1) * head)
            raw = raw_ref[:, cols]
            inverse = lax.rsqrt(jnp.mean(raw * raw, axis=-1, keepdims=True) + EPSILON)
            unit = raw * inverse
            dgain_ref[...] += jnp.sum(own * unit, axis=0, keepdims=True)
            dq_ref[:, cols] = back(own, unit, inverse, gain_ref[...]).astype(BF16)

    @pl.when(block == pl.num_programs(0) - 1)
    def _():
        for n in range(kv_heads):
            key_cols = slice(2 * n * head, (2 * n + 1) * head)
            value_cols = slice((2 * n + 1) * head, (2 * n + 2) * head)
            dkv_ref[:, :, key_cols] = (acc[:, :, key_cols] * scale).astype(BF16)
            dkv_ref[:, :, value_cols] = acc[:, :, value_cols].astype(BF16)


def attend_backward(query, index, kv, marks, grad, out, mass, raw, cosine, sine, gain, head, kv_heads):
    lo, hi, pk_row, unused, unused_too, pq_row, sq_row = marks
    unused, rows, width = query.shape
    group = width // (kv_heads * head)
    blocks = rows // QROWS
    own = lambda i, *s: (i, 0)
    line = lambda i, *s: (i, 0, 0)
    of = lambda cols: pl.BlockSpec((None, QROWS, cols), lambda i, *s: (index, i, 0))
    return pl.pallas_call(
        functools.partial(backward_kernel, head, kv_heads),
        grid_spec=pltpu.PrefetchScalarGridSpec(
            num_scalar_prefetch=2,
            grid=(blocks,),
            in_specs=[
                of(width),
                whole(kv.shape),
                whole(pk_row.shape),
                pl.BlockSpec((1, 1, group * QROWS), line),
                pl.BlockSpec((1, 1, group * QROWS), line),
                pl.BlockSpec((QROWS, width), own),
                pl.BlockSpec((QROWS, width), own),
                pl.BlockSpec((1, kv_heads, group * QROWS), line),
                of(width),
                of(head),
                of(head),
                whole((1, head)),
            ],
            out_specs=[pl.BlockSpec((QROWS, width), own), whole(kv.shape), whole((1, head))],
            scratch_shapes=[VMEM(kv.shape, F32)],
        ),
        out_shape=[
            jax.ShapeDtypeStruct((rows, width), BF16),
            jax.ShapeDtypeStruct(kv.shape, BF16),
            jax.ShapeDtypeStruct((1, head), F32),
        ],
        compiler_params=params(56),
        name="attend_backward",
    )(lo, hi, query, kv, pk_row, pq_row, sq_row, grad, out, mass, raw, cosine, sine, gain)


def key_back_kernel(head, kv_heads, grad_ref, raw_ref, cos_ref, sin_ref, gain_ref, out_ref, dgain_ref):
    cosine, sine = cos_ref[...], sin_ref[...]
    total = jnp.zeros((1, head), F32)
    for n in range(kv_heads):
        at = 2 * n * head
        own = unturn(grad_ref[:, at : at + head].astype(F32), cosine, sine)
        raw = raw_ref[:, n * head : (n + 1) * head]
        inverse = lax.rsqrt(jnp.mean(raw * raw, axis=-1, keepdims=True) + EPSILON)
        unit = raw * inverse
        total = total + jnp.sum(own * unit, axis=0, keepdims=True)
        out_ref[:, at : at + head] = back(own, unit, inverse, gain_ref[...]).astype(BF16)
        out_ref[:, at + head : at + 2 * head] = grad_ref[:, at + head : at + 2 * head]
    dgain_ref[...] = total


def key_back(grad, index, raw, cosine, sine, gain, kv_heads):
    rows = grad.shape[0]
    head = gain.shape[1]
    keys = pl.BlockSpec(
        (None, rows, kv_heads * head), lambda i: (index, 0, raw.shape[2] // (kv_heads * head) - 1)
    )
    turns = pl.BlockSpec((None, rows, head), lambda i: (index, 0, 0))
    return pl.pallas_call(
        functools.partial(key_back_kernel, head, kv_heads),
        grid=(1,),
        out_shape=[jax.ShapeDtypeStruct(grad.shape, BF16), jax.ShapeDtypeStruct((1, head), F32)],
        in_specs=[whole(grad.shape), keys, turns, turns, whole((1, head))],
        out_specs=[whole(grad.shape), whole((1, head))],
        compiler_params=params(32),
        name="key_back",
    )(grad, raw, cosine, sine, gain)


LOAD, SAVE = "load", "save"


class One:
    def __init__(self, array, index):
        self.array, self.index = array, index
        self.shape, self.dtype = array.shape[1:], array.dtype


def source(item):
    return item.array if isinstance(item, One) else item


class Loaded:
    def __init__(self, source, held, sem):
        self.ref = held
        self.copy = lambda: pltpu.make_async_copy(source, held, sem)

    def start(self):
        self.copy().start()

    def wait(self):
        self.copy().wait()


class Saved:
    def __init__(self, held, result, sems, axis):
        self.ref, self.result, self.sems, self.axis = held, result, sems, axis
        self.count = sems.shape[0]

    def part(self, i):
        size = self.ref.shape[self.axis] // self.count
        at = pl.ds(pl.multiple_of(i * size, size), size)
        return (at, slice(None)) if self.axis == 0 else (slice(None), at)

    def copy(self, i):
        at = self.part(i)
        return pltpu.make_async_copy(self.ref.at[at], self.result.at[at], self.sems.at[i])

    def save(self, i):
        self.copy(i).start()

    def finish(self):
        def one(i, carry):
            self.copy(i).wait()
            return carry

        lax.fori_loop(0, self.count, one, 0)


def run_jobs(n_tp, line, jobs, collective, megabytes, name, alias=None):
    rows, width = line[2], line[3]
    dma = pltpu.SemaphoreType.DMA
    line_scratch = [VMEM((rows, width), BF16)] * 5 + [dma((2, CHUNKS)), dma((2, CHUNKS))]
    parts = [(line[0], line[1], line_scratch)] + [job[:3] for job in jobs]
    arrays = [source(array) for part in parts for array, unused in part[0]]
    spec = lambda how: pl.BlockSpec(memory_space=VMEM if how is VMEM else ANY)
    scratch_shapes, plan = [], []
    for ins, outs, scratch in parts:
        at = len(scratch_shapes)
        scratch_shapes += scratch
        plan.append([range(at, len(scratch_shapes)), {}, {}])
        for i, (array, how) in enumerate(ins):
            if how is LOAD:
                plan[-1][1][i] = len(scratch_shapes)
                scratch_shapes += [VMEM(array.shape[-2:], array.dtype), dma]
        for i, (out, how) in enumerate(outs):
            if isinstance(how, tuple):
                plan[-1][2][i] = len(scratch_shapes)
                scratch_shapes += [VMEM(out.shape, out.dtype), dma((how[1],))]
    n_ins = sum(len(part[0]) for part in parts)
    n_outs = sum(len(part[1]) for part in parts)

    def kernel(*refs):
        ins, outs, scratch = refs[:n_ins], refs[n_ins : n_ins + n_outs], refs[n_ins + n_outs :]
        groups, loads, saves = [], [], []
        in_at = out_at = 0
        for (own_ins, own_outs, unused), (own_scratch, loaded, saved) in zip(parts, plan):
            in_refs = list(ins[in_at : in_at + len(own_ins)])
            out_refs = list(outs[out_at : out_at + len(own_outs)])
            in_at += len(own_ins)
            out_at += len(own_outs)
            for i, k in loaded.items():
                which = own_ins[i][0]
                at = in_refs[i].at[which.index] if isinstance(which, One) else in_refs[i]
                in_refs[i] = Loaded(at, scratch[k], scratch[k + 1])
                loads.append(in_refs[i])
            for i, k in saved.items():
                out_refs[i] = Saved(scratch[k], out_refs[i], scratch[k + 1], own_outs[i][1][2])
                saves.append(out_refs[i])
            groups.append((in_refs, out_refs, [scratch[k] for k in own_scratch]))
        for item in loads:
            item.start()
        bound = [job[3](*groups[i + 1]) for i, job in enumerate(jobs)]
        line_sum(n_tp, groups[0][2], line[4](*groups[0][:2]), bound)
        for item in saves:
            item.finish()

    return pl.pallas_call(
        kernel,
        out_shape=[out[0] for part in parts for out in part[1]],
        in_specs=[spec(how) for part in parts for unused, how in part[0]],
        out_specs=[spec(how) for part in parts for unused, how in part[1]],
        scratch_shapes=scratch_shapes,
        input_output_aliases=alias or {},
        compiler_params=params(megabytes, collective),
        name=name,
    )(*arrays)


def piece(c, rows):
    return pl.ds(pl.multiple_of(c * rows, rows), rows)


def line_sum(n_tp, scratch, main, jobs):
    part, from_left, from_right, to_right, to_left, send_sem, recv_sem = scratch
    produce_ready, consume_ready, produce, consume = main
    chunks = CHUNKS
    size = part.shape[0] // chunks
    groups = part.shape[0] // GROUP
    place = lax.axis_index("tp")
    line = lax.axis_index("ctx")
    has_left, has_right = place > 0, place < n_tp - 1
    barrier = pltpu.get_barrier_semaphore()
    peers = [peer for job in jobs for peer in job[0]]
    for peer in peers:
        pl.semaphore_signal(barrier, inc=1, device_id=peer, device_id_type=MESH)

    @pl.when(has_left)
    def _():
        pl.semaphore_signal(barrier, inc=1, device_id=(line, place - 1), device_id_type=MESH)

    @pl.when(has_right)
    def _():
        pl.semaphore_signal(barrier, inc=1, device_id=(line, place + 1), device_id_type=MESH)

    def fill(g):
        part[piece(g, GROUP), :] = produce(g).astype(BF16)

    for item in produce_ready:
        item.wait()
    fill(0)
    pl.semaphore_wait(
        barrier, has_left.astype(jnp.int32) + has_right.astype(jnp.int32) + len(peers)
    )
    for job in jobs:
        job[1]()

    def right(c):
        return pltpu.make_async_remote_copy(
            src_ref=to_right.at[piece(c, size)],
            dst_ref=from_left.at[piece(c, size)],
            send_sem=send_sem.at[0, c],
            recv_sem=recv_sem.at[0, c],
            device_id=(line, place + 1),
            device_id_type=MESH,
        )

    def left(c):
        return pltpu.make_async_remote_copy(
            src_ref=to_left.at[piece(c, size)],
            dst_ref=from_right.at[piece(c, size)],
            send_sem=send_sem.at[1, c],
            recv_sem=recv_sem.at[1, c],
            device_id=(line, place - 1),
            device_id_type=MESH,
        )

    def plus(a, b):
        return (a.astype(F32) + b.astype(F32)).astype(BF16)

    late = LAG * jnp.maximum(place, n_tp - 1 - place)

    def step(s, carry):
        c_right = s - LAG * place
        c_left = s - LAG * (n_tp - 1 - place)
        c_out = s - late

        @pl.when((c_right >= 0) & (c_right < chunks))
        def _():
            at = piece(c_right, size)

            @pl.when(jnp.logical_not(has_left))
            def _():
                to_right[at, :] = part[at, :]

            @pl.when(has_left)
            def _():
                right(c_right).wait_recv()
                to_right[at, :] = plus(part[at, :], from_left[at, :])

            @pl.when(has_right)
            def _():
                right(c_right).start()

        @pl.when((c_left >= 0) & (c_left < chunks))
        def _():
            at = piece(c_left, size)

            @pl.when(jnp.logical_not(has_right))
            def _():
                to_left[at, :] = part[at, :]

            @pl.when(has_right)
            def _():
                left(c_left).wait_recv()
                to_left[at, :] = plus(part[at, :], from_right[at, :])

            @pl.when(has_left)
            def _():
                left(c_left).start()

        @pl.when((s + 1 < groups))
        def _():
            fill(s + 1)

        @pl.when(s == 1)
        def _():
            for item in consume_ready:
                item.wait()

        @pl.when((c_out >= 0) & (c_out < chunks))
        def _():
            at = piece(c_out, size)

            @pl.when(has_right)
            def _():
                consume(c_out, to_right[at, :].astype(F32) + from_right[at, :].astype(F32))

            @pl.when(jnp.logical_not(has_right))
            def _():
                consume(c_out, to_right[at, :].astype(F32))

        for job in jobs:
            job[2](s)
        return carry

    lax.fori_loop(0, chunks + LAG * (n_tp - 1), step, 0)

    for job in jobs:
        job[3]()

    def finish(c, carry):
        @pl.when(has_right)
        def _():
            right(c).wait_send()

        @pl.when(has_left)
        def _():
            left(c).wait_send()

        return carry

    lax.fori_loop(0, chunks, finish, 0)


def mean_square(values):
    return jnp.mean(values * values, axis=-1, keepdims=True)


def shape(rows, width, dtype=BF16):
    return jax.ShapeDtypeStruct((rows, width), dtype)


def attn_out_line(mixed, place, weight, inputs, gain):
    rows, width = inputs.shape
    size = rows // CHUNKS
    groups = rows // GROUP

    def bind(ins, outs):
        mixed_in, place_in, w_in, x_in, gain_ref = ins
        own_out, middle_out, normed_out = outs

        def produce(g):
            own = nn(place_in.ref[piece(g, GROUP), :], mixed_in.ref[...].astype(BF16)).astype(BF16)
            own_out.ref[piece(g, GROUP), :] = own
            own_out.save(g)
            return nt(own, w_in.ref[...])

        def consume(c, total):
            at = piece(c, size)
            middle = x_in.ref[at, :].astype(F32) + total
            middle_out.ref[at, :] = middle.astype(BF16)
            middle_out.save(c)
            unit = middle * lax.rsqrt(mean_square(middle) + EPSILON)
            normed_out.ref[at, :] = (unit * gain_ref[...]).astype(BF16)
            normed_out.save(c)

        return [mixed_in, place_in, w_in], [x_in], produce, consume

    return (
        [(mixed, LOAD), (place, LOAD), (weight, LOAD), (inputs, LOAD), (gain, VMEM)],
        [
            (shape(*mixed.shape), (SAVE, groups, 0)),
            (shape(rows, width), (SAVE, CHUNKS, 0)),
            (shape(rows, width), (SAVE, CHUNKS, 0)),
        ],
        rows,
        width,
        bind,
    )


def middle_back_line(part, grad, middle, gain, weight):
    rows, width = grad.shape
    size = rows // CHUNKS
    groups = rows // GROUP
    each = GROUP // size

    def bind(ins, outs):
        part_in, g_in, middle_in, gain_ref, w_in = ins
        low_out, mixed_out, dgain_ref = outs
        dgain_ref[...] = jnp.zeros_like(dgain_ref)

        def produce(g):
            return part_in.ref[piece(g, GROUP), :]

        def consume(c, total):
            at = piece(c, size)
            middle = middle_in.ref[at, :].astype(F32)
            inverse = lax.rsqrt(mean_square(middle) + EPSILON)
            unit = middle * inverse
            dgain_ref[...] += jnp.sum(total * unit, axis=0, keepdims=True)
            grad = g_in.ref[at, :].astype(F32) + back(total, unit, inverse, gain_ref[...])
            low_out.ref[at, :] = grad.astype(BF16)
            low_out.save(c)

            @pl.when(lax.rem(c, each) == each - 1)
            def _():
                g = c // each
                at = piece(g, GROUP)
                mixed_out.ref[at, :] = nn(low_out.ref[at, :], w_in.ref[...]).astype(BF16)
                mixed_out.save(g)

        return [part_in], [g_in, middle_in, w_in], produce, consume

    return (
        [(part, LOAD), (grad, LOAD), (middle, LOAD), (gain, VMEM), (weight, LOAD)],
        [
            (shape(rows, width), (SAVE, CHUNKS, 0)),
            (shape(rows, weight.shape[1]), (SAVE, groups, 0)),
            (shape(1, width, F32), VMEM),
        ],
        rows,
        width,
        bind,
    )


def input_back_line(gq, gkv, place, weight, inputs, mid, gain):
    rows, width = inputs.shape
    size = rows // CHUNKS

    def bind(ins, outs):
        gq_in, gkv_in, place_in, w_in, x_in, mid_in, gain_ref = ins
        out, dgain_ref = outs
        queries = gq.shape[1]
        dgain_ref[...] = jnp.zeros_like(dgain_ref)

        def produce(g):
            slots = place_in.ref[piece(g, GROUP), :]
            own_q = nn(slots, gq_in.ref[...]).astype(BF16)
            own_kv = nn(slots, gkv_in.ref[...]).astype(BF16)
            return nt(own_q, w_in.ref[:, :queries]) + nt(own_kv, w_in.ref[:, queries:])

        def consume(c, total):
            at = piece(c, size)
            x = x_in.ref[at, :].astype(F32)
            inverse = lax.rsqrt(mean_square(x) + EPSILON)
            unit = x * inverse
            dgain_ref[...] += jnp.sum(total * unit, axis=0, keepdims=True)
            grad = mid_in.ref[at, :].astype(F32) + back(total, unit, inverse, gain_ref[...])
            out.ref[at, :] = grad.astype(BF16)
            out.save(c)

        return [gq_in, gkv_in, place_in, w_in], [x_in, mid_in], produce, consume

    return (
        [(item, LOAD) for item in (gq, gkv, place, weight, inputs, mid)] + [(gain, VMEM)],
        [(shape(rows, width), (SAVE, CHUNKS, 0)), (shape(1, width, F32), VMEM)],
        rows,
        width,
        bind,
    )


def gather_job(own, n_ctx):
    chips = n_ctx // 2
    dma = pltpu.SemaphoreType.DMA

    def bind(ins, outs, scratch):
        peers, start, relay, finish = gather_parts([ins[0].at[own.index]], outs, scratch, n_ctx)

        def hook(s):
            for d in range(1, chips):

                @pl.when(s == (CHUNKS + d if d > 2 else CHUNKS - 5 + d))
                def _(d=d):
                    relay(0, d)

        return peers, start, hook, finish

    return (
        [(own, ANY)],
        [(shape(n_ctx * own.shape[0], own.shape[1]), ANY)],
        [dma((1,))] + [dma((1, chips))] * 4,
        bind,
    )


def mlp_job(middle, normed, grad, weight, n_tp):
    rows, width = normed.shape
    units = weight.shape[1] // 3
    tile = 256
    tiles, down_tiles = units // tile, width // tile
    share = 1.0 / n_tp
    every = max(1, CHUNKS // 16)
    dma = pltpu.SemaphoreType.DMA

    def bind(ins, outs, scratch):
        middle_in, x_in, g_in, w_hbm = ins
        hid, gg, gu, down_out, gn_out = outs
        w_ref, sem = scratch

        def load(t, part):
            at = pl.ds(pl.multiple_of(part * units + t * tile, tile), tile)
            return pltpu.make_async_copy(w_hbm.at[:, at], w_ref.at[:, at], sem.at[part, t])

        def start():
            for t in range(tiles):
                for part in range(3):
                    load(t, part).start()

        def first(t):
            for part in range(3):
                load(t, part).wait()
            cols = [
                pl.ds(pl.multiple_of(part * units + t * tile, tile), tile) for part in range(3)
            ]
            gate = nn(x_in.ref[...], w_ref[:, cols[0]])
            up = nn(x_in.ref[...], w_ref[:, cols[1]])
            grad = nn(g_in.ref[...], w_ref[:, cols[2]])
            sigmoid = jax.nn.sigmoid(gate)
            silu = gate * sigmoid
            hid.ref[:, cols[0]] = (silu * up).astype(BF16)
            gu.ref[:, cols[0]] = (grad * silu).astype(BF16)
            gg.ref[:, cols[0]] = (grad * up * sigmoid * (1.0 + gate * (1.0 - sigmoid))).astype(BF16)
            for out in (hid, gu, gg):
                out.save(t)

        def second(t):
            at = pl.ds(pl.multiple_of(t * tile, tile), tile)
            down = nt(hid.ref[...], w_ref[at, 2 * units :])
            down_out.ref[:, at] = (down + middle_in.ref[:, at].astype(F32) * share).astype(BF16)
            gn_out.ref[:, at] = (
                nt(gg.ref[...], w_ref[at, :units]) + nt(gu.ref[...], w_ref[at, units : 2 * units])
            ).astype(BF16)
            down_out.save(t)
            gn_out.save(t)

        def hook(s):
            h = (s - 1) // every
            now = lax.rem(s - 1, every) == 0

            @pl.when(s == 1)
            def _():
                for item in (middle_in, x_in, g_in):
                    item.wait()

            @pl.when(now & (s >= 1) & (h < tiles))
            def _():
                first(h)

            @pl.when(now & (h >= tiles) & (h < tiles + down_tiles))
            def _():
                second(h - tiles)

        return [], start, hook, lambda: None

    return (
        [(middle, LOAD), (normed, LOAD), (grad, LOAD), (weight, ANY)],
        [(shape(rows, units), (SAVE, tiles, 1))] * 3
        + [(shape(rows, width), (SAVE, down_tiles, 1))] * 2,
        [VMEM(weight.shape, BF16), dma((3, tiles))],
        bind,
    )


def weight_job(lefts, groups, tile, every, room):
    rows, width = lefts[0].shape
    rights = [side for unused, sides in groups for side in sides]
    counts = [sides[0].shape[1] // tile for unused, sides in groups]
    total = sum(counts)
    dma = pltpu.SemaphoreType.DMA
    sources = list(lefts) + rights

    def bind(ins, outs, scratch):
        (out_hbm,) = outs
        held = [item.ref for item in ins[: len(sources)]]
        out_buf, out_sem = scratch

        def save(h):
            slot = lax.rem(h, 2)
            return pltpu.make_async_copy(
                out_buf.at[slot],
                out_hbm.at[:, pl.ds(pl.multiple_of(h * tile, tile), tile)],
                out_sem.at[slot],
            )

        def hook(s):
            @pl.when(s == 1)
            def _():
                for item in ins[: len(sources)]:
                    item.wait()

            h = (s - 1) // every
            now = (s >= 1) & (lax.rem(s - 1, every) == 0) & (h < total)

            @pl.when(now & (h >= 2))
            def _():
                save(h - 2).wait()

            first, at = 0, len(lefts)
            for (indices, sides), count in zip(groups, counts):
                left_refs = [held[i] for i in indices]
                right_refs = held[at : at + len(sides)]
                at += len(sides)

                @pl.when(now & (h >= first) & (h < first + count))
                def _(left_refs=left_refs, right_refs=right_refs, first=first):
                    cols = pl.ds(pl.multiple_of((h - first) * tile, tile), tile)
                    grads = tn(left_refs[0][...], right_refs[0][:, cols])
                    for left_ref, right_ref in zip(left_refs[1:], right_refs[1:]):
                        grads = grads + tn(left_ref[...], right_ref[:, cols])
                    out_buf[lax.rem(h, 2)] = grads.astype(BF16)

                first += count

            @pl.when(now)
            def _():
                save(h).start()

        def finish():
            save(total - 2).wait()
            save(total - 1).wait()

        return [], lambda: None, hook, finish

    return (
        [(item, LOAD) for item in sources] + [(room, ANY)],
        [(shape(width, total * tile), ANY)],
        [VMEM((2, width, tile), BF16), dma((2,))],
        bind,
    )


def scatter_job(whole_rows, n_ctx, dtype, first, second):
    total, width = whole_rows.shape
    rows = total // n_ctx
    chips = n_ctx // 2
    dma = pltpu.SemaphoreType.DMA

    def bind(ins, outs, scratch):
        (source,), (out_ref,) = ins, outs
        mine, near, far, load_sem, near_send, near_recv, far_send, far_recv = scratch
        me, column = lax.axis_index("ctx"), lax.axis_index("tp")
        chip, core = me // 2, lax.rem(me, 2)

        def block(d, which):
            at = (jnp.bitwise_xor(chip, d) * 2 + which) * rows
            return source.at[pl.ds(pl.multiple_of(at, rows), rows)]

        def load(d):
            return pltpu.make_async_copy(block(d, core), mine.at[d], load_sem.at[d])

        def beside(d):
            return pltpu.make_async_remote_copy(
                src_ref=block(d, 1 - core),
                dst_ref=near.at[d],
                send_sem=near_send.at[d],
                recv_sem=near_recv.at[d],
                device_id=(chip * 2 + 1 - core, column),
                device_id_type=MESH,
            )

        def across(d):
            return pltpu.make_async_remote_copy(
                src_ref=mine.at[d],
                dst_ref=far.at[d - 1],
                send_sem=far_send.at[d],
                recv_sem=far_recv.at[d],
                device_id=(jnp.bitwise_xor(chip, d) * 2 + core, column),
                device_id_type=MESH,
            )

        peers = [(chip * 2 + 1 - core, column)] + [
            (jnp.bitwise_xor(chip, d) * 2 + core, column) for d in range(1, chips)
        ]
        order = list(range(chips - 1, -1, -1))

        def start():
            for d in order:
                load(d).start()
                beside(d).start()

        def near_sum():
            for d in order:
                load(d).wait()
                beside(d).wait_recv()
                mine[d] = (mine[d].astype(F32) + near[d].astype(F32)).astype(BF16)
                if d > 0:
                    across(d).start()

        def far_sum():
            for d in range(1, chips):
                across(d).wait_recv()
            result = mine[0].astype(F32)
            for d in range(1, chips):
                result = result + far[d - 1].astype(F32)
            out_ref[...] = result.astype(dtype)

        def hook(s):
            @pl.when(s == first)
            def _():
                near_sum()

            @pl.when(s == second)
            def _():
                far_sum()

        def finish():
            for d in range(chips):
                beside(d).wait_send()
                if d > 0:
                    across(d).wait_send()

        return peers, start, hook, finish

    return (
        [(whole_rows, ANY)],
        [(shape(rows, width, dtype), VMEM)],
        [
            VMEM((chips, rows, width), BF16),
            VMEM((chips, rows, width), BF16),
            VMEM((chips - 1, rows, width), BF16),
        ]
        + [dma((chips,))] * 5,
        bind,
    )


def weight_kernel(starts, parts, *refs):
    out_ref = refs[-1]
    step = pl.program_id(0)
    at = 0
    for index, (lefts, first, last) in enumerate(starts):
        left_refs = [refs[i] for i in lefts]
        right_refs = refs[parts + at : parts + at + len(lefts)]
        at += len(lefts)

        @pl.when((step >= first) & (step < last))
        def _(left_refs=left_refs, right_refs=right_refs):
            total = tn(left_refs[0][...], right_refs[0][...])
            for left_ref, right_ref in zip(left_refs[1:], right_refs[1:]):
                total = total + tn(left_ref[...], right_ref[...])
            out_ref[...] = total.astype(BF16)


def weight_grads(lefts, groups, tile):
    rows, width = lefts[0].shape
    starts, specs, rights, at = [], [], [], 0
    for indices, sides in groups:
        tiles = sides[0].shape[1] // tile
        starts.append((indices, at, at + tiles))
        for side in sides:
            rights.append(side)
            specs.append(
                pl.BlockSpec(
                    (rows, tile), lambda j, at=at, tiles=tiles: (0, jnp.clip(j - at, 0, tiles - 1))
                )
            )
        at += tiles
    return pl.pallas_call(
        functools.partial(weight_kernel, starts, len(lefts)),
        grid=(at,),
        out_shape=jax.ShapeDtypeStruct((width, at * tile), BF16),
        in_specs=[
            pl.BlockSpec((None, rows, width), lambda j, at=left.index: (at, 0, 0))
            if isinstance(left, One)
            else whole((rows, width))
            for left in lefts
        ]
        + specs,
        out_specs=pl.BlockSpec((width, tile), lambda j: (0, j)),
        compiler_params=params(60),
        name="weight_grads",
    )(*[source(left) for left in lefts], *rights)


def mlp_results_kernel(grads_ref, gate_ref, up_ref, down_ref):
    units = gate_ref.shape[1]
    gate_ref[...] = grads_ref[:, :units].astype(F32)
    up_ref[...] = grads_ref[:, units : 2 * units].astype(F32)
    down_ref[...] = grads_ref[:, 2 * units :].astype(F32).T


def mlp_results(grads):
    rows, units = grads.shape[0], grads.shape[1] // 3
    shapes = [(rows, units), (rows, units), (units, rows)]
    return pl.pallas_call(
        mlp_results_kernel,
        grid=(1,),
        out_shape=[jax.ShapeDtypeStruct(item, F32) for item in shapes],
        in_specs=[whole(grads.shape)],
        out_specs=[whole(item) for item in shapes],
        compiler_params=params(60),
        name="mlp_results",
    )(grads)


def attn_results_kernel(head, grads_ref, query_ref, key_ref, value_ref, out_ref):
    at = query_ref.shape[1]
    query_ref[...] = grads_ref[:, :at]
    for n in range(key_ref.shape[1] // head):
        own = slice(n * head, (n + 1) * head)
        key_ref[:, own] = grads_ref[:, at : at + head]
        value_ref[:, own] = grads_ref[:, at + head : at + 2 * head]
        at += 2 * head
    out_ref[...] = grads_ref[:, at:].T


def attn_results(grads, head, queries, keys):
    rows = grads.shape[0]
    shapes = [(rows, queries), (rows, keys), (rows, keys), (queries, rows)]
    return pl.pallas_call(
        functools.partial(attn_results_kernel, head),
        grid=(1,),
        out_shape=[jax.ShapeDtypeStruct(item, F32) for item in shapes],
        in_specs=[whole(grads.shape)],
        out_specs=[whole(item) for item in shapes],
        compiler_params=params(60),
        name="attn_results",
    )(grads)


def gains_kernel(n_ctx, n_tp, x_ref, out_ref, got, send_sem, recv_sem, line_got, line_send, line_recv):
    me, place = lax.axis_index("ctx"), lax.axis_index("tp")
    barrier = pltpu.get_barrier_semaphore()
    others = [lax.rem(me + d, n_ctx) for d in range(1, n_ctx)]
    members = [lax.rem(place + d, n_tp) for d in range(1, n_tp)]
    for other in others:
        pl.semaphore_signal(barrier, inc=1, device_id=(other, place), device_id_type=MESH)
    for member in members:
        pl.semaphore_signal(barrier, inc=1, device_id=(me, member), device_id_type=MESH)
    pl.semaphore_wait(barrier, n_ctx + n_tp - 2)
    copies = [
        pltpu.make_async_remote_copy(
            src_ref=x_ref.at[other],
            dst_ref=got.at[d],
            send_sem=send_sem.at[d],
            recv_sem=recv_sem.at[d],
            device_id=(other, place),
            device_id_type=MESH,
        )
        for d, other in enumerate(others)
    ]
    for copy in copies:
        copy.start()
    total = x_ref[me]
    for d, copy in enumerate(copies):
        copy.wait()
        total = total + got[d]
    out_ref[...] = total
    copies = [
        pltpu.make_async_remote_copy(
            src_ref=out_ref,
            dst_ref=line_got.at[d],
            send_sem=line_send.at[d],
            recv_sem=line_recv.at[d],
            device_id=(me, member),
            device_id_type=MESH,
        )
        for d, member in enumerate(members)
    ]
    for copy in copies:
        copy.start()
    low = total[4:]
    for d, copy in enumerate(copies):
        copy.wait()
        low = low + line_got[d, 4:, :]
    out_ref[4:, :] = low


def sum_gains(blocks, n_ctx, n_tp, collective):
    dma = pltpu.SemaphoreType.DMA
    return pl.pallas_call(
        functools.partial(gains_kernel, n_ctx, n_tp),
        out_shape=jax.ShapeDtypeStruct((8, 128), F32),
        in_specs=[pl.BlockSpec(memory_space=VMEM)],
        out_specs=pl.BlockSpec(memory_space=VMEM),
        scratch_shapes=[
            VMEM((n_ctx - 1, 8, 128), F32),
            dma((n_ctx - 1,)),
            dma((n_ctx - 1,)),
            VMEM((n_tp - 1, 8, 128), F32),
            dma((n_tp - 1,)),
            dma((n_tp - 1,)),
        ],
        compiler_params=params(16, collective),
        name="sum_gains",
    )(blocks)


def attention_marks(in_order, newest, oldest, n_ctx, group):
    rows = newest.shape[0]
    blocks = rows // SUB
    grouped = in_order.reshape(n_ctx, blocks, SUB)
    smallest = jnp.min(grouped[:, :, 0], axis=0)
    largest = jnp.max(grouped[:, :, SUB - 1], axis=0)
    first = oldest.reshape(-1, QROWS)[:, 0]
    last = newest.reshape(-1, QROWS)[:, QROWS - 1]
    lo = jnp.sum((largest[None, :] < first[:, None]).astype(jnp.int32), axis=1)
    hi = jnp.sum((smallest[None, :] <= last[:, None]).astype(jnp.int32), axis=1)
    keys = grouped.transpose(1, 0, 2).reshape(blocks, 1, n_ctx * SUB)
    of_group = lambda column: jnp.tile(column.reshape(-1, 1, QROWS), (1, 1, group))
    return lo, hi, keys, newest, oldest, of_group(newest), of_group(oldest)


def on_device(
    n_ctx,
    n_tp,
    hidden_in,
    seq_lengths,
    token_order,
    attn_gain,
    w_query,
    w_key,
    w_value,
    query_gain,
    key_gain,
    w_out,
    mlp_gain,
    w_gate,
    w_up,
    w_down,
    cotangent,
):
    micro_count, rows, width = hidden_in.shape
    head = query_gain.shape[0]
    heads, kv_heads = w_query.shape[1] // head, w_key.shape[1] // head
    rank = lax.axis_index("ctx")
    queries = heads * head
    units = w_gate.shape[1]
    q_gain, k_gain = query_gain[None, :], key_gain[None, :]
    a_gain, m_gain = attn_gain[None, :], mlp_gain[None, :]

    frequency = jnp.exp(jnp.arange(head // 2, dtype=F32) * (-2.0 * math.log(THETA) / head))
    one = jnp.ones((head // 2,), F32)
    frequency = jnp.stack([jnp.tile(frequency, 2), jnp.concatenate([-one, one])])
    (
        qkv_w,
        out_w,
        mlp_own,
        sorted_normed,
        to_slot,
        to_sorted,
        cosine,
        sine,
        in_order,
        newest,
        oldest,
    ) = begin(
        hidden_in,
        token_order.reshape(micro_count * n_ctx, rows),
        seq_lengths,
        a_gain,
        frequency,
        (w_query, w_key, w_value, w_out, w_gate, w_up, w_down),
        n_ctx,
        head,
        kv_heads,
        0,
    )
    both = range(micro_count)
    last = micro_count - 1
    orders = [
        (
            to_slot[b],
            to_sorted[b],
            attention_marks(
                in_order[b * n_ctx : (b + 1) * n_ctx], newest[b], oldest[b], n_ctx, heads // kv_heads
            ),
        )
        for b in both
    ]
    query, kv_own, raw = project_qkv(
        sorted_normed, qkv_w, cosine, sine, q_gain, k_gain, heads, kv_heads
    )
    kv_first = gather_ctx(kv_own, 0, n_ctx, 1)
    kv_all = [kv_first.reshape(n_ctx, rows, -1)]
    mlp_w = lax.all_gather(after(mlp_own, kv_first), "ctx", axis=0, tiled=True)

    def forward(b):
        return attend_forward(query, b, kv_all[b], orders[b][2], head, kv_heads)

    def out_line(b):
        return attn_out_line(attended[b][0], One(to_slot, b), out_w, One(hidden_in, b), m_gain)

    def middle_line(b):
        return middle_back_line(fed[b][4], One(cotangent, b), middles[b][1], m_gain, out_w)

    def feed(b):
        return mlp_job(middles[b][1], middles[b][2], One(cotangent, b), mlp_w, n_tp)

    attended, middles, fed, mids, backs = [], [], [], [], []
    attended.append(forward(0))
    results = run_jobs(n_tp, out_line(0), [gather_job(One(kv_own, 1), n_ctx)], 2, 60, "attn_out_gather")
    middles.append(results[:3])
    kv_all.append(results[3].reshape(n_ctx, rows, -1))
    attended.append(forward(1))
    results = run_jobs(n_tp, out_line(1), [feed(0)], 3, 60, "attn_out_mlp")
    middles.append(results[:3])
    fed.append(results[3:])
    results = run_jobs(n_tp, middle_line(0), [feed(1)], 4, 60, "middle_back_mlp")
    mids.append(results[:3])
    fed.append(results[3:])

    layer_out = jnp.stack(lax.psum([fed[b][3] for b in both], "tp"))

    def backward(b, grad):
        unused, sorting, marks = orders[b]
        g_mixed = nn(sorting, grad).astype(BF16)
        mixed_full, mass = attended[b]
        return attend_backward(
            query, b, kv_all[b], marks, g_mixed, mixed_full, mass, raw, cosine, sine, q_gain, head, kv_heads
        )

    backs.append(backward(0, mids[0][1]))
    tile = 512 if units % 512 == 0 else 256
    line = middle_line(1)
    line[0][0] = (after(line[0][0][0], backs[0][0]), LOAD)
    results = run_jobs(
        n_tp,
        line,
        [
            weight_job(
                [middles[b][2] for b in both] + [One(cotangent, b) for b in both],
                [
                    (tuple(both), [fed[b][1] for b in both]),
                    (tuple(both), [fed[b][2] for b in both]),
                    (tuple(micro_count + b for b in both), [fed[b][0] for b in both]),
                ],
                tile,
                2 * max(1, CHUNKS // 16),
                mlp_w,
            ),
            scatter_job(backs[0][1].reshape(n_ctx * rows, -1), n_ctx, BF16, CHUNKS // 4, CHUNKS),
        ],
        5,
        60,
        "middle_back_weights",
        {5 + 5 * micro_count: 3},
    )
    mids.append(results[:3])
    mlp_grads = lax.psum_scatter(results[3], "ctx", scatter_dimension=0, tiled=True)
    dkv_first = results[4]
    backs.append(backward(1, mids[1][1]))

    def key_part(b, dkv):
        return key_back(dkv, b, raw, cosine, sine, k_gain, kv_heads)

    def in_line(b, gkv):
        return input_back_line(
            backs[b][0], gkv, One(to_slot, b), qkv_w, One(hidden_in, b), mids[b][0], a_gain
        )

    gkv_first, dk_gain_first = key_part(0, after(dkv_first, backs[1][0]))
    results = run_jobs(
        n_tp,
        in_line(0, gkv_first),
        [scatter_job(backs[1][1].reshape(n_ctx * rows, -1), n_ctx, BF16, CHUNKS // 4, CHUNKS)],
        6,
        60,
        "input_back_keys",
    )
    grad_in_first, da_gain_first, dkv_last = results
    gkv_last, dk_gain_last = key_part(1, dkv_last)
    tile = min(512, 2 * kv_heads * head, queries)
    gkvs = [gkv_first, gkv_last]
    attn_grads = weight_grads(
        [One(sorted_normed, b) for b in both] + [mids[b][0] for b in both],
        [
            (tuple(both), [backs[b][0] for b in both]),
            (tuple(both), [gkvs[b] for b in both]),
            (tuple(micro_count + b for b in both), [middles[b][0] for b in both]),
        ],
        tile,
    )
    results = run_jobs(
        n_tp,
        in_line(1, gkv_last),
        [scatter_job(attn_grads, n_ctx, F32, CHUNKS // 4, CHUNKS + 2)],
        7,
        60,
        "input_back_weights",
    )
    grad_in_last, da_gain_last, attn_grads = results
    grads_in = [grad_in_first, grad_in_last]
    d_attn_gain = [da_gain_first, da_gain_last]
    d_key_gain = [dk_gain_first, dk_gain_last]

    share = width // n_ctx // 128
    own = lambda gain: sum(gain).reshape(n_ctx, share, 128)
    spread = lambda gain: jnp.broadcast_to(sum(gain)[None], (n_ctx, 1, 128))
    blank = jnp.zeros((n_ctx, 4 - 2 * share, 128), F32)
    low_blank = jnp.zeros((n_ctx, 2, 128), F32)
    gains = sum_gains(
        jnp.concatenate(
            [
                own(d_attn_gain),
                own([mids[b][2] for b in both]),
                blank,
                spread([backs[b][2] for b in both]),
                spread(d_key_gain),
                low_blank,
            ],
            axis=1,
        ),
        n_ctx,
        n_tp,
        8,
    )

    grad_query, grad_key, grad_value, grad_out = attn_results(
        attn_grads, head, queries, kv_heads * head
    )
    grad_gate, grad_up, grad_down = mlp_results(mlp_grads)
    return (
        layer_out,
        jnp.stack(grads_in).astype(F32),
        gains[:share].reshape(-1),
        grad_query,
        grad_key,
        grad_value,
        gains[4],
        gains[5],
        grad_out,
        gains[share : 2 * share].reshape(-1),
        grad_gate,
        grad_up,
        grad_down,
    )


def solution(mesh):
    rows = P("ctx", "tp")
    columns = P("tp", "ctx")
    tokens = P(None, "ctx", None)
    in_specs = (
        tokens,
        P(),
        P(),
        P(),
        rows,
        rows,
        rows,
        P(),
        P(),
        columns,
        P(),
        rows,
        rows,
        columns,
        tokens,
    )
    out_specs = (
        tokens,
        tokens,
        P("ctx"),
        rows,
        rows,
        rows,
        P(),
        P(),
        columns,
        P("ctx"),
        rows,
        rows,
        columns,
    )
    return jax.shard_map(
        functools.partial(on_device, mesh.shape["ctx"], mesh.shape["tp"]),
        mesh=mesh,
        in_specs=in_specs,
        out_specs=out_specs,
        check_vma=False,
    )
```
